32 devices in a mesh: dp: 4 (over x, core), seq: 8 (over z, y).
Axes of the slice: x: 2, y: 2, z: 4, core: 2. Of those that a mesh axis runs over, the one named last changes fastest.
Arguments:
- hidden_in: bfloat16 [16, 1024, 640], P('dp', 'seq'), may hold values from -6 to 6
- positions: int32 [16, 1024], P('dp', 'seq'), may hold values from 0 to 1023, as said below
- out_grad: bfloat16 [16, 1024, 640], P('dp', 'seq'), may hold values from -6 to 6
- w_attn_in: bfloat16 [2, 640, 1536], P(None, None, ('dp', 'seq')), may hold values from -0.25 to 0.25
- w_attn_out: bfloat16 [2, 1024, 640], P(None, ('dp', 'seq')), may hold values from -0.1875 to 0.1875
- w_ffn_in: bfloat16 [2, 640, 4096], P(None, None, ('dp', 'seq')), may hold values from -0.25 to 0.25
- w_ffn_out: bfloat16 [2, 2048, 640], P(None, ('dp', 'seq')), may hold values from -0.125 to 0.125
- gains: bfloat16 [2, 3072], P(None, ('dp', 'seq')), may hold values from 0.5 to 1.5
Outputs:
- hidden_out: bfloat16 [16, 1024, 640], P('dp', 'seq')
- input_grad: float32 [16, 1024, 640], P('dp', 'seq')
- grad_attn_in: float32 [2, 640, 1536], P(None, None, ('dp', 'seq'))
- grad_attn_out: float32 [2, 1024, 640], P(None, ('dp', 'seq'))
- grad_ffn_in: float32 [2, 640, 4096], P(None, None, ('dp', 'seq'))
- grad_ffn_out: float32 [2, 2048, 640], P(None, ('dp', 'seq'))
- grad_gains: float32 [2, 3072], P(None, ('dp', 'seq'))
The draws below stay inside these ranges and needn't reach their ends.
Inputs may be any that keep to these rules, and one draw needn't show every extreme that they name: Within each sequence documents lie end to end and positions count up by one from 0 in each; in each group of 4 sequences along dp, one sequence is a single document.
All inputs are finite; a program needn't handle non-finite values.
Results may differ from the reference program's by a relative error of at most 0.02.
Values may be sent and summed in bfloat16 or wider, within the bound.
No kernel may reach another device: no remote copies, remote signals or barrier semaphores. Data moves between devices by JAX's collectives and lax.ppermute only.
A program may use at most 192 MiB of HBM per device.

```python
import jax
import jax.numpy as jnp
from jax import lax

D = 640
HEADS = 4
HEAD_DIM = 256
FF = 2048
WINDOW = 512
LAYERS = 2
SEQ_DEV = 4
LENGTH = 1024
SEQS = 16


def draw_positions(key, part):
    key = jax.random.fold_in(key, 11)
    start_key, whole_key = jax.random.split(key)
    column = jnp.arange(LENGTH, dtype=jnp.int32)
    starts = jax.random.randint(start_key, (SEQS, LENGTH), 0, LENGTH) < 3
    groups = SEQS // SEQ_DEV
    chosen = jax.random.randint(whole_key, (groups,), 0, SEQ_DEV) + SEQ_DEV * jnp.arange(groups, dtype=jnp.int32)
    row_ids = jnp.arange(SEQS, dtype=jnp.int32)
    single = jnp.any(row_ids[:, None] == chosen[None, :], axis=1)
    starts = starts & jnp.logical_not(single)[:, None] | (column[None, :] == 0)
    begins = lax.cummax(jnp.where(starts, column[None, :], 0), axis=1)
    return (column[None, :] - begins).astype(jnp.int32)


def block_scale(key, shape, shards, low, high):
    def one(position, parts):
        draws = jax.random.uniform(jax.random.fold_in(jax.random.fold_in(key, 6), position), (parts,), jnp.float32, low / len(shards), high / len(shards))
        return jnp.repeat(jnp.exp(draws), shape[position] // parts).reshape((-1,) + (1,) * (len(shape) - position - 1))

    loudness = one(*shards[0])
    for cut in shards[1:]:
        loudness = loudness * one(*cut)
    return loudness


def centred(key, extent, spread, most, shards=(), kind=jnp.bfloat16):
    array = spread * jax.random.normal(key, extent, jnp.float32)
    if shards:
        array = array * block_scale(key, extent, shards, -0.22, 0.18)
    return jnp.clip(array, -most, most).astype(kind)


def setup_inputs(seed: int = 0) -> dict:
    key_of = jax.random.split(jax.random.key(seed), 9)
    return {
        "hidden_in": centred(key_of[0], (SEQS, LENGTH, D), 1.0, 6.0, ((0, 4), (1, 8))),
        "positions": draw_positions(jax.random.fold_in(key_of[8], 71), 0),
        "out_grad": centred(key_of[2], (SEQS, LENGTH, D), 1.0, 6.0, ((0, 4), (1, 8))),
        "w_attn_in": centred(key_of[3], (LAYERS, D, (HEADS + 2) * HEAD_DIM), D ** -0.5, 0.25, ((2, 32),)),
        "w_attn_out": centred(key_of[4], (LAYERS, HEADS * HEAD_DIM, D), (HEADS * HEAD_DIM) ** -0.5, 0.1875, ((1, 32),)),
        "w_ffn_in": centred(key_of[5], (LAYERS, D, 2 * FF), D ** -0.5, 0.25, ((2, 32),)),
        "w_ffn_out": centred(key_of[6], (LAYERS, FF, D), FF ** -0.5, 0.125, ((1, 32),)),
        "gains": jnp.clip(1.0 + 0.1 * jax.random.normal(key_of[7], (LAYERS, 4 * D + 2 * HEAD_DIM), jnp.float32), 0.5, 1.5).astype(jnp.bfloat16),
    }


EPSILON = 1e-06
ROPE_BASE = 10000.0
SCORE_SCALE = 0.0625
MASKED_SCORE = -1e+30

@jax.custom_vjp
def low(v):
    return lax.optimization_barrier(v.astype(jnp.bfloat16)).astype(jnp.float32)

@jax.custom_vjp
def lowered_backward(v):
    return v

def low_keep(v):
    return (low(v), None)

def low_pass(kept, grad):
    return (grad,)

def back_keep(v):
    return (v, None)

def back_low(kept, grad):
    return (low(grad),)
low.defvjp(low_keep, low_pass)
lowered_backward.defvjp(back_keep, back_low)

def gated_product(pattern, left, right):
    return jnp.einsum(pattern, left, right, precision=lax.Precision.HIGHEST)

def rms_norm(values, gain):
    return values * lax.rsqrt(lax.optimization_barrier(jnp.mean(values * values, axis=-1, keepdims=True)) + EPSILON) * gain

def angle_tables(places):
    half_dim = HEAD_DIM // 2
    inverse = ROPE_BASE ** (-(2.0 * jnp.arange(half_dim, dtype=jnp.float32)) / HEAD_DIM)
    phases = places.astype(jnp.float32)[..., None] * inverse
    return (jnp.cos(phases), jnp.sin(phases))

def rotate(values, cosine_tab, sine_tab):
    half_dim = values.shape[-1] // 2
    first_half = values[..., :half_dim]
    second_half = values[..., half_dim:]
    return jnp.concatenate([first_half * cosine_tab - second_half * sine_tab, second_half * cosine_tab + first_half * sine_tab], axis=-1)

def prepare(raw_part, gain_part, cosine_tab, sine_tab):
    return rotate(rms_norm(raw_part, gain_part), cosine_tab, sine_tab)

def gated_gelu(gate_and_up_rows):
    half_width = gate_and_up_rows.shape[-1] // 2
    return jax.nn.gelu(gate_and_up_rows[..., :half_width], approximate=True) * gate_and_up_rows[..., half_width:]

def attention(queries, keys_rot, values, places):
    seq_count, length = (queries.shape[0], queries.shape[1])
    block_count = length // WINDOW
    keys_pad = jnp.pad(keys_rot, ((0, 0), (WINDOW, 0), (0, 0)))
    values_pad = jnp.pad(values, ((0, 0), (WINDOW, 0), (0, 0)))
    query_blocks = jnp.moveaxis(queries.reshape(seq_count, block_count, WINDOW, HEADS, HEAD_DIM), 1, 0)
    place_blocks = jnp.moveaxis(places.reshape(seq_count, block_count, WINDOW), 1, 0)

    @jax.checkpoint
    def one_block(block_item):
        query_block, place_block, block_index = block_item
        offset = (block_index * WINDOW).astype(jnp.int32)
        key_block = lax.dynamic_slice_in_dim(keys_pad, offset, 2 * WINDOW, 1)
        value_block = lax.dynamic_slice_in_dim(values_pad, offset, 2 * WINDOW, 1)
        query_at = offset + jnp.arange(WINDOW, dtype=jnp.int32)
        key_at = offset - WINDOW + jnp.arange(2 * WINDOW, dtype=jnp.int32)
        distance = query_at[:, None] - key_at[None, :]
        inside = (distance >= 0) & (distance < WINDOW)
        same_doc = key_at[None, None, :] >= (query_at[None, :] - place_block)[:, :, None]
        allowed = inside[None] & same_doc
        scores = lowered_backward(SCORE_SCALE * gated_product('sqhd,skd->shqk', query_block, key_block))
        scores = jnp.where(allowed[:, None], scores, MASKED_SCORE)
        row_max = lax.optimization_barrier(jnp.max(scores, axis=-1, keepdims=True))
        weights_exp = jnp.exp(scores - row_max)
        probs = low(weights_exp / lax.optimization_barrier(jnp.sum(weights_exp, axis=-1, keepdims=True)))
        return gated_product('shqk,skd->sqhd', probs, value_block)
    block_ids = jnp.arange(block_count, dtype=jnp.int32)
    attended_values = lax.map(one_block, (query_blocks, place_blocks, block_ids))
    return jnp.moveaxis(attended_values, 0, 1).reshape(seq_count, length, HEADS * HEAD_DIM)

def one_layer(stream, places, cosine_tab, sine_tab, attention_input_rows, attention_output_rows, feedforward_input, feedforward_output, gain_row):
    pre_attn = gain_row[0:D]
    post_attn = gain_row[D:2 * D]
    pre_ffn = gain_row[2 * D:3 * D]
    post_ffn = gain_row[3 * D:4 * D]
    query_gain = gain_row[4 * D:4 * D + HEAD_DIM]
    key_gain = gain_row[4 * D + HEAD_DIM:4 * D + 2 * HEAD_DIM]
    seq_count, length = (stream.shape[0], stream.shape[1])
    query_cols = HEADS * HEAD_DIM
    normalized_rows = low(rms_norm(stream, pre_attn))
    projected_rows = lowered_backward(gated_product('ynt,tg->yng', normalized_rows, attention_input_rows))
    query_raw = projected_rows[..., :query_cols].reshape(seq_count, length, HEADS, HEAD_DIM)
    key_raw = projected_rows[..., query_cols:query_cols + HEAD_DIM]
    values = low(projected_rows[..., query_cols + HEAD_DIM:])
    queries = low(prepare(query_raw, query_gain, cosine_tab[:, :, None, :], sine_tab[:, :, None, :]))
    keys_rot = low(prepare(key_raw, key_gain, cosine_tab, sine_tab))
    attended_values = lowered_backward(low(attention(queries, keys_rot, values, places)))
    residual_branch = lowered_backward(gated_product('mqa,af->mqf', attended_values, attention_output_rows))
    middle = stream + rms_norm(residual_branch, post_attn)
    feedforward_normalized = low(rms_norm(middle, pre_ffn))
    gate_and_up_rows = lowered_backward(gated_product('enj,jp->enp', feedforward_normalized, feedforward_input))
    inner_activation = low(gated_gelu(gate_and_up_rows))
    feedforward_branch = lowered_backward(gated_product('xki,iz->xkz', inner_activation, feedforward_output))
    return middle + rms_norm(feedforward_branch, post_ffn)

def forward_all(stream, places, weights):
    cosine_tab, sine_tab = angle_tables(places)
    for layer_index in range(LAYERS):
        stream = one_layer(stream, places, cosine_tab, sine_tab, *[weight[layer_index] for weight in weights])
    return stream

def reference(hidden_in, positions, out_grad, w_attn_in, w_attn_out, w_ffn_in, w_ffn_out, gains):
    weights = tuple((weight.astype(jnp.float32) for weight in (w_attn_in, w_attn_out, w_ffn_in, w_ffn_out, gains)))
    length = hidden_in.shape[1]
    groups = hidden_in.shape[0] // SEQ_DEV
    inputs = hidden_in.astype(jnp.float32).reshape(groups, SEQ_DEV, length, D)
    places = positions.reshape(groups, SEQ_DEV, length)
    cotangent = out_grad.astype(jnp.float32).reshape(groups, SEQ_DEV, length, D)

    def group_step(totals, block_item):
        block_input, block_places, block_cotangent = block_item

        def run_group(stream, *layer_weights):
            return forward_all(stream, block_places, layer_weights)
        result, pull_back = jax.vjp(run_group, block_input, *weights)
        gradients = pull_back(block_cotangent)
        totals = tuple((total + gradient for total, gradient in zip(totals, gradients[1:])))
        return (totals, (result, gradients[0]))
    zero_acc = tuple((jnp.zeros(weight.shape, jnp.float32) for weight in weights))
    totals, (results, input_grads) = lax.scan(group_step, zero_acc, (inputs, places, cotangent))
    hidden_out = results.reshape(hidden_in.shape).astype(jnp.bfloat16)
    input_grad = input_grads.reshape(hidden_in.shape)
    return (hidden_out, input_grad, totals[0], totals[1], totals[2], totals[3], totals[4])
```

```python
import jax
import jax.numpy as jnp
from jax import lax
from jax.experimental import pallas as pl
from jax.experimental.pallas import tpu as pltpu
from jax.sharding import PartitionSpec as P

D = 640
HEADS = 4
HEAD_DIM = 256
WINDOW = 512
QUERY_BLOCK = 256

EPSILON = 1e-06
ROPE_BASE = 10000.0
SCORE_SCALE = 0.0625
MASKED_SCORE = -1e30
BF16 = jnp.bfloat16
F32 = jnp.float32
ALL = ("dp", "seq")


def dot(a, b, a_dim, b_dim):
    return lax.dot_general(a, b, (((a_dim,), (b_dim,)), ((), ())), preferred_element_type=F32)


def rms_norm(values, gain):
    return values * lax.rsqrt(jnp.mean(values * values, axis=-1, keepdims=True) + EPSILON) * gain


def angle_tables(places):
    half_dim = HEAD_DIM // 2
    inverse = ROPE_BASE ** (-(2.0 * jnp.arange(half_dim, dtype=F32)) / HEAD_DIM)
    phases = places.astype(F32)[..., None] * inverse
    return (jnp.cos(phases), jnp.sin(phases))


def rotate(values, cosine_tab, sine_tab):
    half_dim = values.shape[-1] // 2
    first_half = values[..., :half_dim]
    second_half = values[..., half_dim:]
    return jnp.concatenate(
        [
            first_half * cosine_tab - second_half * sine_tab,
            second_half * cosine_tab + first_half * sine_tab,
        ],
        axis=-1,
    )


def prepare(raw_part, gain_part, cosine_tab, sine_tab):
    return rotate(rms_norm(raw_part, gain_part), cosine_tab, sine_tab)


def gated_gelu(gate_and_up_rows):
    half_width = gate_and_up_rows.shape[-1] // 2
    return (
        jax.nn.gelu(gate_and_up_rows[..., :half_width], approximate=True)
        * gate_and_up_rows[..., half_width:]
    )


def split_gains(gain_full):
    return (
        gain_full[0:D],
        gain_full[D : 2 * D],
        gain_full[2 * D : 3 * D],
        gain_full[3 * D : 4 * D],
        gain_full[4 * D : 4 * D + HEAD_DIM],
        gain_full[4 * D + HEAD_DIM : 4 * D + 2 * HEAD_DIM],
    )


def to_long(block):
    count, size = block.shape[0], lax.axis_size("seq")
    per = size // count
    me = lax.axis_index("seq")
    received = []
    for k in range(count):
        route = [(i, ((i + k) % count) * per + i // count) for i in range(size)]
        piece = lax.dynamic_index_in_dim(block, (me + k) % count, 0, keepdims=False)
        received.append(lax.ppermute(piece, "seq", route))
    own = me // per
    twice = jnp.stack((received[::-1] * 2)[: 2 * count - 1])
    long = lax.dynamic_slice_in_dim(twice, count - 1 - own, count, 0)
    return long.reshape((count * block.shape[1],) + block.shape[2:])


def to_short(long, count):
    size = lax.axis_size("seq")
    per = size // count
    me = lax.axis_index("seq")
    own = me // per
    parts = long.reshape((count, long.shape[0] // count) + long.shape[1:])
    received = []
    for k in range(count):
        route = [(((i + k) % count) * per + i // count, i) for i in range(size)]
        piece = lax.dynamic_index_in_dim(parts, (own - k) % count, 0, keepdims=False)
        received.append(lax.ppermute(piece, "seq", route))
    twice = jnp.stack((received * 2)[: 2 * count - 1])
    return lax.dynamic_slice_in_dim(twice, (count - me % count) % count, count, 0)


def neighbour(block, back):
    size = lax.axis_size("seq")
    per = size // SEQ_PER_DP
    pairs = [(i, i + 1) for i in range(size) if (i + 1) % per]
    if back:
        pairs = [(j, i) for i, j in pairs]
    return lax.ppermute(block, "seq", pairs)


SEQ_PER_DP = 4


def halving(array):
    n_dp, n_seq = lax.axis_size("dp"), lax.axis_size("seq")
    rest = array.shape[1:]
    steps = []
    bit = 1
    while bit < n_dp:
        steps.append(("dp", bit))
        bit *= 2
    bit = 1
    while bit < n_seq:
        steps.append(("seq", bit))
        bit *= 2
    dtype = array.dtype
    left = {"dp": n_dp, "seq": n_seq}
    for axis, bit in steps:
        size = lax.axis_size(axis)
        mine = (lax.axis_index(axis) // bit) % 2
        inner = left["seq"] if axis == "dp" else 1
        view = array.reshape((-1, 2, inner) + rest)
        send = lax.dynamic_index_in_dim(view, 1 - mine, 1, keepdims=False)
        keep = lax.dynamic_index_in_dim(view, mine, 1, keepdims=False)
        got = lax.ppermute(send, axis, [(i, i ^ bit) for i in range(size)])
        array = (keep.astype(F32) + got.astype(F32)).astype(dtype)
        left[axis] //= 2
    return array.reshape(rest)


def allowed_pairs(start, key_count, reach, lanes):
    key_at = lax.broadcasted_iota(jnp.int32, (key_count, lanes), 0)
    query_at = lax.broadcasted_iota(jnp.int32, (key_count, lanes), 1) % QUERY_BLOCK
    distance = query_at + WINDOW - key_at
    return (distance >= 0) & (distance <= reach)


def stacked_heads(ref, start):
    return jnp.concatenate(
        [
            ref[start : start + QUERY_BLOCK, h * HEAD_DIM : (h + 1) * HEAD_DIM]
            for h in range(HEADS)
        ],
        axis=0,
    )


def window_rows(before_ref, own_ref, start, count):
    return jnp.concatenate([before_ref[start:, :], own_ref[: count - (WINDOW - start), :]], axis=0)


def attention_forward_kernel(q_ref, kb_ref, vb_ref, k_ref, v_ref, reach_ref, ctx_ref, lse_ref):
    key_count = QUERY_BLOCK + WINDOW
    for block in range(q_ref.shape[0] // QUERY_BLOCK):
        start = block * QUERY_BLOCK
        queries = stacked_heads(q_ref, start)
        keys = window_rows(kb_ref, k_ref, start, key_count)
        values = window_rows(vb_ref, v_ref, start, key_count)
        allowed = allowed_pairs(start, key_count, reach_ref[block : block + 1, :], HEADS * QUERY_BLOCK)
        scores = jnp.where(allowed, dot(keys, queries, 1, 1), MASKED_SCORE)
        row_max = jnp.max(scores, axis=0, keepdims=True)
        weights = jnp.exp(scores - row_max)
        row_sum = jnp.sum(weights, axis=0, keepdims=True)
        probs = (weights * (1.0 / row_sum)).astype(BF16)
        lse_ref[block : block + 1, :] = row_max + jnp.log(row_sum)
        context = dot(probs, values, 0, 0).astype(BF16)
        for h in range(HEADS):
            ctx_ref[start : start + QUERY_BLOCK, h * HEAD_DIM : (h + 1) * HEAD_DIM] = context[
                h * QUERY_BLOCK : (h + 1) * QUERY_BLOCK
            ]


def attention_backward_kernel(
    q_ref, kb_ref, vb_ref, k_ref, v_ref, reach_ref, lse_ref, g_ref, dq_ref, before_ref, own_ref, acc
):
    key_count = QUERY_BLOCK + WINDOW
    acc[...] = jnp.zeros_like(acc)
    for block in range(q_ref.shape[0] // QUERY_BLOCK):
        start = block * QUERY_BLOCK
        queries = stacked_heads(q_ref, start)
        grads = stacked_heads(g_ref, start)
        keys = window_rows(kb_ref, k_ref, start, key_count)
        values = window_rows(vb_ref, v_ref, start, key_count)
        allowed = allowed_pairs(start, key_count, reach_ref[block : block + 1, :], HEADS * QUERY_BLOCK)
        scores = jnp.where(allowed, dot(keys, queries, 1, 1), MASKED_SCORE)
        probs = jnp.exp(scores - lse_ref[block : block + 1, :])
        grad_probs = dot(values, grads, 1, 1)
        inner = jnp.sum(probs * grad_probs, axis=0, keepdims=True)
        grad_scores = (probs * (grad_probs - inner)).astype(BF16)
        acc[start : start + key_count, HEAD_DIM:] += dot(probs.astype(BF16), grads, 1, 0)
        acc[start : start + key_count, :HEAD_DIM] += dot(grad_scores, queries, 1, 0)
        grad_queries = dot(grad_scores, keys, 0, 0) * SCORE_SCALE
        for h in range(HEADS):
            dq_ref[start : start + QUERY_BLOCK, h * HEAD_DIM : (h + 1) * HEAD_DIM] = grad_queries[
                h * QUERY_BLOCK : (h + 1) * QUERY_BLOCK
            ]
    before_ref[...] = acc[:WINDOW, :].astype(BF16)
    own_ref[...] = acc[WINDOW:, :]


def vmem(count):
    return [pl.BlockSpec(memory_space=pltpu.VMEM)] * count


def attention_forward(queries, before, own, reach):
    tokens = queries.shape[0]
    kb, vb = before[:, :HEAD_DIM], before[:, HEAD_DIM:]
    k, v = own[:, :HEAD_DIM], own[:, HEAD_DIM:]
    return pl.pallas_call(
        attention_forward_kernel,
        out_shape=(
            jax.ShapeDtypeStruct((tokens, HEADS * HEAD_DIM), BF16),
            jax.ShapeDtypeStruct(reach.shape, F32),
        ),
        in_specs=vmem(6),
        out_specs=tuple(vmem(2)),
        compiler_params=pltpu.CompilerParams(vmem_limit_bytes=40 * 2**20),
        cost_estimate=pl.CostEstimate(
            flops=4 * tokens * HEADS * HEAD_DIM * (QUERY_BLOCK + WINDOW),
            bytes_accessed=6 * 2**20,
            transcendentals=tokens * HEADS * (QUERY_BLOCK + WINDOW),
        ),
        name="attention_forward",
    )(queries, kb, vb, k, v, reach)


def attention_backward(queries, before, own, reach, lse, grads):
    tokens = queries.shape[0]
    kb, vb = before[:, :HEAD_DIM], before[:, HEAD_DIM:]
    k, v = own[:, :HEAD_DIM], own[:, HEAD_DIM:]
    return pl.pallas_call(
        attention_backward_kernel,
        out_shape=(
            jax.ShapeDtypeStruct((tokens, HEADS * HEAD_DIM), F32),
            jax.ShapeDtypeStruct((WINDOW, 2 * HEAD_DIM), BF16),
            jax.ShapeDtypeStruct((tokens, 2 * HEAD_DIM), F32),
        ),
        in_specs=vmem(8),
        out_specs=tuple(vmem(3)),
        scratch_shapes=[pltpu.VMEM((WINDOW + tokens, 2 * HEAD_DIM), F32)],
        compiler_params=pltpu.CompilerParams(vmem_limit_bytes=40 * 2**20),
        cost_estimate=pl.CostEstimate(
            flops=10 * tokens * HEADS * HEAD_DIM * (QUERY_BLOCK + WINDOW),
            bytes_accessed=10 * 2**20,
            transcendentals=tokens * HEADS * (QUERY_BLOCK + WINDOW),
        ),
        name="attention_backward",
    )(queries, kb, vb, k, v, reach, lse, grads)


def forward_layer(stream, weights, tables, reach):
    attn_in, attn_out, ffn_in, ffn_out, gain_row = weights
    pre_attn, post_attn, pre_ffn, post_ffn, query_gain, key_gain = split_gains(gain_row)
    cosine_tab, sine_tab = tables
    tokens = stream.shape[0]
    query_cols = HEADS * HEAD_DIM
    normed = rms_norm(stream, pre_attn).astype(BF16)
    key_value_raw = dot(normed, attn_in[query_cols:], 1, 1)
    key_raw = key_value_raw[:, :HEAD_DIM]
    keys = prepare(key_raw, key_gain, cosine_tab, sine_tab).astype(BF16)
    own = jnp.concatenate([keys, key_value_raw[:, HEAD_DIM:].astype(BF16)], axis=1)
    before = neighbour(own, False)
    query_raw = dot(normed, attn_in[:query_cols], 1, 1).reshape(tokens, HEADS, HEAD_DIM)
    queries = prepare(query_raw, query_gain, cosine_tab[:, None, :], sine_tab[:, None, :])
    queries = (queries.astype(BF16) * SCORE_SCALE).reshape(tokens, query_cols)
    context, lse = attention_forward(queries, before, own, reach)
    branch = dot(context, attn_out, 1, 0)
    middle = stream + rms_norm(branch, post_attn)
    ffn_normed = rms_norm(middle, pre_ffn).astype(BF16)
    gate_up = dot(ffn_normed, ffn_in, 1, 1)
    inner = gated_gelu(gate_up).astype(BF16)
    ffn_branch = dot(inner, ffn_out, 1, 0)
    result = middle + rms_norm(ffn_branch, post_ffn)
    record = (
        stream, normed, query_raw, key_raw, queries, before, own, lse, context,
        branch, middle, ffn_normed, gate_up, inner, ffn_branch,
    )
    return record, result


def pieces(array):
    devices = lax.axis_size("dp") * lax.axis_size("seq")
    return array.astype(BF16).reshape(devices, array.shape[0] // devices, array.shape[1])


def backward_layer(grad_out, weights, record, tables, reach):
    attn_in, attn_out, ffn_in, ffn_out, gain_row = weights
    pre_attn, post_attn, pre_ffn, post_ffn, query_gain, key_gain = split_gains(gain_row)
    cosine_tab, sine_tab = tables
    (
        stream, normed, query_raw, key_raw, queries, before, own, lse, context,
        branch, middle, ffn_normed, gate_up, inner, ffn_branch,
    ) = record
    tokens = stream.shape[0]
    query_cols = HEADS * HEAD_DIM
    _, pull_post_ffn = jax.vjp(rms_norm, ffn_branch, post_ffn)
    grad_ffn_branch, grad_post_ffn = pull_post_ffn(grad_out)
    grad_ffn_branch = grad_ffn_branch.astype(BF16)
    grad_ffn_out = halving(pieces(dot(inner, grad_ffn_branch, 0, 0)))
    grad_inner = dot(grad_ffn_branch, ffn_out, 1, 1)
    _, pull_act = jax.vjp(gated_gelu, gate_up)
    grad_gate_up = pull_act(grad_inner)[0].astype(BF16)
    grad_ffn_in = halving(pieces(dot(grad_gate_up, ffn_normed, 0, 0)))
    grad_ffn_normed = dot(grad_gate_up, ffn_in, 1, 0)
    _, pull_pre_ffn = jax.vjp(rms_norm, middle, pre_ffn)
    grad_middle_part, grad_pre_ffn = pull_pre_ffn(grad_ffn_normed)
    grad_middle = grad_out + grad_middle_part
    _, pull_post_attn = jax.vjp(rms_norm, branch, post_attn)
    grad_branch, grad_post_attn = pull_post_attn(grad_middle)
    grad_branch = grad_branch.astype(BF16)
    grad_attn_out = halving(pieces(dot(context, grad_branch, 0, 0)))
    grad_context = dot(grad_branch, attn_out, 1, 1).astype(BF16)
    grad_queries, grad_before, grad_own = attention_backward(
        queries, before, own, reach, lse, grad_context
    )
    grad_own = grad_own + neighbour(grad_before, True).astype(F32)
    _, pull_query = jax.vjp(
        lambda raw, gain: prepare(raw, gain, cosine_tab[:, None, :], sine_tab[:, None, :]),
        query_raw,
        query_gain,
    )
    grad_query_raw, grad_query_gain = pull_query(grad_queries.reshape(tokens, HEADS, HEAD_DIM))
    _, pull_key = jax.vjp(
        lambda raw, gain: prepare(raw, gain, cosine_tab, sine_tab), key_raw, key_gain
    )
    grad_key_raw, grad_key_gain = pull_key(grad_own[:, :HEAD_DIM])
    grad_projected = jnp.concatenate(
        [grad_query_raw.reshape(tokens, query_cols), grad_key_raw, grad_own[:, HEAD_DIM:]], axis=-1
    ).astype(BF16)
    grad_attn_in = halving(pieces(dot(grad_projected, normed, 0, 0)))
    grad_normed = dot(grad_projected, attn_in, 1, 0)
    _, pull_pre_attn = jax.vjp(rms_norm, stream, pre_attn)
    grad_stream_part, grad_pre_attn = pull_pre_attn(grad_normed)
    grad_in = grad_middle + grad_stream_part
    grad_gain_row = jnp.concatenate(
        [grad_pre_attn, grad_post_attn, grad_pre_ffn, grad_post_ffn, grad_query_gain, grad_key_gain]
    )
    return grad_in, (grad_attn_in, grad_attn_out, grad_ffn_in, grad_ffn_out, grad_gain_row)


def gather_weights(w_attn_in, w_attn_out, w_ffn_in, w_ffn_out, gains):
    parts = [w_attn_in.T, w_attn_out, w_ffn_in.T, w_ffn_out]
    sizes = [part.shape[0] for part in parts]
    gain_rows = jnp.pad(gains[None, :], ((0, 15), (0, D - gains.shape[0])))
    packed = jnp.concatenate(parts + [gain_rows], axis=0)
    whole = lax.all_gather(packed, ALL, axis=0, tiled=False)
    out, at = [], 0
    for size in sizes:
        out.append(whole[:, at : at + size].reshape(-1, D))
        at += size
    gain_full = whole[:, at, : gains.shape[0]].reshape(-1).astype(F32)
    return tuple(out) + (gain_full,)


def body(hidden_in, positions, out_grad, w_attn_in, w_attn_out, w_ffn_in, w_ffn_out, gains):
    count = hidden_in.shape[0]
    layer_count = w_attn_in.shape[0]
    weights = [
        gather_weights(w_attn_in[l], w_attn_out[l], w_ffn_in[l], w_ffn_out[l], gains[l])
        for l in range(layer_count)
    ]
    places = to_long(positions)
    stream = to_long(hidden_in).astype(F32)
    tables = angle_tables(places)
    tokens = places.shape[0]
    blocks = tokens // QUERY_BLOCK
    reach = jnp.minimum(places, WINDOW - 1).reshape(blocks, QUERY_BLOCK)
    reach = jnp.tile(reach, (1, HEADS))
    records = []
    for layer_index in range(layer_count):
        record, stream = forward_layer(stream, weights[layer_index], tables, reach)
        records.append(record)
    hidden_out = to_short(stream.astype(BF16), count)
    grad_stream = to_long(out_grad).astype(F32)
    layer_grads = [None] * layer_count
    for layer_index in reversed(range(layer_count)):
        grad_stream, layer_grads[layer_index] = backward_layer(
            grad_stream, weights[layer_index], records[layer_index], tables, reach
        )
    input_grad = to_short(grad_stream.astype(BF16), count).astype(F32)
    devices = lax.axis_size("dp") * lax.axis_size("seq")
    gain_grads = jnp.stack([entry[4].reshape(devices, -1) for entry in layer_grads], axis=1)
    gain_grads = halving(gain_grads)
    members = [jnp.stack([entry[m].astype(F32) for entry in layer_grads]) for m in range(4)]
    return (
        hidden_out,
        input_grad,
        members[0].transpose(0, 2, 1),
        members[1],
        members[2].transpose(0, 2, 1),
        members[3],
        gain_grads,
    )


def solution(mesh):
    return jax.shard_map(
        body,
        mesh=mesh,
        in_specs=(
            P("dp", "seq", None),
            P("dp", "seq"),
            P("dp", "seq", None),
            P(None, None, ("dp", "seq")),
            P(None, ("dp", "seq"), None),
            P(None, None, ("dp", "seq")),
            P(None, ("dp", "seq"), None),
            P(None, ("dp", "seq")),
        ),
        out_specs=(
            P("dp", "seq", None),
            P("dp", "seq", None),
            P(None, None, ("dp", "seq")),
            P(None, ("dp", "seq"), None),
            P(None, None, ("dp", "seq")),
            P(None, ("dp", "seq"), None),
            P(None, ("dp", "seq")),
        ),
        check_vma=False,
    )
```

```python
from functools import partial

import jax
import jax.numpy as jnp
from jax import lax
from jax.experimental import pallas as pl
from jax.experimental.pallas import tpu as pltpu
from jax.sharding import PartitionSpec as P

D = 640
HEADS = 4
HEAD_DIM = 256
WINDOW = 512
QUERY_BLOCK = 256

EPSILON = 1e-06
ROPE_BASE = 10000.0
SCORE_SCALE = 0.0625
MASKED_SCORE = -1e30
BF16 = jnp.bfloat16
F32 = jnp.float32
ALL = ("dp", "seq")
TILE = 16
QUERY_COLS = HEADS * HEAD_DIM
GELU_A = 0.7978845608028654
GELU_B = 0.044715
HIDDEN_BLOCK = 512


def dot(a, b, a_dim, b_dim):
    return lax.dot_general(a, b, (((a_dim,), (b_dim,)), ((), ())), preferred_element_type=F32)


def angle_tables(places):
    half_dim = HEAD_DIM // 2
    inverse = ROPE_BASE ** (-(2.0 * jnp.arange(half_dim, dtype=F32)) / HEAD_DIM)
    phases = places.astype(F32)[..., None] * inverse
    return (jnp.cos(phases), jnp.sin(phases))


def inverse_rms(values):
    return lax.rsqrt(jnp.mean(values * values, axis=-1, keepdims=True) + EPSILON)


def rms_norm(values, gain):
    return values * inverse_rms(values) * gain


def rms_backward(values, gain, grad):
    scale = inverse_rms(values)
    weighted = grad * gain
    shared = jnp.mean(weighted * values, axis=-1, keepdims=True) * (scale * scale * scale)
    grad_gain = jnp.sum(grad * (values * scale), axis=0, keepdims=True)
    return weighted * scale - values * shared, grad_gain


def rotate(values, cosine_tab, sine_tab):
    half_dim = HEAD_DIM // 2
    first, second = values[:, :half_dim], values[:, half_dim:]
    return jnp.concatenate(
        [first * cosine_tab - second * sine_tab, second * cosine_tab + first * sine_tab], axis=-1
    )


def rotate_back(values, cosine_tab, sine_tab):
    return rotate(values, cosine_tab, -sine_tab)


def gain_of(gains_ref, which):
    starts = (0, D, 2 * D, 3 * D, 4 * D, 4 * D + HEAD_DIM)
    return gains_ref[:, starts[which] : starts[which] + (D if which < 4 else HEAD_DIM)]


PRE_ATTN, POST_ATTN, PRE_FFN, POST_FFN, QUERY_GAIN, KEY_GAIN = range(6)


def weight_rows(ref, start, size):
    shards, rows, width = ref.shape
    if shards == 1:
        return ref[0, start : start + size, :]
    first, last = start // rows, -(-(start + size) // rows)
    value = ref[first:last].reshape((last - first) * rows, width)
    skip = start - first * rows
    return value[skip : skip + size]


def fetch(weight, ref, scratch, sem):
    _, start, rows = weight
    copy = pltpu.make_async_copy(ref.at[:, pl.ds(start, rows), :], scratch, sem)
    copy.start()
    return copy


def weight_scratch(weight):
    array, _, rows = weight
    return pltpu.VMEM((array.shape[0], rows, D), BF16)


def vmem(count):
    return [pl.BlockSpec(memory_space=pltpu.VMEM)] * count


def call(kernel, name, arrays, weights, outs, flops, scratch=()):
    outs = [jax.ShapeDtypeStruct(shape, dtype) for shape, dtype in outs]
    moved = sum(a.size * a.dtype.itemsize for a in list(arrays) + outs)
    return pl.pallas_call(
        kernel,
        out_shape=tuple(outs),
        in_specs=vmem(len(arrays)) + [pl.BlockSpec(memory_space=pl.ANY)] * len(weights),
        out_specs=tuple(vmem(len(outs))),
        scratch_shapes=[weight_scratch(w) for w in weights]
        + ([pltpu.SemaphoreType.DMA((len(weights),))] if weights else [])
        + list(scratch),
        compiler_params=pltpu.CompilerParams(vmem_limit_bytes=VMEM_LIMIT),
        cost_estimate=pl.CostEstimate(flops=flops, bytes_accessed=moved, transcendentals=0),
        name=name,
    )(*arrays, *[w[0] for w in weights])


VMEM_LIMIT = 44 * 2**20


def chunk_route(count, k):
    n_dp, n_seq = lax.axis_size("dp"), lax.axis_size("seq")
    chips = n_seq // (2 * count)
    pairs = []
    for dp in range(n_dp):
        for i in range(n_seq):
            chunk = i // count
            sequence = (dp % 2) * count + (i + k) % count
            target_dp = dp - dp % 2 + chunk % 2
            pairs.append((dp * n_seq + i, target_dp * n_seq + sequence * chips + chunk // 2))
    return pairs


def place(count):
    chips = lax.axis_size("seq") // (2 * count)
    return (lax.axis_index("seq") // chips) % count


def to_long(block):
    count = block.shape[0]
    me = lax.axis_index("seq")
    received = []
    for k in range(count):
        piece = lax.dynamic_index_in_dim(block, (me + k) % count, 0, keepdims=False)
        received.append(lax.ppermute(piece, ALL, chunk_route(count, k)))
    twice = jnp.stack((received[::-1] * 2)[: 2 * count - 1])
    long = lax.dynamic_slice_in_dim(twice, count - 1 - place(count), count, 0)
    return long.reshape((count * block.shape[1],) + block.shape[2:])


def to_short(long, count):
    me = lax.axis_index("seq")
    parts = long.reshape((count, long.shape[0] // count) + long.shape[1:])
    received = []
    for k in range(count):
        piece = lax.dynamic_index_in_dim(parts, (place(count) - k) % count, 0, keepdims=False)
        route = [(j, i) for i, j in chunk_route(count, k)]
        received.append(lax.ppermute(piece, ALL, route))
    twice = jnp.stack((received * 2)[: 2 * count - 1])
    return lax.dynamic_slice_in_dim(twice, (count - me % count) % count, count, 0)


def neighbour(block, count, back):
    n_dp, n_seq = lax.axis_size("dp"), lax.axis_size("seq")
    chips = n_seq // (2 * count)
    pairs = []
    for dp in range(n_dp):
        for i in range(n_seq):
            if dp % 2 == 0:
                pairs.append((dp * n_seq + i, (dp + 1) * n_seq + i))
            elif (i + 1) % chips:
                pairs.append((dp * n_seq + i, (dp - 1) * n_seq + i + 1))
    if back:
        pairs = [(j, i) for i, j in pairs]
    return lax.ppermute(block, ALL, pairs)


def bits(axis):
    out, bit = [], 1
    while bit < lax.axis_size(axis):
        out.append((axis, bit))
        bit *= 2
    return out


def order(first):
    core, *wide = bits("dp")
    near, *far = bits("seq")
    if first == "dp":
        return [core] + wide + [near] + far[::-1]
    return [core, near] + wide + far[::-1]


def swap(array, step):
    axis, bit = step
    return lax.ppermute(array, axis, [(i, i ^ bit) for i in range(lax.axis_size(axis))])


def advance(value, chains):
    if not chains:
        return value
    held = lax.optimization_barrier((value,) + tuple(chain.got for chain in chains))
    for chain, got in zip(chains, held[1:]):
        chain.got = got
        chain.advance()
    return held[0]


def halving(array):
    n_seq = lax.axis_size("seq")
    dims = bits("dp")[::-1] + bits("seq")[::-1]
    me = lax.axis_index("dp") * n_seq + lax.axis_index("seq")
    rest = array.shape[1:]
    array = jnp.take(array, me ^ jnp.arange(array.shape[0]), axis=0)
    array = array.reshape((2,) * len(dims) + rest)
    for step in order("dp"):
        at = dims.index(step)
        dims.remove(step)
        keep = lax.index_in_dim(array, 0, at, keepdims=False)
        array = keep + swap(lax.index_in_dim(array, 1, at, keepdims=False), step)
    return array


def block_numbers():
    me = lax.axis_index("dp")
    core = me % 2
    wide = [me // 2, (me // 2) ^ 1]
    leave = [2 * w + 1 - core for w in wide]
    stay = [2 * w + core for w in wide]
    return jnp.stack(leave + stay + [lax.axis_index("seq")]).astype(jnp.int32)


def product_kernel(rows, split, added, numbers_ref, a_ref, b_ref, *refs):
    got_ref = refs[0] if added else None
    outs, acc = refs[1 if added else 0 : -1], refs[-1]
    acc[...] = dot(a_ref[...], b_ref[...], 0, 0)
    me = numbers_ref[4]
    for entry in range(a_ref.shape[1] // rows):
        source = pl.multiple_of((me ^ entry) * rows, TILE)
        value = acc[pl.ds(source, rows), :]
        if added:
            value = value + got_ref[0, entry].astype(F32)
        if split:
            outs[entry % 2][0, entry // 2] = value.astype(BF16)
        else:
            outs[0][0, entry] = value.astype(BF16)


def product(left, right, numbers, first, blocks, got=None, got_first=0, split=False):
    tokens, n_seq = left.shape[0], lax.axis_size("seq")
    width = left.shape[1] // lax.axis_size("dp")
    rows = width // n_seq
    out_entries = n_seq // 2 if split else n_seq
    specs = [
        pl.BlockSpec((tokens, width), lambda i, n: (0, n[first + i])),
        pl.BlockSpec((tokens, D), lambda i, n: (0, 0)),
    ]
    operands = [left, right]
    if got is not None:
        specs.append(pl.BlockSpec((1, n_seq, rows, D), lambda i, n: (i + got_first, 0, 0, 0)))
        operands.append(got)
    shape = jax.ShapeDtypeStruct((blocks, out_entries, rows, D), BF16)
    count = 2 if split else 1
    return pl.pallas_call(
        partial(product_kernel, rows, split, got is not None),
        grid_spec=pltpu.PrefetchScalarGridSpec(
            num_scalar_prefetch=1,
            grid=(blocks,),
            in_specs=specs,
            out_specs=[pl.BlockSpec((1, out_entries, rows, D), lambda i, n: (i, 0, 0, 0))] * count,
            scratch_shapes=[pltpu.VMEM((width, D), F32)],
        ),
        out_shape=[shape] * count,
        compiler_params=pltpu.CompilerParams(vmem_limit_bytes=24 * 2**20),
        cost_estimate=pl.CostEstimate(
            flops=2 * tokens * width * blocks * D,
            bytes_accessed=2 * (tokens * width * blocks + tokens * D + 2 * width * blocks * D),
            transcendentals=0,
        ),
        name="weight_gradient",
    )(numbers, *operands)


class Chain:
    def __init__(self, left, right, first):
        self.steps = order(first)
        self.dims = bits("dp")[::-1] + bits("seq")[::-1]
        n_dp, n_seq = lax.axis_size("dp"), lax.axis_size("seq")
        width = left.shape[1] // n_dp
        self.rows = width // n_seq
        self.factors = None
        step = self.steps[0]
        if n_dp == 4 and width % 128 == 0 and self.rows % TILE == 0 and width % n_seq == 0:
            self.factors = (left, right, block_numbers())
            (send,) = product(left, right, self.factors[2], 0, 2)
            self.dims.remove(step)
            self.got = swap(send, step)
        else:
            whole = dot(left, right, 0, 0).astype(BF16).reshape(n_dp * n_seq, self.rows, D)
            me = lax.axis_index("dp") * n_seq + lax.axis_index("seq")
            self.send(jnp.take(whole, me ^ jnp.arange(n_dp * n_seq), axis=0))

    def send(self, array):
        step = self.steps[0]
        array = array.reshape((2,) * len(self.dims) + (self.rows, D))
        at = self.dims.index(step)
        self.dims.remove(step)
        self.keep = lax.index_in_dim(array, 0, at, keepdims=False)
        self.got = swap(lax.index_in_dim(array, 1, at, keepdims=False), step)

    def advance(self):
        self.steps = self.steps[1:]
        if self.factors:
            left, right, numbers = self.factors
            self.factors = None
            step = self.steps[0]
            if step[0] == "dp":
                (send,) = product(left, right, numbers, 3, 1, self.got, 1)
                (self.keep,) = product(left, right, numbers, 2, 1, self.got, 0)
            else:
                self.keep, send = product(left, right, numbers, 2, 2, self.got, 0, True)
            self.dims.remove(step)
            self.got = swap(send, step)
            return
        array = self.keep.astype(F32) + self.got.reshape(self.keep.shape).astype(F32)
        if self.steps:
            self.send(array.astype(BF16))
        else:
            self.result = array.reshape(self.rows, D)

    def finish(self):
        while self.steps:
            self.advance()
        return self.result


def allowed_pairs(start, key_count, reach, lanes):
    key_at = lax.broadcasted_iota(jnp.int32, (key_count, lanes), 0)
    query_at = lax.broadcasted_iota(jnp.int32, (key_count, lanes), 1) % QUERY_BLOCK
    distance = query_at + WINDOW - key_at
    return (distance >= 0) & (distance <= reach)


def stacked_heads(ref, start):
    return jnp.concatenate(
        [
            ref[start : start + QUERY_BLOCK, h * HEAD_DIM : (h + 1) * HEAD_DIM]
            for h in range(HEADS)
        ],
        axis=0,
    )


def window_rows(before_ref, own_ref, start, count, columns):
    return jnp.concatenate(
        [before_ref[start:, columns], own_ref[: count - (WINDOW - start), columns]], axis=0
    )


KEYS, VALUES = slice(0, HEAD_DIM), slice(HEAD_DIM, 2 * HEAD_DIM)
KEY_COUNT = QUERY_BLOCK + WINDOW


def key_value_kernel(weights, stream_ref, gains_ref, cos_ref, sin_ref, w_any, normed_ref, raw_ref, own_ref, w_ref, sem):
    copy = fetch(weights[0], w_any, w_ref, sem.at[0])
    normed = rms_norm(stream_ref[...], gain_of(gains_ref, PRE_ATTN)).astype(BF16)
    normed_ref[...] = normed
    copy.wait()
    raw = dot(normed, weight_rows(w_ref, QUERY_COLS, 2 * HEAD_DIM), 1, 1)
    raw_ref[...] = raw[:, KEYS]
    keys = rms_norm(raw[:, KEYS], gain_of(gains_ref, KEY_GAIN))
    own_ref[:, KEYS] = rotate(keys, cos_ref[...], sin_ref[...]).astype(BF16)
    own_ref[:, VALUES] = raw[:, VALUES].astype(BF16)


def query_kernel(weights, normed_ref, gains_ref, cos_ref, sin_ref, w_any, raw_ref, q_ref, w_ref, sem):
    copy = fetch(weights[0], w_any, w_ref, sem.at[0])
    copy.wait()
    cosine_tab, sine_tab = cos_ref[...], sin_ref[...]
    normed = normed_ref[...]
    for h in range(HEADS):
        columns = slice(h * HEAD_DIM, (h + 1) * HEAD_DIM)
        raw = dot(normed, weight_rows(w_ref, h * HEAD_DIM, HEAD_DIM), 1, 1)
        raw_ref[:, columns] = raw
        queries = rotate(rms_norm(raw, gain_of(gains_ref, QUERY_GAIN)), cosine_tab, sine_tab)
        q_ref[:, columns] = queries.astype(BF16) * SCORE_SCALE


def gelu_parts(gate):
    inner = GELU_A * (gate + GELU_B * gate * gate * gate)
    tanh = jnp.tanh(inner)
    return tanh, 0.5 * gate * (1.0 + tanh)


def block_kernel(
    weights, q_ref, before_ref, own_ref, reach_ref, stream_ref, gains_ref, wa_any, wi_any, wo_any,
    ctx_ref, lse_ref, branch_ref, middle_ref, fn_ref, gu_ref, inner_ref, fb_ref, result_ref,
    wa_ref, wi_ref, wo_ref, sem,
):
    copies = [
        fetch(weight, source, target, sem.at[i])
        for i, (weight, source, target) in enumerate(
            zip(weights, (wa_any, wi_any, wo_any), (wa_ref, wi_ref, wo_ref))
        )
    ]
    for block in range(q_ref.shape[0] // QUERY_BLOCK):
        start = block * QUERY_BLOCK
        queries = stacked_heads(q_ref, start)
        keys = window_rows(before_ref, own_ref, start, KEY_COUNT, KEYS)
        values = window_rows(before_ref, own_ref, start, KEY_COUNT, VALUES)
        allowed = allowed_pairs(start, KEY_COUNT, reach_ref[block : block + 1, :], HEADS * QUERY_BLOCK)
        scores = jnp.where(allowed, dot(keys, queries, 1, 1), MASKED_SCORE)
        row_max = jnp.max(scores, axis=0, keepdims=True)
        exps = jnp.exp(scores - row_max)
        row_sum = jnp.sum(exps, axis=0, keepdims=True)
        probs = (exps * (1.0 / row_sum)).astype(BF16)
        lse_ref[block : block + 1, :] = row_max + jnp.log(row_sum)
        context = dot(probs, values, 0, 0).astype(BF16)
        for h in range(HEADS):
            ctx_ref[start : start + QUERY_BLOCK, h * HEAD_DIM : (h + 1) * HEAD_DIM] = context[
                h * QUERY_BLOCK : (h + 1) * QUERY_BLOCK
            ]
    copies[0].wait()
    branch = dot(ctx_ref[...], weight_rows(wa_ref, 0, QUERY_COLS), 1, 0)
    branch_ref[...] = branch
    middle = stream_ref[...] + rms_norm(branch, gain_of(gains_ref, POST_ATTN))
    middle_ref[...] = middle
    ffn_normed = rms_norm(middle, gain_of(gains_ref, PRE_FFN)).astype(BF16)
    fn_ref[...] = ffn_normed
    copies[1].wait()
    copies[2].wait()
    hidden = inner_ref.shape[1]
    total = jnp.zeros(branch_ref.shape, F32)
    for start in range(0, hidden, HIDDEN_BLOCK):
        gate_cols = slice(start, start + HIDDEN_BLOCK)
        up_cols = slice(hidden + start, hidden + start + HIDDEN_BLOCK)
        gate = dot(ffn_normed, weight_rows(wi_ref, start, HIDDEN_BLOCK), 1, 1)
        up = dot(ffn_normed, weight_rows(wi_ref, hidden + start, HIDDEN_BLOCK), 1, 1)
        gu_ref[:, gate_cols] = gate.astype(BF16)
        gu_ref[:, up_cols] = up.astype(BF16)
        inner = (gelu_parts(gate)[1] * up).astype(BF16)
        inner_ref[:, gate_cols] = inner
        total += dot(inner, weight_rows(wo_ref, start, HIDDEN_BLOCK), 1, 0)
    fb_ref[...] = total
    result_ref[...] = middle + rms_norm(total, gain_of(gains_ref, POST_FFN))


def forward_layer(stream, weights, gains, tables, reach, count):
    tokens = stream.shape[0]
    cosine_tab, sine_tab = tables
    attn_in, attn_out, ffn_in, ffn_out = weights
    hidden = ffn_out[0].shape[0] * ffn_out[2]
    normed, key_raw, own = call(
        partial(key_value_kernel, [attn_in]), "key_value",
        (stream, gains, cosine_tab, sine_tab), [attn_in],
        [((tokens, D), BF16), ((tokens, HEAD_DIM), F32), ((tokens, 2 * HEAD_DIM), BF16)],
        4 * tokens * D * HEAD_DIM,
    )
    before = neighbour(own, count, False)
    query_raw, queries = call(
        partial(query_kernel, [attn_in]), "query",
        (normed, gains, cosine_tab, sine_tab), [attn_in],
        [((tokens, QUERY_COLS), F32), ((tokens, QUERY_COLS), BF16)],
        2 * tokens * D * QUERY_COLS,
    )
    context, lse, branch, middle, ffn_normed, gate_up, inner, ffn_branch, result = call(
        partial(block_kernel, [attn_out, ffn_in, ffn_out]), "block_forward",
        (queries, before, own, reach, stream, gains), [attn_out, ffn_in, ffn_out],
        [
            ((tokens, QUERY_COLS), BF16), (reach.shape, F32), ((tokens, D), F32), ((tokens, D), F32),
            ((tokens, D), BF16), ((tokens, 2 * hidden), BF16), ((tokens, hidden), BF16),
            ((tokens, D), F32), ((tokens, D), F32),
        ],
        2 * tokens * (D * (QUERY_COLS + 3 * hidden) + 2 * QUERY_COLS * KEY_COUNT),
    )
    record = (
        stream, normed, query_raw, key_raw, queries, before, own, lse, context,
        branch, middle, ffn_normed, gate_up, inner, ffn_branch,
    )
    return record, result


def block_backward_kernel(
    weights, grad_ref, fb_ref, gu_ref, middle_ref, branch_ref, gains_ref, wa_any, wi_any, wo_any,
    gfb_ref, ggu_ref, gb_ref, gctx_ref, gmid_ref, sums_ref,
    wa_ref, wi_ref, wo_ref, sem,
):
    copies = [
        fetch(weight, source, target, sem.at[i])
        for i, (weight, source, target) in enumerate(
            zip(weights, (wa_any, wi_any, wo_any), (wa_ref, wi_ref, wo_ref))
        )
    ]
    grad_out = grad_ref[...]
    grad_ffn_branch, post_ffn = rms_backward(fb_ref[...], gain_of(gains_ref, POST_FFN), grad_out)
    grad_ffn_branch = grad_ffn_branch.astype(BF16)
    gfb_ref[...] = grad_ffn_branch
    copies[2].wait()
    copies[1].wait()
    hidden = gu_ref.shape[1] // 2
    total = jnp.zeros(grad_ref.shape, F32)
    for start in range(0, hidden, HIDDEN_BLOCK):
        gate_cols = slice(start, start + HIDDEN_BLOCK)
        up_cols = slice(hidden + start, hidden + start + HIDDEN_BLOCK)
        grad_inner = dot(grad_ffn_branch, weight_rows(wo_ref, start, HIDDEN_BLOCK), 1, 1)
        gate = gu_ref[:, gate_cols].astype(F32)
        up = gu_ref[:, up_cols].astype(F32)
        tanh, value = gelu_parts(gate)
        slope = 0.5 * (1.0 + tanh) + 0.5 * gate * (1.0 - tanh * tanh) * GELU_A * (
            1.0 + 3.0 * GELU_B * gate * gate
        )
        grad_gate = (grad_inner * up * slope).astype(BF16)
        grad_up = (grad_inner * value).astype(BF16)
        ggu_ref[:, gate_cols] = grad_gate
        ggu_ref[:, up_cols] = grad_up
        total += dot(grad_gate, weight_rows(wi_ref, start, HIDDEN_BLOCK), 1, 0)
        total += dot(grad_up, weight_rows(wi_ref, hidden + start, HIDDEN_BLOCK), 1, 0)
    grad_part, pre_ffn = rms_backward(middle_ref[...], gain_of(gains_ref, PRE_FFN), total)
    grad_middle = grad_out + grad_part
    gmid_ref[...] = grad_middle
    grad_branch, post_attn = rms_backward(branch_ref[...], gain_of(gains_ref, POST_ATTN), grad_middle)
    grad_branch = grad_branch.astype(BF16)
    gb_ref[...] = grad_branch
    sums_ref[0:1, :] = post_attn
    sums_ref[1:2, :] = pre_ffn
    sums_ref[2:3, :] = post_ffn
    copies[0].wait()
    gctx_ref[...] = dot(grad_branch, weight_rows(wa_ref, 0, QUERY_COLS), 1, 1).astype(BF16)


def attention_backward_kernel(
    q_ref, before_ref, own_ref, reach_ref, lse_ref, g_ref, dq_ref, gbefore_ref, gown_ref, acc
):
    acc[...] = jnp.zeros_like(acc)
    for block in range(q_ref.shape[0] // QUERY_BLOCK):
        start = block * QUERY_BLOCK
        queries = stacked_heads(q_ref, start)
        grads = stacked_heads(g_ref, start)
        keys = window_rows(before_ref, own_ref, start, KEY_COUNT, KEYS)
        values = window_rows(before_ref, own_ref, start, KEY_COUNT, VALUES)
        allowed = allowed_pairs(start, KEY_COUNT, reach_ref[block : block + 1, :], HEADS * QUERY_BLOCK)
        scores = jnp.where(allowed, dot(keys, queries, 1, 1), MASKED_SCORE)
        probs = jnp.exp(scores - lse_ref[block : block + 1, :])
        grad_probs = dot(values, grads, 1, 1)
        inner = jnp.sum(probs * grad_probs, axis=0, keepdims=True)
        grad_scores = (probs * (grad_probs - inner)).astype(BF16)
        acc[start : start + KEY_COUNT, VALUES] += dot(probs.astype(BF16), grads, 1, 0)
        acc[start : start + KEY_COUNT, KEYS] += dot(grad_scores, queries, 1, 0)
        grad_queries = dot(grad_scores, keys, 0, 0) * SCORE_SCALE
        for h in range(HEADS):
            dq_ref[start : start + QUERY_BLOCK, h * HEAD_DIM : (h + 1) * HEAD_DIM] = grad_queries[
                h * QUERY_BLOCK : (h + 1) * QUERY_BLOCK
            ]
    gbefore_ref[...] = acc[:WINDOW, :].astype(BF16)
    gown_ref[...] = acc[WINDOW:, :]


def query_backward_kernel(dq_ref, raw_ref, gains_ref, cos_ref, sin_ref, gq_ref, sums_ref):
    cosine_tab, sine_tab = cos_ref[...], sin_ref[...]
    sums = jnp.zeros((1, HEAD_DIM), F32)
    for h in range(HEADS):
        columns = slice(h * HEAD_DIM, (h + 1) * HEAD_DIM)
        grad = rotate_back(dq_ref[:, columns], cosine_tab, sine_tab)
        grad, part = rms_backward(raw_ref[:, columns], gain_of(gains_ref, QUERY_GAIN), grad)
        gq_ref[:, columns] = grad.astype(BF16)
        sums += part
    sums_ref[...] = sums


def input_backward_kernel(
    weights, gq_ref, gown_ref, got_ref, kraw_ref, gmid_ref, stream_ref, gains_ref, cos_ref, sin_ref, w_any,
    gproj_ref, gin_ref, sums_ref, key_sums_ref, w_ref, sem,
):
    copy = fetch(weights[0], w_any, w_ref, sem.at[0])
    total = gown_ref[...] + got_ref[...].astype(F32)
    grad_keys = rotate_back(total[:, KEYS], cos_ref[...], sin_ref[...])
    grad_keys, key_sums = rms_backward(kraw_ref[...], gain_of(gains_ref, KEY_GAIN), grad_keys)
    gproj_ref[:, :QUERY_COLS] = gq_ref[...]
    gproj_ref[:, QUERY_COLS : QUERY_COLS + HEAD_DIM] = grad_keys.astype(BF16)
    gproj_ref[:, QUERY_COLS + HEAD_DIM :] = total[:, VALUES].astype(BF16)
    key_sums_ref[...] = key_sums
    copy.wait()
    grad_normed = dot(gproj_ref[...], weight_rows(w_ref, 0, QUERY_COLS + 2 * HEAD_DIM), 1, 0)
    grad_part, sums = rms_backward(stream_ref[...], gain_of(gains_ref, PRE_ATTN), grad_normed)
    gin_ref[...] = gmid_ref[...] + grad_part
    sums_ref[...] = sums


def backward_layer(grad_out, weights, gains, record, tables, reach, count, pump, chains):
    attn_in, attn_out, ffn_in, ffn_out = weights
    cosine_tab, sine_tab = tables
    (
        stream, normed, query_raw, key_raw, queries, before, own, lse, context,
        branch, middle, ffn_normed, gate_up, inner, ffn_branch,
    ) = record
    tokens = stream.shape[0]
    hidden = inner.shape[1]
    grad_out = pump(0, grad_out)
    grad_ffn_branch, grad_gate_up, grad_branch, grad_context, grad_middle, sums = call(
        partial(block_backward_kernel, [attn_out, ffn_in, ffn_out]), "block_backward",
        (grad_out, ffn_branch, gate_up, middle, branch, gains), [attn_out, ffn_in, ffn_out],
        [
            ((tokens, D), BF16), ((tokens, 2 * hidden), BF16), ((tokens, D), BF16),
            ((tokens, QUERY_COLS), BF16), ((tokens, D), F32), ((8, D), F32),
        ],
        2 * tokens * D * (QUERY_COLS + 3 * hidden),
    )
    chains["ffn_in"] = Chain(grad_gate_up, ffn_normed, "dp")
    chains["ffn_out"] = Chain(inner, grad_ffn_branch, "seq")
    chains["attn_out"] = Chain(context, grad_branch, "seq")
    grad_context = pump(1, grad_context)
    grad_queries, grad_before, grad_own = call(
        attention_backward_kernel, "attention_backward",
        (queries, before, own, reach, lse, grad_context), [],
        [((tokens, QUERY_COLS), F32), ((WINDOW, 2 * HEAD_DIM), BF16), ((tokens, 2 * HEAD_DIM), F32)],
        10 * tokens * QUERY_COLS * KEY_COUNT,
        [pltpu.VMEM((WINDOW + tokens, 2 * HEAD_DIM), F32)],
    )
    got = neighbour(grad_before, count, True)
    grad_queries = pump(2, grad_queries)
    grad_query_raw, query_sums = call(
        query_backward_kernel, "query_backward",
        (grad_queries, query_raw, gains, cosine_tab, sine_tab), [],
        [((tokens, QUERY_COLS), BF16), ((1, HEAD_DIM), F32)],
        20 * tokens * QUERY_COLS,
    )
    grad_query_raw = pump(3, grad_query_raw)
    grad_projected, grad_in, pre_sums, key_sums = call(
        partial(input_backward_kernel, [attn_in]), "input_backward",
        (grad_query_raw, grad_own, got, key_raw, grad_middle, stream, gains, cosine_tab, sine_tab),
        [attn_in],
        [
            ((tokens, QUERY_COLS + 2 * HEAD_DIM), BF16), ((tokens, D), F32), ((1, D), F32),
            ((1, HEAD_DIM), F32),
        ],
        2 * tokens * D * (QUERY_COLS + 2 * HEAD_DIM),
    )
    chains["attn_in"] = Chain(grad_projected, normed, "dp")
    grad_gain_row = jnp.concatenate(
        [pre_sums[0], sums[0], sums[1], sums[2], query_sums[0], key_sums[0]]
    )
    return grad_in, grad_gain_row


PLAN = {
    0: [(1, "attn_out"), (1, "ffn_out"), (1, "attn_in")],
    1: [(0, "ffn_in"), (0, "ffn_out"), (1, "ffn_in"), (1, "attn_in"), (1, "attn_out")],
    2: [(0, "attn_out"), (1, "ffn_out"), (1, "attn_in"), (1, "attn_out")],
    3: [(0, "ffn_out"), (1, "ffn_in"), (1, "attn_out")],
}


def gather_weights(w_attn_in, w_attn_out, w_ffn_in, w_ffn_out, gains):
    layers = w_attn_in.shape[0]
    kinds = [w_ffn_in.transpose(0, 2, 1), w_ffn_out, w_attn_in.transpose(0, 2, 1), w_attn_out]
    gain_rows = jnp.pad(gains, ((0, 16 - layers), (0, D - gains.shape[1])))
    packed = jnp.concatenate([kind.reshape(-1, D) for kind in kinds] + [gain_rows], axis=0)
    whole = lax.all_gather(packed, ALL, axis=0, tiled=False)
    out, at = [[] for _ in range(layers)], 0
    for kind in kinds:
        for layer in range(layers):
            out[layer].append((at, kind.shape[1]))
            at += kind.shape[1]
    gain_full = whole[:, at : at + layers, : gains.shape[1]].astype(F32)

    def of(layer):
        found = []
        for start, size in out[layer]:
            if size % TILE:
                found.append((whole[:, start : start + size].reshape(1, -1, D), 0, size * whole.shape[0]))
            else:
                found.append((whole, start, size))
        ffn_in, ffn_out, attn_in, attn_out = found
        return (attn_in, attn_out, ffn_in, ffn_out), gain_full[:, layer].reshape(1, -1)

    return of


def body(hidden_in, positions, out_grad, w_attn_in, w_attn_out, w_ffn_in, w_ffn_out, gains):
    count = hidden_in.shape[0]
    layer_count = w_attn_in.shape[0]
    layer_weights = gather_weights(w_attn_in, w_attn_out, w_ffn_in, w_ffn_out, gains)
    places = to_long(positions)
    stream = to_long(hidden_in).astype(F32)
    grad_stream = to_long(out_grad).astype(F32)
    tables = angle_tables(places)
    tokens = places.shape[0]
    blocks = tokens // QUERY_BLOCK
    reach = jnp.minimum(places, WINDOW - 1).reshape(blocks, QUERY_BLOCK)
    reach = jnp.tile(reach, (1, HEADS))
    records, weights = [], []
    for layer_index in range(layer_count):
        weights.append(layer_weights(layer_index))
        record, stream = forward_layer(stream, *weights[-1], tables, reach, count)
        records.append(record)
    hidden_out = to_short(stream.astype(BF16), count)
    gain_grads = [None] * layer_count
    chains = [{} for _ in range(layer_count + 1)]
    for layer_index in reversed(range(layer_count)):

        def pump(where, value):
            active = [
                chains[layer_index + above][name]
                for above, name in PLAN[where]
                if name in chains[layer_index + above]
            ]
            return advance(value, [chain for chain in active if chain.steps])

        grad_stream, gain_grads[layer_index] = backward_layer(
            grad_stream, *weights[layer_index], records[layer_index], tables, reach, count, pump,
            chains[layer_index],
        )
    input_grad = to_short(grad_stream.astype(BF16), count).astype(F32)
    devices = lax.axis_size("dp") * lax.axis_size("seq")
    gain_grads = halving(jnp.stack([entry.reshape(devices, -1) for entry in gain_grads], axis=1))
    members = {
        name: jnp.stack([chains[layer][name].finish() for layer in range(layer_count)])
        for name in chains[0]
    }
    return (
        hidden_out,
        input_grad,
        members["attn_in"].transpose(0, 2, 1),
        members["attn_out"],
        members["ffn_in"].transpose(0, 2, 1),
        members["ffn_out"],
        gain_grads,
    )


def solution(mesh):
    return jax.shard_map(
        body,
        mesh=mesh,
        in_specs=(
            P("dp", "seq", None),
            P("dp", "seq"),
            P("dp", "seq", None),
            P(None, None, ("dp", "seq")),
            P(None, ("dp", "seq"), None),
            P(None, None, ("dp", "seq")),
            P(None, ("dp", "seq"), None),
            P(None, ("dp", "seq")),
        ),
        out_specs=(
            P("dp", "seq", None),
            P("dp", "seq", None),
            P(None, None, ("dp", "seq")),
            P(None, ("dp", "seq"), None),
            P(None, None, ("dp", "seq")),
            P(None, ("dp", "seq"), None),
            P(None, ("dp", "seq")),
        ),
        check_vma=False,
    )
```

```python
from functools import partial

import jax
import jax.numpy as jnp
from jax import lax
from jax.experimental import pallas as pl
from jax.experimental.pallas import tpu as pltpu
from jax.sharding import PartitionSpec as P

D = 640
HEADS = 4
HEAD_DIM = 256
WINDOW = 512
QUERY_BLOCK = 256

EPSILON = 1e-06
ROPE_BASE = 10000.0
SCORE_SCALE = 0.0625
MASKED_SCORE = -1e30
BF16 = jnp.bfloat16
F32 = jnp.float32
ALL = ("dp", "seq")
TILE = 16
QUERY_COLS = HEADS * HEAD_DIM
GELU_A = 0.7978845608028654
GELU_B = 0.044715
HIDDEN_BLOCK = 512


def dot(a, b, a_dim, b_dim):
    return lax.dot_general(a, b, (((a_dim,), (b_dim,)), ((), ())), preferred_element_type=F32)


def angle_tables(places):
    half_dim = HEAD_DIM // 2
    inverse = ROPE_BASE ** (-(2.0 * jnp.arange(half_dim, dtype=F32)) / HEAD_DIM)
    phases = places.astype(F32)[..., None] * inverse
    return (jnp.cos(phases), jnp.sin(phases))


def inverse_rms(values):
    return lax.rsqrt(jnp.mean(values * values, axis=-1, keepdims=True) + EPSILON)


def rms_norm(values, gain):
    return values * inverse_rms(values) * gain


def rms_backward(values, gain, grad):
    scale = inverse_rms(values)
    weighted = grad * gain
    shared = jnp.mean(weighted * values, axis=-1, keepdims=True) * (scale * scale * scale)
    grad_gain = jnp.sum(grad * (values * scale), axis=0, keepdims=True)
    return weighted * scale - values * shared, grad_gain


def rotate(values, cosine_tab, sine_tab):
    half_dim = HEAD_DIM // 2
    first, second = values[:, :half_dim], values[:, half_dim:]
    return jnp.concatenate(
        [first * cosine_tab - second * sine_tab, second * cosine_tab + first * sine_tab], axis=-1
    )


def rotate_back(values, cosine_tab, sine_tab):
    return rotate(values, cosine_tab, -sine_tab)


def gain_of(gains_ref, which):
    starts = (0, D, 2 * D, 3 * D, 4 * D, 4 * D + HEAD_DIM)
    return gains_ref[:, starts[which] : starts[which] + (D if which < 4 else HEAD_DIM)]


PRE_ATTN, POST_ATTN, PRE_FFN, POST_FFN, QUERY_GAIN, KEY_GAIN = range(6)


def weight_rows(ref, start, size):
    shards, rows, width = ref.shape
    if shards == 1:
        return ref[0, start : start + size, :]
    first, last = start // rows, -(-(start + size) // rows)
    value = ref[first:last].reshape((last - first) * rows, width)
    skip = start - first * rows
    return value[skip : skip + size]


def fetch(weight, ref, scratch, sem):
    _, start, rows = weight
    copy = pltpu.make_async_copy(ref.at[:, pl.ds(start, rows), :], scratch, sem)
    copy.start()
    return copy


def weight_scratch(weight):
    array, _, rows = weight
    return pltpu.VMEM((array.shape[0], rows, D), BF16)


def vmem(count):
    return [pl.BlockSpec(memory_space=pltpu.VMEM)] * count


def call(kernel, name, arrays, weights, outs, flops, scratch=()):
    outs = [jax.ShapeDtypeStruct(shape, dtype) for shape, dtype in outs]
    moved = sum(a.size * a.dtype.itemsize for a in list(arrays) + outs)
    return pl.pallas_call(
        kernel,
        out_shape=tuple(outs),
        in_specs=vmem(len(arrays)) + [pl.BlockSpec(memory_space=pl.ANY)] * len(weights),
        out_specs=tuple(vmem(len(outs))),
        scratch_shapes=[weight_scratch(w) for w in weights]
        + ([pltpu.SemaphoreType.DMA((len(weights),))] if weights else [])
        + list(scratch),
        compiler_params=pltpu.CompilerParams(vmem_limit_bytes=VMEM_LIMIT),
        cost_estimate=pl.CostEstimate(flops=flops, bytes_accessed=moved, transcendentals=0),
        name=name,
    )(*arrays, *[w[0] for w in weights])


VMEM_LIMIT = 44 * 2**20


def chunk_route(count, k):
    n_dp, n_seq = lax.axis_size("dp"), lax.axis_size("seq")
    chips = n_seq // (2 * count)
    pairs = []
    for dp in range(n_dp):
        for i in range(n_seq):
            chunk = i // count
            sequence = (dp % 2) * count + (i + k) % count
            target_dp = dp - dp % 2 + chunk % 2
            pairs.append((dp * n_seq + i, target_dp * n_seq + sequence * chips + chunk // 2))
    return pairs


def place(count):
    chips = lax.axis_size("seq") // (2 * count)
    return (lax.axis_index("seq") // chips) % count


def to_long(block):
    count = block.shape[0]
    me = lax.axis_index("seq")
    received = []
    for k in range(count):
        piece = lax.dynamic_index_in_dim(block, (me + k) % count, 0, keepdims=False)
        received.append(lax.ppermute(piece, ALL, chunk_route(count, k)))
    twice = jnp.stack((received[::-1] * 2)[: 2 * count - 1])
    long = lax.dynamic_slice_in_dim(twice, count - 1 - place(count), count, 0)
    return long.reshape((count * block.shape[1],) + block.shape[2:])


def to_short(long, count):
    me = lax.axis_index("seq")
    parts = long.reshape((count, long.shape[0] // count) + long.shape[1:])
    received = []
    for k in range(count):
        piece = lax.dynamic_index_in_dim(parts, (place(count) - k) % count, 0, keepdims=False)
        route = [(j, i) for i, j in chunk_route(count, k)]
        received.append(lax.ppermute(piece, ALL, route))
    twice = jnp.stack((received * 2)[: 2 * count - 1])
    return lax.dynamic_slice_in_dim(twice, (count - me % count) % count, count, 0)


def neighbour(block, count, back):
    n_dp, n_seq = lax.axis_size("dp"), lax.axis_size("seq")
    chips = n_seq // (2 * count)
    pairs = []
    for dp in range(n_dp):
        for i in range(n_seq):
            if dp % 2 == 0:
                pairs.append((dp * n_seq + i, (dp + 1) * n_seq + i))
            elif (i + 1) % chips:
                pairs.append((dp * n_seq + i, (dp - 1) * n_seq + i + 1))
    if back:
        pairs = [(j, i) for i, j in pairs]
    return lax.ppermute(block, ALL, pairs)


def bits(axis):
    out, bit = [], 1
    while bit < lax.axis_size(axis):
        out.append((axis, bit))
        bit *= 2
    return out


def order(first):
    core, *wide = bits("dp")
    near, *far = bits("seq")
    if first == "dp":
        return [core] + wide + [near] + far[::-1]
    return [core, near] + wide + far[::-1]


def swap(array, step):
    axis, bit = step
    return lax.ppermute(array, axis, [(i, i ^ bit) for i in range(lax.axis_size(axis))])


def launch(value, chains):
    chains = [chain for chain in chains if chain.pending is not None]
    if not chains:
        return value
    held = lax.optimization_barrier((value,) + tuple(chain.pending for chain in chains))
    for chain, pending in zip(chains, held[1:]):
        chain.got = swap(pending, chain.steps[0])
        chain.pending = None
    return held[0]


def advance(value, chains):
    chains = [chain for chain in chains if chain.steps]
    if not chains:
        return value
    held = lax.optimization_barrier((value,) + tuple(chain.got for chain in chains))
    for chain, got in zip(chains, held[1:]):
        chain.got = got
        chain.advance()
    return launch(held[0], chains)


def block_numbers():
    me = lax.axis_index("dp")
    core = me % 2
    wide = [me // 2, (me // 2) ^ 1]
    leave = [2 * w + 1 - core for w in wide]
    stay = [2 * w + core for w in wide]
    return jnp.stack(leave + stay + [lax.axis_index("seq")]).astype(jnp.int32)


def product_kernel(rows, split, added, numbers_ref, a_ref, b_ref, *refs):
    got_ref = refs[0] if added else None
    outs = refs[1 if added else 0 :]
    me = numbers_ref[4]
    width = a_ref.shape[1]
    part = width if width <= 512 else 512
    for start in range(0, width, part):
        total = dot(a_ref[:, start : start + part], b_ref[...], 0, 0)
        for at in range(0, part, rows):
            entry = me ^ ((start + at) // rows)
            value = total[at : at + rows]
            if added:
                value = value + got_ref[0, entry].astype(F32)
            value = value.astype(BF16)
            if split:
                even = lax.rem(entry, 2) == 0

                @pl.when(even)
                def _():
                    outs[0][0, entry // 2] = value

                @pl.when(jnp.logical_not(even))
                def _():
                    outs[1][0, entry // 2] = value

            else:
                outs[0][0, entry] = value


def product(left, right, numbers, first, blocks, got=None, got_first=0, split=False):
    tokens, n_seq = left.shape[0], lax.axis_size("seq")
    width, columns = left.shape[1] // lax.axis_size("dp"), right.shape[1]
    rows = width // n_seq
    out_entries = n_seq // 2 if split else n_seq
    specs = [
        pl.BlockSpec((tokens, width), lambda i, n: (0, n[first + i])),
        pl.BlockSpec((tokens, columns), lambda i, n: (0, 0)),
    ]
    operands = [left, right]
    if got is not None:
        specs.append(pl.BlockSpec((1, n_seq, rows, columns), lambda i, n: (i + got_first, 0, 0, 0)))
        operands.append(got)
    shape = jax.ShapeDtypeStruct((blocks, out_entries, rows, columns), BF16)
    count = 2 if split else 1
    return pl.pallas_call(
        partial(product_kernel, rows, split, got is not None),
        grid_spec=pltpu.PrefetchScalarGridSpec(
            num_scalar_prefetch=1,
            grid=(blocks,),
            in_specs=specs,
            out_specs=[pl.BlockSpec((1, out_entries, rows, columns), lambda i, n: (i, 0, 0, 0))] * count,
        ),
        out_shape=[shape] * count,
        compiler_params=pltpu.CompilerParams(vmem_limit_bytes=24 * 2**20),
        cost_estimate=pl.CostEstimate(
            flops=2 * tokens * width * blocks * columns,
            bytes_accessed=2 * (tokens * width * blocks + tokens * columns + 2 * width * blocks * columns),
            transcendentals=0,
        ),
        name="weight_gradient",
    )(numbers, *operands)


class Chain:
    def __init__(self, left, right, first, extra=None):
        self.steps = order(first)
        self.dims = bits("dp")[::-1] + bits("seq")[::-1]
        n_dp, n_seq = lax.axis_size("dp"), lax.axis_size("seq")
        width = left.shape[1] // n_dp
        self.rows, self.columns = width // n_seq, right.shape[1]
        self.factors = None
        self.extra = None
        self.pending = None
        step = self.steps[0]
        me = lax.axis_index("dp") * n_seq + lax.axis_index("seq")
        if extra is not None:
            extra = jnp.take(extra, me ^ jnp.arange(n_dp * n_seq), axis=0)
        if n_dp == 4 and width % 128 == 0 and self.rows % TILE == 0 and width % n_seq == 0:
            self.factors = (left, right, block_numbers())
            (send,) = product(left, right, self.factors[2], 0, 2)
            self.dims.remove(step)
            if extra is not None:
                extra = extra.reshape((2, 2, n_seq) + extra.shape[1:])
                self.extra = extra[:, 0]
                send = jnp.concatenate([send, extra[:, 1]], axis=2)
            self.pending = send
        else:
            whole = dot(left, right, 0, 0).astype(BF16).reshape(n_dp * n_seq, self.rows, self.columns)
            whole = jnp.take(whole, me ^ jnp.arange(n_dp * n_seq), axis=0)
            if extra is not None:
                whole = jnp.concatenate([whole, extra], axis=1)
                self.rows = whole.shape[1]
            self.send(whole)

    def send(self, array):
        step = self.steps[0]
        array = array.reshape((2,) * len(self.dims) + (self.rows, self.columns))
        at = self.dims.index(step)
        self.dims.remove(step)
        self.keep = lax.index_in_dim(array, 0, at, keepdims=False)
        self.pending = lax.index_in_dim(array, 1, at, keepdims=False)

    def advance(self):
        self.steps = self.steps[1:]
        if self.factors:
            left, right, numbers = self.factors
            self.factors = None
            step = self.steps[0]
            self.dims.remove(step)
            got = self.got
            if self.extra is not None:
                more = (self.extra.astype(F32) + got[:, :, self.rows :].astype(F32)).astype(BF16)
                got = got[:, :, : self.rows]
            if step[0] == "dp":
                (send,) = product(left, right, numbers, 3, 1, got, 1)
                (self.keep,) = product(left, right, numbers, 2, 1, got, 0)
                if self.extra is not None:
                    send = jnp.concatenate([send, more[1:]], axis=2)
                    self.keep = jnp.concatenate([self.keep, more[:1]], axis=2)
                    self.rows = send.shape[2]
            else:
                self.keep, send = product(left, right, numbers, 2, 2, got, 0, True)
            self.pending = send
            return
        array = self.keep.astype(F32) + self.got.reshape(self.keep.shape).astype(F32)
        if self.steps:
            self.send(array.astype(BF16))
        else:
            self.result = array.reshape(self.rows, self.columns)

    def finish(self):
        while self.steps:
            if self.pending is not None:
                self.got = swap(self.pending, self.steps[0])
                self.pending = None
            self.advance()
        return self.result


def allowed_pairs(start, key_count, reach, lanes):
    key_at = lax.broadcasted_iota(jnp.int32, (key_count, lanes), 0)
    query_at = lax.broadcasted_iota(jnp.int32, (key_count, lanes), 1) % QUERY_BLOCK
    distance = query_at + WINDOW - key_at
    return (distance >= 0) & (distance <= reach)


def stacked_heads(ref, start):
    return jnp.concatenate(
        [
            ref[start : start + QUERY_BLOCK, h * HEAD_DIM : (h + 1) * HEAD_DIM]
            for h in range(HEADS)
        ],
        axis=0,
    )


def window_rows(before_ref, own_ref, start, count, columns):
    return jnp.concatenate(
        [before_ref[start:, columns], own_ref[: count - (WINDOW - start), columns]], axis=0
    )


KEYS, VALUES = slice(0, HEAD_DIM), slice(HEAD_DIM, 2 * HEAD_DIM)
KEY_COUNT = QUERY_BLOCK + WINDOW


def key_value_kernel(weights, stream_ref, gains_ref, cos_ref, sin_ref, w_any, normed_ref, raw_ref, own_ref, w_ref, sem):
    copy = fetch(weights[0], w_any, w_ref, sem.at[0])
    normed = rms_norm(stream_ref[...], gain_of(gains_ref, PRE_ATTN)).astype(BF16)
    normed_ref[...] = normed
    copy.wait()
    raw = dot(normed, weight_rows(w_ref, QUERY_COLS, 2 * HEAD_DIM), 1, 1)
    raw_ref[...] = raw[:, KEYS]
    keys = rms_norm(raw[:, KEYS], gain_of(gains_ref, KEY_GAIN))
    own_ref[:, KEYS] = rotate(keys, cos_ref[...], sin_ref[...]).astype(BF16)
    own_ref[:, VALUES] = raw[:, VALUES].astype(BF16)


def query_kernel(weights, normed_ref, gains_ref, cos_ref, sin_ref, w_any, raw_ref, q_ref, w_ref, sem):
    copy = fetch(weights[0], w_any, w_ref, sem.at[0])
    copy.wait()
    cosine_tab, sine_tab = cos_ref[...], sin_ref[...]
    normed = normed_ref[...]
    for h in range(HEADS):
        columns = slice(h * HEAD_DIM, (h + 1) * HEAD_DIM)
        raw = dot(normed, weight_rows(w_ref, h * HEAD_DIM, HEAD_DIM), 1, 1)
        raw_ref[:, columns] = raw
        queries = rotate(rms_norm(raw, gain_of(gains_ref, QUERY_GAIN)), cosine_tab, sine_tab)
        q_ref[:, columns] = queries.astype(BF16) * SCORE_SCALE


def gelu_parts(gate):
    inner = GELU_A * (gate + GELU_B * gate * gate * gate)
    tanh = jnp.tanh(inner)
    return tanh, 0.5 * gate * (1.0 + tanh)


def block_kernel(
    weights, q_ref, before_ref, own_ref, reach_ref, stream_ref, gains_ref, wa_any, wi_any, wo_any,
    ctx_ref, lse_ref, branch_ref, middle_ref, fn_ref, gu_ref, inner_ref, fb_ref, result_ref,
    wa_ref, wi_ref, wo_ref, sem,
):
    copies = [
        fetch(weight, source, target, sem.at[i])
        for i, (weight, source, target) in enumerate(
            zip(weights, (wa_any, wi_any, wo_any), (wa_ref, wi_ref, wo_ref))
        )
    ]
    for block in range(q_ref.shape[0] // QUERY_BLOCK):
        start = block * QUERY_BLOCK
        queries = stacked_heads(q_ref, start)
        keys = window_rows(before_ref, own_ref, start, KEY_COUNT, KEYS)
        values = window_rows(before_ref, own_ref, start, KEY_COUNT, VALUES)
        allowed = allowed_pairs(start, KEY_COUNT, reach_ref[block : block + 1, :], HEADS * QUERY_BLOCK)
        scores = jnp.where(allowed, dot(keys, queries, 1, 1), MASKED_SCORE)
        row_max = jnp.max(scores, axis=0, keepdims=True)
        exps = jnp.exp(scores - row_max)
        row_sum = jnp.sum(exps, axis=0, keepdims=True)
        probs = (exps * (1.0 / row_sum)).astype(BF16)
        lse_ref[block : block + 1, :] = row_max + jnp.log(row_sum)
        context = dot(probs, values, 0, 0).astype(BF16)
        for h in range(HEADS):
            ctx_ref[start : start + QUERY_BLOCK, h * HEAD_DIM : (h + 1) * HEAD_DIM] = context[
                h * QUERY_BLOCK : (h + 1) * QUERY_BLOCK
            ]
    copies[0].wait()
    branch = dot(ctx_ref[...], weight_rows(wa_ref, 0, QUERY_COLS), 1, 0)
    branch_ref[...] = branch
    middle = stream_ref[...] + rms_norm(branch, gain_of(gains_ref, POST_ATTN))
    middle_ref[...] = middle
    ffn_normed = rms_norm(middle, gain_of(gains_ref, PRE_FFN)).astype(BF16)
    fn_ref[...] = ffn_normed
    copies[1].wait()
    copies[2].wait()
    hidden = inner_ref.shape[1]
    total = jnp.zeros(branch_ref.shape, F32)
    for start in range(0, hidden, HIDDEN_BLOCK):
        gate_cols = slice(start, start + HIDDEN_BLOCK)
        up_cols = slice(hidden + start, hidden + start + HIDDEN_BLOCK)
        gate = dot(ffn_normed, weight_rows(wi_ref, start, HIDDEN_BLOCK), 1, 1)
        up = dot(ffn_normed, weight_rows(wi_ref, hidden + start, HIDDEN_BLOCK), 1, 1)
        gu_ref[:, gate_cols] = gate.astype(BF16)
        gu_ref[:, up_cols] = up.astype(BF16)
        inner = (gelu_parts(gate)[1] * up).astype(BF16)
        inner_ref[:, gate_cols] = inner
        total += dot(inner, weight_rows(wo_ref, start, HIDDEN_BLOCK), 1, 0)
    fb_ref[...] = total
    result_ref[...] = middle + rms_norm(total, gain_of(gains_ref, POST_FFN))


def forward_layer(stream, weights, gains, tables, reach, count):
    tokens = stream.shape[0]
    cosine_tab, sine_tab = tables
    attn_in, attn_out, ffn_in, ffn_out = weights
    hidden = ffn_out[0].shape[0] * ffn_out[2]
    normed, key_raw, own = call(
        partial(key_value_kernel, [attn_in]), "key_value",
        (stream, gains, cosine_tab, sine_tab), [attn_in],
        [((tokens, D), BF16), ((tokens, HEAD_DIM), F32), ((tokens, 2 * HEAD_DIM), BF16)],
        4 * tokens * D * HEAD_DIM,
    )
    before = neighbour(own, count, False)
    query_raw, queries = call(
        partial(query_kernel, [attn_in]), "query",
        (normed, gains, cosine_tab, sine_tab), [attn_in],
        [((tokens, QUERY_COLS), F32), ((tokens, QUERY_COLS), BF16)],
        2 * tokens * D * QUERY_COLS,
    )
    context, lse, branch, middle, ffn_normed, gate_up, inner, ffn_branch, result = call(
        partial(block_kernel, [attn_out, ffn_in, ffn_out]), "block_forward",
        (queries, before, own, reach, stream, gains), [attn_out, ffn_in, ffn_out],
        [
            ((tokens, QUERY_COLS), BF16), (reach.shape, F32), ((tokens, D), F32), ((tokens, D), F32),
            ((tokens, D), BF16), ((tokens, 2 * hidden), BF16), ((tokens, hidden), BF16),
            ((tokens, D), F32), ((tokens, D), F32),
        ],
        2 * tokens * (D * (QUERY_COLS + 3 * hidden) + 2 * QUERY_COLS * KEY_COUNT),
    )
    record = (
        stream, normed, query_raw, key_raw, queries, before, own, lse, context,
        branch, middle, ffn_normed, gate_up, inner, ffn_branch,
    )
    return record, result


def block_backward_kernel(
    weights, grad_ref, fb_ref, gu_ref, middle_ref, branch_ref, gains_ref, wa_any, wi_any, wo_any,
    gfb_ref, ggu_ref, gb_ref, gctx_ref, gmid_ref, sums_ref,
    wa_ref, wi_ref, wo_ref, sem,
):
    copies = [
        fetch(weight, source, target, sem.at[i])
        for i, (weight, source, target) in enumerate(
            zip(weights, (wa_any, wi_any, wo_any), (wa_ref, wi_ref, wo_ref))
        )
    ]
    grad_out = grad_ref[...]
    grad_ffn_branch, post_ffn = rms_backward(fb_ref[...], gain_of(gains_ref, POST_FFN), grad_out)
    grad_ffn_branch = grad_ffn_branch.astype(BF16)
    gfb_ref[...] = grad_ffn_branch
    copies[2].wait()
    copies[1].wait()
    hidden = gu_ref.shape[1] // 2
    total = jnp.zeros(grad_ref.shape, F32)
    for start in range(0, hidden, HIDDEN_BLOCK):
        gate_cols = slice(start, start + HIDDEN_BLOCK)
        up_cols = slice(hidden + start, hidden + start + HIDDEN_BLOCK)
        grad_inner = dot(grad_ffn_branch, weight_rows(wo_ref, start, HIDDEN_BLOCK), 1, 1)
        gate = gu_ref[:, gate_cols].astype(F32)
        up = gu_ref[:, up_cols].astype(F32)
        tanh, value = gelu_parts(gate)
        slope = 0.5 * (1.0 + tanh) + 0.5 * gate * (1.0 - tanh * tanh) * GELU_A * (
            1.0 + 3.0 * GELU_B * gate * gate
        )
        grad_gate = (grad_inner * up * slope).astype(BF16)
        grad_up = (grad_inner * value).astype(BF16)
        ggu_ref[:, gate_cols] = grad_gate
        ggu_ref[:, up_cols] = grad_up
        total += dot(grad_gate, weight_rows(wi_ref, start, HIDDEN_BLOCK), 1, 0)
        total += dot(grad_up, weight_rows(wi_ref, hidden + start, HIDDEN_BLOCK), 1, 0)
    grad_part, pre_ffn = rms_backward(middle_ref[...], gain_of(gains_ref, PRE_FFN), total)
    grad_middle = grad_out + grad_part
    gmid_ref[...] = grad_middle
    grad_branch, post_attn = rms_backward(branch_ref[...], gain_of(gains_ref, POST_ATTN), grad_middle)
    grad_branch = grad_branch.astype(BF16)
    gb_ref[...] = grad_branch
    sums_ref[0:1, :] = post_attn
    sums_ref[1:2, :] = pre_ffn
    sums_ref[2:3, :] = post_ffn
    copies[0].wait()
    gctx_ref[...] = dot(grad_branch, weight_rows(wa_ref, 0, QUERY_COLS), 1, 1).astype(BF16)


def attention_backward_kernel(
    q_ref, before_ref, own_ref, reach_ref, lse_ref, g_ref, dq_ref, gbefore_ref, gown_ref, acc
):
    acc[...] = jnp.zeros_like(acc)
    for block in range(q_ref.shape[0] // QUERY_BLOCK):
        start = block * QUERY_BLOCK
        queries = stacked_heads(q_ref, start)
        grads = stacked_heads(g_ref, start)
        keys = window_rows(before_ref, own_ref, start, KEY_COUNT, KEYS)
        values = window_rows(before_ref, own_ref, start, KEY_COUNT, VALUES)
        allowed = allowed_pairs(start, KEY_COUNT, reach_ref[block : block + 1, :], HEADS * QUERY_BLOCK)
        scores = jnp.where(allowed, dot(keys, queries, 1, 1), MASKED_SCORE)
        probs = jnp.exp(scores - lse_ref[block : block + 1, :])
        grad_probs = dot(values, grads, 1, 1)
        inner = jnp.sum(probs * grad_probs, axis=0, keepdims=True)
        grad_scores = (probs * (grad_probs - inner)).astype(BF16)
        acc[start : start + KEY_COUNT, VALUES] += dot(probs.astype(BF16), grads, 1, 0)
        acc[start : start + KEY_COUNT, KEYS] += dot(grad_scores, queries, 1, 0)
        grad_queries = dot(grad_scores, keys, 0, 0) * SCORE_SCALE
        for h in range(HEADS):
            dq_ref[start : start + QUERY_BLOCK, h * HEAD_DIM : (h + 1) * HEAD_DIM] = grad_queries[
                h * QUERY_BLOCK : (h + 1) * QUERY_BLOCK
            ]
    gbefore_ref[...] = acc[:WINDOW, :].astype(BF16)
    gown_ref[...] = acc[WINDOW:, :]


def query_backward_kernel(dq_ref, raw_ref, gains_ref, cos_ref, sin_ref, gq_ref, sums_ref):
    cosine_tab, sine_tab = cos_ref[...], sin_ref[...]
    sums = jnp.zeros((1, HEAD_DIM), F32)
    for h in range(HEADS):
        columns = slice(h * HEAD_DIM, (h + 1) * HEAD_DIM)
        grad = rotate_back(dq_ref[:, columns], cosine_tab, sine_tab)
        grad, part = rms_backward(raw_ref[:, columns], gain_of(gains_ref, QUERY_GAIN), grad)
        gq_ref[:, columns] = grad.astype(BF16)
        sums += part
    sums_ref[...] = sums


def input_backward_kernel(
    weights, gq_ref, gown_ref, got_ref, kraw_ref, gmid_ref, stream_ref, gains_ref, cos_ref, sin_ref, w_any,
    gproj_ref, gin_ref, sums_ref, key_sums_ref, w_ref, sem,
):
    copy = fetch(weights[0], w_any, w_ref, sem.at[0])
    total = gown_ref[...] + got_ref[...].astype(F32)
    grad_keys = rotate_back(total[:, KEYS], cos_ref[...], sin_ref[...])
    grad_keys, key_sums = rms_backward(kraw_ref[...], gain_of(gains_ref, KEY_GAIN), grad_keys)
    gproj_ref[:, :QUERY_COLS] = gq_ref[...]
    gproj_ref[:, QUERY_COLS : QUERY_COLS + HEAD_DIM] = grad_keys.astype(BF16)
    gproj_ref[:, QUERY_COLS + HEAD_DIM :] = total[:, VALUES].astype(BF16)
    key_sums_ref[...] = key_sums
    copy.wait()
    grad_normed = dot(gproj_ref[...], weight_rows(w_ref, 0, QUERY_COLS + 2 * HEAD_DIM), 1, 0)
    grad_part, sums = rms_backward(stream_ref[...], gain_of(gains_ref, PRE_ATTN), grad_normed)
    gin_ref[...] = gmid_ref[...] + grad_part
    sums_ref[...] = sums


def backward_layer(grad_out, weights, gains, record, tables, reach, count, pump, chains):
    attn_in, attn_out, ffn_in, ffn_out = weights
    cosine_tab, sine_tab = tables
    (
        stream, normed, query_raw, key_raw, queries, before, own, lse, context,
        branch, middle, ffn_normed, gate_up, inner, ffn_branch,
    ) = record
    tokens = stream.shape[0]
    hidden = inner.shape[1]
    grad_out = pump(0, grad_out)
    grad_ffn_branch, grad_gate_up, grad_branch, grad_context, grad_middle, sums = call(
        partial(block_backward_kernel, [attn_out, ffn_in, ffn_out]), "block_backward",
        (grad_out, ffn_branch, gate_up, middle, branch, gains), [attn_out, ffn_in, ffn_out],
        [
            ((tokens, D), BF16), ((tokens, 2 * hidden), BF16), ((tokens, D), BF16),
            ((tokens, QUERY_COLS), BF16), ((tokens, D), F32), ((8, D), F32),
        ],
        2 * tokens * D * (QUERY_COLS + 3 * hidden),
    )
    cut = 3 * D // 5
    chains["ffn_in"] = Chain(grad_gate_up, ffn_normed[:, :cut], "dp")
    chains["ffn_in_rest"] = Chain(grad_gate_up, ffn_normed[:, cut:], "seq")
    chains["ffn_out"] = Chain(inner, grad_ffn_branch, "dp")
    chains["attn_out"] = Chain(context, grad_branch, "seq")
    grad_context = launch(grad_context, list(chains.values()))
    grad_context = pump(1, grad_context)
    grad_queries, grad_before, grad_own = call(
        attention_backward_kernel, "attention_backward",
        (queries, before, own, reach, lse, grad_context), [],
        [((tokens, QUERY_COLS), F32), ((WINDOW, 2 * HEAD_DIM), BF16), ((tokens, 2 * HEAD_DIM), F32)],
        10 * tokens * QUERY_COLS * KEY_COUNT,
        [pltpu.VMEM((WINDOW + tokens, 2 * HEAD_DIM), F32)],
    )
    got = neighbour(grad_before, count, True)
    grad_queries = pump(2, grad_queries)
    grad_query_raw, query_sums = call(
        query_backward_kernel, "query_backward",
        (grad_queries, query_raw, gains, cosine_tab, sine_tab), [],
        [((tokens, QUERY_COLS), BF16), ((1, HEAD_DIM), F32)],
        20 * tokens * QUERY_COLS,
    )
    grad_query_raw = pump(3, grad_query_raw)
    grad_projected, grad_in, pre_sums, key_sums = call(
        partial(input_backward_kernel, [attn_in]), "input_backward",
        (grad_query_raw, grad_own, got, key_raw, grad_middle, stream, gains, cosine_tab, sine_tab),
        [attn_in],
        [
            ((tokens, QUERY_COLS + 2 * HEAD_DIM), BF16), ((tokens, D), F32), ((1, D), F32),
            ((1, HEAD_DIM), F32),
        ],
        2 * tokens * D * (QUERY_COLS + 2 * HEAD_DIM),
    )
    gain_grads = jnp.concatenate([pre_sums[0], sums[0], sums[1], sums[2], query_sums[0], key_sums[0]])
    devices = lax.axis_size("dp") * lax.axis_size("seq")
    gain_grads = gain_grads.astype(BF16).reshape(devices, 1, -1)
    extra = jnp.pad(gain_grads, ((0, 0), (0, TILE - 1), (0, D - gain_grads.shape[2])))
    chains["attn_in"] = Chain(grad_projected, normed, "dp", extra)
    return launch(grad_in, [chains["attn_in"]])


PLAN = {
    0: [(1, "attn_in"), (1, "attn_out"), (1, "ffn_in_rest"), (1, "ffn_out")],
    1: [
        (0, "ffn_in"), (0, "ffn_in_rest"), (0, "ffn_out"), (0, "attn_out"),
        (1, "ffn_in"), (1, "ffn_in_rest"), (1, "ffn_out"), (1, "attn_in"), (1, "attn_out"),
    ],
    2: [(1, "attn_out"), (1, "attn_in")],
    3: [(1, "ffn_in"), (1, "ffn_in_rest"), (1, "ffn_out")],
    4: [
        (0, "attn_out"), (0, "ffn_in_rest"), (0, "ffn_out"), (1, "attn_in"), (1, "attn_out"),
        (1, "ffn_in"), (1, "ffn_in_rest"), (1, "ffn_out"),
    ],
}


def gather_weights(w_attn_in, w_attn_out, w_ffn_in, w_ffn_out, gains):
    layers = w_attn_in.shape[0]
    kinds = [w_ffn_in.transpose(0, 2, 1), w_ffn_out, w_attn_in.transpose(0, 2, 1), w_attn_out]
    gain_rows = jnp.pad(gains, ((0, 16 - layers), (0, D - gains.shape[1])))
    packed = jnp.concatenate([kind.reshape(-1, D) for kind in kinds] + [gain_rows], axis=0)
    whole = lax.all_gather(packed, ALL, axis=0, tiled=False)
    out, at = [[] for _ in range(layers)], 0
    for kind in kinds:
        for layer in range(layers):
            out[layer].append((at, kind.shape[1]))
            at += kind.shape[1]
    gain_full = whole[:, at : at + layers, : gains.shape[1]].astype(F32)

    def of(layer):
        found = []
        for start, size in out[layer]:
            if size % TILE:
                found.append((whole[:, start : start + size].reshape(1, -1, D), 0, size * whole.shape[0]))
            else:
                found.append((whole, start, size))
        ffn_in, ffn_out, attn_in, attn_out = found
        return (attn_in, attn_out, ffn_in, ffn_out), gain_full[:, layer].reshape(1, -1)

    return of


def body(hidden_in, positions, out_grad, w_attn_in, w_attn_out, w_ffn_in, w_ffn_out, gains):
    count = hidden_in.shape[0]
    layer_count = w_attn_in.shape[0]
    layer_weights = gather_weights(w_attn_in, w_attn_out, w_ffn_in, w_ffn_out, gains)
    places = to_long(positions)
    stream = to_long(hidden_in).astype(F32)
    tables = angle_tables(places)
    tokens = places.shape[0]
    blocks = tokens // QUERY_BLOCK
    reach = jnp.minimum(places, WINDOW - 1).reshape(blocks, QUERY_BLOCK)
    reach = jnp.tile(reach, (1, HEADS))
    records, weights = [], []
    for layer_index in range(layer_count):
        weights.append(layer_weights(layer_index))
        record, stream = forward_layer(stream, *weights[-1], tables, reach, count)
        records.append(record)
        if layer_index == 0:
            stream, out_grad = lax.optimization_barrier((stream, out_grad))
            grad_stream = to_long(out_grad).astype(F32)
    hidden_out = to_short(stream.astype(BF16), count)
    chains = [{} for _ in range(layer_count + 1)]
    for layer_index in reversed(range(layer_count)):

        def pump(where, value):
            active = [
                chains[layer_index + above][name]
                for above, name in PLAN[where]
                if name in chains[layer_index + above]
            ]
            return advance(value, active)

        grad_stream = backward_layer(
            grad_stream, *weights[layer_index], records[layer_index], tables, reach, count, pump,
            chains[layer_index],
        )
    grad_stream = pump(4, grad_stream)
    input_grad = to_short(grad_stream.astype(BF16), count).astype(F32)
    members = {
        name: jnp.stack([chains[layer][name].finish() for layer in range(layer_count)])
        for name in chains[0]
    }
    attn_in_rows = w_attn_in.shape[2]
    ffn_in = jnp.concatenate([members["ffn_in"], members["ffn_in_rest"]], axis=2)
    return (
        hidden_out,
        input_grad,
        members["attn_in"][:, :attn_in_rows].transpose(0, 2, 1),
        members["attn_out"],
        ffn_in.transpose(0, 2, 1),
        members["ffn_out"],
        members["attn_in"][:, attn_in_rows, : gains.shape[1]],
    )


def solution(mesh):
    return jax.shard_map(
        body,
        mesh=mesh,
        in_specs=(
            P("dp", "seq", None),
            P("dp", "seq"),
            P("dp", "seq", None),
            P(None, None, ("dp", "seq")),
            P(None, ("dp", "seq"), None),
            P(None, None, ("dp", "seq")),
            P(None, ("dp", "seq"), None),
            P(None, ("dp", "seq")),
        ),
        out_specs=(
            P("dp", "seq", None),
            P("dp", "seq", None),
            P(None, None, ("dp", "seq")),
            P(None, ("dp", "seq"), None),
            P(None, None, ("dp", "seq")),
            P(None, ("dp", "seq"), None),
            P(None, ("dp", "seq")),
        ),
        check_vma=False,
    )
```

```python
from functools import partial

import jax
import jax.numpy as jnp
from jax import lax
from jax.experimental import pallas as pl
from jax.experimental.pallas import tpu as pltpu
from jax.sharding import PartitionSpec as P

D = 640
HEADS = 4
HEAD_DIM = 256
WINDOW = 512
QUERY_BLOCK = 256

EPSILON = 1e-06
ROPE_BASE = 10000.0
SCORE_SCALE = 0.0625
MASKED_SCORE = -1e30
BF16 = jnp.bfloat16
F32 = jnp.float32
ALL = ("dp", "seq")
TILE = 16
QUERY_COLS = HEADS * HEAD_DIM
GELU_A = 0.7978845608028654
GELU_B = 0.044715
HIDDEN_BLOCK = 512


def dot(a, b, a_dim, b_dim):
    return lax.dot_general(a, b, (((a_dim,), (b_dim,)), ((), ())), preferred_element_type=F32)


def angle_tables(places):
    half_dim = HEAD_DIM // 2
    inverse = ROPE_BASE ** (-(2.0 * jnp.arange(half_dim, dtype=F32)) / HEAD_DIM)
    phases = places.astype(F32)[..., None] * inverse
    return (jnp.cos(phases), jnp.sin(phases))


def inverse_rms(values):
    return lax.rsqrt(jnp.mean(values * values, axis=-1, keepdims=True) + EPSILON)


def rms_norm(values, gain):
    return values * inverse_rms(values) * gain


def rms_backward(values, gain, grad):
    scale = inverse_rms(values)
    weighted = grad * gain
    shared = jnp.mean(weighted * values, axis=-1, keepdims=True) * (scale * scale * scale)
    grad_gain = jnp.sum(grad * (values * scale), axis=0, keepdims=True)
    return weighted * scale - values * shared, grad_gain


def rotate(values, cosine_tab, sine_tab):
    half_dim = HEAD_DIM // 2
    first, second = values[:, :half_dim], values[:, half_dim:]
    return jnp.concatenate(
        [first * cosine_tab - second * sine_tab, second * cosine_tab + first * sine_tab], axis=-1
    )


def rotate_back(values, cosine_tab, sine_tab):
    return rotate(values, cosine_tab, -sine_tab)


def gain_of(gains_ref, which):
    starts = (0, D, 2 * D, 3 * D, 4 * D, 4 * D + HEAD_DIM)
    return gains_ref[:, starts[which] : starts[which] + (D if which < 4 else HEAD_DIM)]


PRE_ATTN, POST_ATTN, PRE_FFN, POST_FFN, QUERY_GAIN, KEY_GAIN = range(6)


def weight_rows(ref, start, size):
    shards, rows, width = ref.shape
    if shards == 1:
        return ref[0, start : start + size, :]
    first, last = start // rows, -(-(start + size) // rows)
    value = ref[first:last].reshape((last - first) * rows, width)
    skip = start - first * rows
    return value[skip : skip + size]


def fetch(weight, ref, scratch, sem):
    _, start, rows = weight
    copy = pltpu.make_async_copy(ref.at[:, pl.ds(start, rows), :], scratch, sem)
    copy.start()
    return copy


def weight_scratch(weight):
    array, _, rows = weight
    return pltpu.VMEM((array.shape[0], rows, D), BF16)


def vmem(count):
    return [pl.BlockSpec(memory_space=pltpu.VMEM)] * count


def call(kernel, name, arrays, weights, outs, flops, scratch=()):
    outs = [jax.ShapeDtypeStruct(shape, dtype) for shape, dtype in outs]
    moved = sum(a.size * a.dtype.itemsize for a in list(arrays) + outs)
    return pl.pallas_call(
        kernel,
        out_shape=tuple(outs),
        in_specs=vmem(len(arrays)) + [pl.BlockSpec(memory_space=pl.ANY)] * len(weights),
        out_specs=tuple(vmem(len(outs))),
        scratch_shapes=[weight_scratch(w) for w in weights]
        + ([pltpu.SemaphoreType.DMA((len(weights),))] if weights else [])
        + list(scratch),
        compiler_params=pltpu.CompilerParams(vmem_limit_bytes=VMEM_LIMIT),
        cost_estimate=pl.CostEstimate(flops=flops, bytes_accessed=moved, transcendentals=0),
        name=name,
    )(*arrays, *[w[0] for w in weights])


VMEM_LIMIT = 44 * 2**20


def chunk_route(count, k):
    n_dp, n_seq = lax.axis_size("dp"), lax.axis_size("seq")
    chips = n_seq // (2 * count)
    pairs = []
    for dp in range(n_dp):
        for i in range(n_seq):
            chunk = i // count
            sequence = (dp % 2) * count + (i + k) % count
            target_dp = dp - dp % 2 + chunk % 2
            pairs.append((dp * n_seq + i, target_dp * n_seq + sequence * chips + chunk // 2))
    return pairs


def place(count):
    chips = lax.axis_size("seq") // (2 * count)
    return (lax.axis_index("seq") // chips) % count


def to_long(block):
    count = block.shape[0]
    me = lax.axis_index("seq")
    received = []
    for k in range(count):
        piece = lax.dynamic_index_in_dim(block, (me + k) % count, 0, keepdims=False)
        received.append(lax.ppermute(piece, ALL, chunk_route(count, k)))
    twice = jnp.stack((received[::-1] * 2)[: 2 * count - 1])
    long = lax.dynamic_slice_in_dim(twice, count - 1 - place(count), count, 0)
    return long.reshape((count * block.shape[1],) + block.shape[2:])


def to_short(long, count):
    me = lax.axis_index("seq")
    parts = long.reshape((count, long.shape[0] // count) + long.shape[1:])
    received = []
    for k in range(count):
        piece = lax.dynamic_index_in_dim(parts, (place(count) - k) % count, 0, keepdims=False)
        route = [(j, i) for i, j in chunk_route(count, k)]
        received.append(lax.ppermute(piece, ALL, route))
    twice = jnp.stack((received * 2)[: 2 * count - 1])
    return lax.dynamic_slice_in_dim(twice, (count - me % count) % count, count, 0)


def neighbour(block, count, back):
    n_dp, n_seq = lax.axis_size("dp"), lax.axis_size("seq")
    chips = n_seq // (2 * count)
    pairs = []
    for dp in range(n_dp):
        for i in range(n_seq):
            if dp % 2 == 0:
                pairs.append((dp * n_seq + i, (dp + 1) * n_seq + i))
            elif (i + 1) % chips:
                pairs.append((dp * n_seq + i, (dp - 1) * n_seq + i + 1))
    if back:
        pairs = [(j, i) for i, j in pairs]
    return lax.ppermute(block, ALL, pairs)


def bits(axis):
    out, bit = [], 1
    while bit < lax.axis_size(axis):
        out.append((axis, bit))
        bit *= 2
    return out


def order(first, scatter):
    core, *wide = bits("dp")
    near, *far = bits("seq")
    if scatter:
        return [core] + wide
    if first == "dp":
        return [core] + wide + [near] + far[::-1]
    return [core, near] + wide + far[::-1]


def swap(array, step):
    axis, bit = step
    return lax.ppermute(array, axis, [(i, i ^ bit) for i in range(lax.axis_size(axis))])


def launch(value, chains):
    chains = [chain for chain in chains if chain.pending is not None]
    if not chains:
        return value
    held = lax.optimization_barrier((value,) + tuple(chain.pending for chain in chains))
    for chain, pending in zip(chains, held[1:]):
        chain.got = swap(pending, chain.steps[0])
        chain.pending = None
    return held[0]


def advance(value, chains):
    chains = [chain for chain in chains if chain.steps]
    if not chains:
        return value
    held = lax.optimization_barrier((value,) + tuple(chain.got for chain in chains))
    for chain, got in zip(chains, held[1:]):
        chain.got = got
        chain.advance()
    return launch(held[0], chains)


def block_numbers(scatter):
    me = lax.axis_index("dp")
    core = me % 2
    wide = [me // 2, (me // 2) ^ 1]
    leave = [2 * w + 1 - core for w in wide]
    stay = [2 * w + core for w in wide]
    along = lax.axis_index("seq") * (0 if scatter else 1)
    return jnp.stack(leave + stay + [along]).astype(jnp.int32)


def product_kernel(pairs, extra, added, split, scatter, columns, n_seq, numbers_ref, *refs):
    lefts, rights, refs = refs[:pairs], refs[pairs : 2 * pairs], refs[2 * pairs :]
    if extra:
        extra_ref, refs = refs[0], refs[1:]
    if added:
        got_ref, refs = refs[0], refs[1:]
    me = numbers_ref[4]

    def store(shard, base, value):
        entry = me ^ shard
        if not scatter:
            entry = lax.rem(entry, 2) * (n_seq // 2) + entry // 2
        place = slice(base, base + value.shape[0])
        if added:
            value = value + got_ref[0, entry, place].astype(F32)
        value = value.astype(BF16)
        if split:
            stays = entry < n_seq // 2

            @pl.when(stays)
            def _():
                refs[0][0, entry, place] = value

            @pl.when(jnp.logical_not(stays))
            def _():
                refs[1][0, entry - n_seq // 2, place] = value

        else:
            refs[0][0, entry, place] = value

    base = 0
    for left, right in zip(lefts, rights):
        width = left.shape[1]
        rows = width // n_seq
        part = min(width, 512)
        for start in range(0, width, part):
            total = dot(left[:, start : start + part], right[:, columns], 0, 0)
            for at in range(0, part, rows):
                store((start + at) // rows, base, total[at : at + rows])
        base += rows
    if extra:
        for shard in range(n_seq):
            store(shard, base, extra_ref[0, shard].astype(F32))


def product(factors, first, blocks, got=None, got_first=0, split=False):
    pairs, extra, numbers, columns, scatter = factors
    n_dp, n_seq = lax.axis_size("dp"), lax.axis_size("seq")
    tokens = pairs[0][0].shape[0]
    wide = columns.stop - columns.start
    widths = [left.shape[1] // n_dp for left, _ in pairs]
    rows = sum(widths) // n_seq + (0 if extra is None else extra.shape[2])
    entries = n_seq // 2 if split else n_seq
    specs = [pl.BlockSpec((tokens, w), lambda i, n: (0, n[first + i])) for w in widths]
    specs += [pl.BlockSpec(right.shape, lambda i, n: (0, 0)) for _, right in pairs]
    operands = [left for left, _ in pairs] + [right for _, right in pairs]
    if extra is not None:
        specs.append(pl.BlockSpec((1,) + extra.shape[1:], lambda i, n: (n[first + i], 0, 0, 0)))
        operands.append(extra)
    if got is not None:
        specs.append(pl.BlockSpec((1, n_seq, rows, wide), lambda i, n: (i + got_first, 0, 0, 0)))
        operands.append(got)
    shape = jax.ShapeDtypeStruct((blocks, entries, rows, wide), BF16)
    count = 2 if split else 1
    return pl.pallas_call(
        partial(
            product_kernel, len(pairs), extra is not None, got is not None, split, scatter, columns, n_seq
        ),
        grid_spec=pltpu.PrefetchScalarGridSpec(
            num_scalar_prefetch=1,
            grid=(blocks,),
            in_specs=specs,
            out_specs=[pl.BlockSpec((1, entries, rows, wide), lambda i, n: (i, 0, 0, 0))] * count,
        ),
        out_shape=[shape] * count,
        compiler_params=pltpu.CompilerParams(vmem_limit_bytes=28 * 2**20),
        cost_estimate=pl.CostEstimate(
            flops=2 * tokens * sum(widths) * blocks * wide,
            bytes_accessed=2 * (tokens + 2 * wide) * sum(widths) * blocks,
            transcendentals=0,
        ),
        name="weight_gradient",
    )(numbers, *operands)


class Chain:
    def __init__(self, pairs, first="dp", scatter=False, columns=slice(0, D), extra=None):
        self.steps = order(first, scatter)
        n_dp, n_seq = lax.axis_size("dp"), lax.axis_size("seq")
        widths = [left.shape[1] // n_dp for left, _ in pairs]
        self.factors = None
        self.shape = (-1, sum(widths) // n_seq + (0 if extra is None else extra.shape[2]), columns.stop - columns.start)
        if n_dp == 4 and all(w % 128 == 0 and w % (n_seq * TILE) == 0 for w in widths):
            self.factors = (pairs, extra, block_numbers(scatter), columns, scatter)
            (self.pending,) = product(self.factors, 0, 2)
            return
        devices = n_dp * n_seq
        parts = [
            dot(left, right[:, columns], 0, 0).astype(BF16).reshape(devices, -1, self.shape[2])
            for left, right in pairs
        ]
        if extra is not None:
            parts.append(extra.reshape(devices, -1, self.shape[2]))
        target = jnp.arange(devices)
        source, left_over = jnp.zeros_like(target), devices
        for axis, bit in self.steps:
            left_over //= 2
            weight = bit * n_seq if axis == "dp" else bit
            source = source + (target // left_over) % 2 * weight
        if scatter:
            source = source + target % n_seq
        me = lax.axis_index("dp") * n_seq
        if not scatter:
            me = me + lax.axis_index("seq")
        self.cut(jnp.take(jnp.concatenate(parts, axis=1), me ^ source, axis=0))

    def cut(self, array):
        half = array.shape[0] // 2
        self.keep, self.pending = array[:half], array[half:]

    def advance(self):
        self.steps = self.steps[1:]
        if self.factors:
            factors, self.factors = self.factors, None
            if self.steps[0][0] == "dp":
                (self.pending,) = product(factors, 3, 1, self.got, 1)
                (self.keep,) = product(factors, 2, 1, self.got, 0)
            else:
                self.keep, self.pending = product(factors, 2, 2, self.got, 0, True)
            self.keep = self.keep.reshape(self.shape)
            self.pending = self.pending.reshape(self.shape)
            return
        array = self.keep.astype(F32) + self.got.astype(F32)
        if self.steps:
            self.cut(array.astype(BF16))
        else:
            self.result = array

    def finish(self):
        while self.steps:
            if self.pending is not None:
                self.got = swap(self.pending, self.steps[0])
                self.pending = None
            self.advance()
        return self.result


def allowed_pairs(start, key_count, reach, lanes):
    key_at = lax.broadcasted_iota(jnp.int32, (key_count, lanes), 0)
    query_at = lax.broadcasted_iota(jnp.int32, (key_count, lanes), 1) % QUERY_BLOCK
    distance = query_at + WINDOW - key_at
    return (distance >= 0) & (distance <= reach)


def stacked_heads(ref, start):
    return jnp.concatenate(
        [
            ref[start : start + QUERY_BLOCK, h * HEAD_DIM : (h + 1) * HEAD_DIM]
            for h in range(HEADS)
        ],
        axis=0,
    )


def window_rows(before_ref, own_ref, start, count, columns):
    return jnp.concatenate(
        [before_ref[start:, columns], own_ref[: count - (WINDOW - start), columns]], axis=0
    )


KEYS, VALUES = slice(0, HEAD_DIM), slice(HEAD_DIM, 2 * HEAD_DIM)
KEY_COUNT = QUERY_BLOCK + WINDOW


def key_value_kernel(weights, stream_ref, gains_ref, cos_ref, sin_ref, w_any, normed_ref, raw_ref, own_ref, w_ref, sem):
    copy = fetch(weights[0], w_any, w_ref, sem.at[0])
    normed = rms_norm(stream_ref[...], gain_of(gains_ref, PRE_ATTN)).astype(BF16)
    normed_ref[...] = normed
    copy.wait()
    raw = dot(normed, weight_rows(w_ref, QUERY_COLS, 2 * HEAD_DIM), 1, 1)
    raw_ref[...] = raw[:, KEYS]
    keys = rms_norm(raw[:, KEYS], gain_of(gains_ref, KEY_GAIN))
    own_ref[:, KEYS] = rotate(keys, cos_ref[...], sin_ref[...]).astype(BF16)
    own_ref[:, VALUES] = raw[:, VALUES].astype(BF16)


def query_kernel(weights, normed_ref, gains_ref, cos_ref, sin_ref, w_any, raw_ref, q_ref, w_ref, sem):
    copy = fetch(weights[0], w_any, w_ref, sem.at[0])
    copy.wait()
    cosine_tab, sine_tab = cos_ref[...], sin_ref[...]
    normed = normed_ref[...]
    for h in range(HEADS):
        columns = slice(h * HEAD_DIM, (h + 1) * HEAD_DIM)
        raw = dot(normed, weight_rows(w_ref, h * HEAD_DIM, HEAD_DIM), 1, 1)
        raw_ref[:, columns] = raw
        queries = rotate(rms_norm(raw, gain_of(gains_ref, QUERY_GAIN)), cosine_tab, sine_tab)
        q_ref[:, columns] = queries.astype(BF16) * SCORE_SCALE


def gelu_parts(gate):
    inner = GELU_A * (gate + GELU_B * gate * gate * gate)
    tanh = jnp.tanh(inner)
    return tanh, 0.5 * gate * (1.0 + tanh)


def block_kernel(
    weights, q_ref, before_ref, own_ref, reach_ref, stream_ref, gains_ref, wa_any, wi_any, wo_any,
    ctx_ref, lse_ref, branch_ref, middle_ref, fn_ref, gu_ref, inner_ref, fb_ref, result_ref,
    wa_ref, wi_ref, wo_ref, sem,
):
    copies = [
        fetch(weight, source, target, sem.at[i])
        for i, (weight, source, target) in enumerate(
            zip(weights, (wa_any, wi_any, wo_any), (wa_ref, wi_ref, wo_ref))
        )
    ]
    for block in range(q_ref.shape[0] // QUERY_BLOCK):
        start = block * QUERY_BLOCK
        queries = stacked_heads(q_ref, start)
        keys = window_rows(before_ref, own_ref, start, KEY_COUNT, KEYS)
        values = window_rows(before_ref, own_ref, start, KEY_COUNT, VALUES)
        allowed = allowed_pairs(start, KEY_COUNT, reach_ref[block : block + 1, :], HEADS * QUERY_BLOCK)
        scores = jnp.where(allowed, dot(keys, queries, 1, 1), MASKED_SCORE)
        row_max = jnp.max(scores, axis=0, keepdims=True)
        exps = jnp.exp(scores - row_max)
        row_sum = jnp.sum(exps, axis=0, keepdims=True)
        probs = (exps * (1.0 / row_sum)).astype(BF16)
        lse_ref[block : block + 1, :] = row_max + jnp.log(row_sum)
        context = dot(probs, values, 0, 0).astype(BF16)
        for h in range(HEADS):
            ctx_ref[start : start + QUERY_BLOCK, h * HEAD_DIM : (h + 1) * HEAD_DIM] = context[
                h * QUERY_BLOCK : (h + 1) * QUERY_BLOCK
            ]
    copies[0].wait()
    branch = dot(ctx_ref[...], weight_rows(wa_ref, 0, QUERY_COLS), 1, 0)
    branch_ref[...] = branch
    middle = stream_ref[...] + rms_norm(branch, gain_of(gains_ref, POST_ATTN))
    middle_ref[...] = middle
    ffn_normed = rms_norm(middle, gain_of(gains_ref, PRE_FFN)).astype(BF16)
    fn_ref[...] = ffn_normed
    copies[1].wait()
    copies[2].wait()
    hidden = inner_ref.shape[1]
    total = jnp.zeros(branch_ref.shape, F32)
    for start in range(0, hidden, HIDDEN_BLOCK):
        gate_cols = slice(start, start + HIDDEN_BLOCK)
        up_cols = slice(hidden + start, hidden + start + HIDDEN_BLOCK)
        gate = dot(ffn_normed, weight_rows(wi_ref, start, HIDDEN_BLOCK), 1, 1)
        up = dot(ffn_normed, weight_rows(wi_ref, hidden + start, HIDDEN_BLOCK), 1, 1)
        gu_ref[:, gate_cols] = gate.astype(BF16)
        gu_ref[:, up_cols] = up.astype(BF16)
        inner = (gelu_parts(gate)[1] * up).astype(BF16)
        inner_ref[:, gate_cols] = inner
        total += dot(inner, weight_rows(wo_ref, start, HIDDEN_BLOCK), 1, 0)
    fb_ref[...] = total
    result_ref[...] = middle + rms_norm(total, gain_of(gains_ref, POST_FFN))


def forward_layer(stream, weights, gains, tables, reach, count):
    tokens = stream.shape[0]
    cosine_tab, sine_tab = tables
    attn_in, attn_out, ffn_in, ffn_out = weights
    hidden = ffn_out[0].shape[0] * ffn_out[2]
    normed, key_raw, own = call(
        partial(key_value_kernel, [attn_in]), "key_value",
        (stream, gains, cosine_tab, sine_tab), [attn_in],
        [((tokens, D), BF16), ((tokens, HEAD_DIM), F32), ((tokens, 2 * HEAD_DIM), BF16)],
        4 * tokens * D * HEAD_DIM,
    )
    before = neighbour(own, count, False)
    query_raw, queries = call(
        partial(query_kernel, [attn_in]), "query",
        (normed, gains, cosine_tab, sine_tab), [attn_in],
        [((tokens, QUERY_COLS), F32), ((tokens, QUERY_COLS), BF16)],
        2 * tokens * D * QUERY_COLS,
    )
    context, lse, branch, middle, ffn_normed, gate_up, inner, ffn_branch, result = call(
        partial(block_kernel, [attn_out, ffn_in, ffn_out]), "block_forward",
        (queries, before, own, reach, stream, gains), [attn_out, ffn_in, ffn_out],
        [
            ((tokens, QUERY_COLS), BF16), (reach.shape, F32), ((tokens, D), F32), ((tokens, D), F32),
            ((tokens, D), BF16), ((tokens, 2 * hidden), BF16), ((tokens, hidden), BF16),
            ((tokens, D), F32), ((tokens, D), F32),
        ],
        2 * tokens * (D * (QUERY_COLS + 3 * hidden) + 2 * QUERY_COLS * KEY_COUNT),
    )
    record = (
        stream, normed, query_raw, key_raw, queries, before, own, lse, context,
        branch, middle, ffn_normed, gate_up, inner, ffn_branch,
    )
    return record, result


def block_backward_kernel(
    weights, grad_ref, fb_ref, gu_ref, middle_ref, branch_ref, gains_ref, wa_any, wi_any, wo_any,
    gfb_ref, ggu_ref, gb_ref, gctx_ref, gmid_ref, sums_ref,
    wa_ref, wi_ref, wo_ref, sem,
):
    copies = [
        fetch(weight, source, target, sem.at[i])
        for i, (weight, source, target) in enumerate(
            zip(weights, (wa_any, wi_any, wo_any), (wa_ref, wi_ref, wo_ref))
        )
    ]
    grad_out = grad_ref[...]
    grad_ffn_branch, post_ffn = rms_backward(fb_ref[...], gain_of(gains_ref, POST_FFN), grad_out)
    grad_ffn_branch = grad_ffn_branch.astype(BF16)
    gfb_ref[...] = grad_ffn_branch
    copies[2].wait()
    copies[1].wait()
    hidden = gu_ref.shape[1] // 2
    total = jnp.zeros(grad_ref.shape, F32)
    for start in range(0, hidden, HIDDEN_BLOCK):
        gate_cols = slice(start, start + HIDDEN_BLOCK)
        up_cols = slice(hidden + start, hidden + start + HIDDEN_BLOCK)
        grad_inner = dot(grad_ffn_branch, weight_rows(wo_ref, start, HIDDEN_BLOCK), 1, 1)
        gate = gu_ref[:, gate_cols].astype(F32)
        up = gu_ref[:, up_cols].astype(F32)
        tanh, value = gelu_parts(gate)
        slope = 0.5 * (1.0 + tanh) + 0.5 * gate * (1.0 - tanh * tanh) * GELU_A * (
            1.0 + 3.0 * GELU_B * gate * gate
        )
        grad_gate = (grad_inner * up * slope).astype(BF16)
        grad_up = (grad_inner * value).astype(BF16)
        ggu_ref[:, gate_cols] = grad_gate
        ggu_ref[:, up_cols] = grad_up
        total += dot(grad_gate, weight_rows(wi_ref, start, HIDDEN_BLOCK), 1, 0)
        total += dot(grad_up, weight_rows(wi_ref, hidden + start, HIDDEN_BLOCK), 1, 0)
    grad_part, pre_ffn = rms_backward(middle_ref[...], gain_of(gains_ref, PRE_FFN), total)
    grad_middle = grad_out + grad_part
    gmid_ref[...] = grad_middle
    grad_branch, post_attn = rms_backward(branch_ref[...], gain_of(gains_ref, POST_ATTN), grad_middle)
    grad_branch = grad_branch.astype(BF16)
    gb_ref[...] = grad_branch
    sums_ref[0:1, :] = post_attn
    sums_ref[1:2, :] = pre_ffn
    sums_ref[2:3, :] = post_ffn
    copies[0].wait()
    gctx_ref[...] = dot(grad_branch, weight_rows(wa_ref, 0, QUERY_COLS), 1, 1).astype(BF16)


def attention_backward_kernel(
    q_ref, before_ref, own_ref, reach_ref, lse_ref, g_ref, dq_ref, gbefore_ref, gown_ref, acc
):
    acc[...] = jnp.zeros_like(acc)
    for block in range(q_ref.shape[0] // QUERY_BLOCK):
        start = block * QUERY_BLOCK
        queries = stacked_heads(q_ref, start)
        grads = stacked_heads(g_ref, start)
        keys = window_rows(before_ref, own_ref, start, KEY_COUNT, KEYS)
        values = window_rows(before_ref, own_ref, start, KEY_COUNT, VALUES)
        allowed = allowed_pairs(start, KEY_COUNT, reach_ref[block : block + 1, :], HEADS * QUERY_BLOCK)
        scores = jnp.where(allowed, dot(keys, queries, 1, 1), MASKED_SCORE)
        probs = jnp.exp(scores - lse_ref[block : block + 1, :])
        grad_probs = dot(values, grads, 1, 1)
        inner = jnp.sum(probs * grad_probs, axis=0, keepdims=True)
        grad_scores = (probs * (grad_probs - inner)).astype(BF16)
        acc[start : start + KEY_COUNT, VALUES] += dot(probs.astype(BF16), grads, 1, 0)
        acc[start : start + KEY_COUNT, KEYS] += dot(grad_scores, queries, 1, 0)
        grad_queries = dot(grad_scores, keys, 0, 0) * SCORE_SCALE
        for h in range(HEADS):
            dq_ref[start : start + QUERY_BLOCK, h * HEAD_DIM : (h + 1) * HEAD_DIM] = grad_queries[
                h * QUERY_BLOCK : (h + 1) * QUERY_BLOCK
            ]
    gbefore_ref[...] = acc[:WINDOW, :].astype(BF16)
    gown_ref[...] = acc[WINDOW:, :]


def query_backward_kernel(dq_ref, raw_ref, gains_ref, cos_ref, sin_ref, gq_ref, sums_ref):
    cosine_tab, sine_tab = cos_ref[...], sin_ref[...]
    sums = jnp.zeros((1, HEAD_DIM), F32)
    for h in range(HEADS):
        columns = slice(h * HEAD_DIM, (h + 1) * HEAD_DIM)
        grad = rotate_back(dq_ref[:, columns], cosine_tab, sine_tab)
        grad, part = rms_backward(raw_ref[:, columns], gain_of(gains_ref, QUERY_GAIN), grad)
        gq_ref[:, columns] = grad.astype(BF16)
        sums += part
    sums_ref[...] = sums


def input_backward_kernel(
    weights, gq_ref, gown_ref, got_ref, kraw_ref, gmid_ref, stream_ref, gains_ref, cos_ref, sin_ref,
    sums_ref, qsums_ref, w_any, gproj_ref, gin_ref, ggains_ref, w_ref, sem,
):
    copy = fetch(weights[0], w_any, w_ref, sem.at[0])
    total = gown_ref[...] + got_ref[...].astype(F32)
    grad_keys = rotate_back(total[:, KEYS], cos_ref[...], sin_ref[...])
    grad_keys, key_sums = rms_backward(kraw_ref[...], gain_of(gains_ref, KEY_GAIN), grad_keys)
    gproj_ref[:, :QUERY_COLS] = gq_ref[...]
    gproj_ref[:, QUERY_COLS : QUERY_COLS + HEAD_DIM] = grad_keys.astype(BF16)
    gproj_ref[:, QUERY_COLS + HEAD_DIM :] = total[:, VALUES].astype(BF16)
    copy.wait()
    grad_normed = dot(gproj_ref[...], weight_rows(w_ref, 0, QUERY_COLS + 2 * HEAD_DIM), 1, 0)
    grad_part, sums = rms_backward(stream_ref[...], gain_of(gains_ref, PRE_ATTN), grad_normed)
    gin_ref[...] = gmid_ref[...] + grad_part
    found = [sums] + [sums_ref[i : i + 1, :] for i in range(3)] + [qsums_ref[...], key_sums]
    ggains_ref[...] = jnp.concatenate(found, axis=1)


def backward_layer(grad_out, weights, gains, record, tables, reach, count, pump, chains, last):
    attn_in, attn_out, ffn_in, ffn_out = weights
    cosine_tab, sine_tab = tables
    (
        stream, normed, query_raw, key_raw, queries, before, own, lse, context,
        branch, middle, ffn_normed, gate_up, inner, ffn_branch,
    ) = record
    tokens = stream.shape[0]
    hidden = inner.shape[1]
    grad_out = pump(0, grad_out)
    grad_ffn_branch, grad_gate_up, grad_branch, grad_context, grad_middle, sums = call(
        partial(block_backward_kernel, [attn_out, ffn_in, ffn_out]), "block_backward",
        (grad_out, ffn_branch, gate_up, middle, branch, gains), [attn_out, ffn_in, ffn_out],
        [
            ((tokens, D), BF16), ((tokens, 2 * hidden), BF16), ((tokens, D), BF16),
            ((tokens, QUERY_COLS), BF16), ((tokens, D), F32), ((8, D), F32),
        ],
        2 * tokens * D * (QUERY_COLS + 3 * hidden),
    )
    ffn = [(grad_gate_up, ffn_normed), (inner, grad_ffn_branch)]
    if last:
        chains["ffn"] = Chain(ffn, "dp", True)
    else:
        cut = 3 * D // 5
        chains["ffn_a"] = Chain(ffn, "dp", columns=slice(0, cut))
        chains["ffn_b"] = Chain(ffn, "seq", columns=slice(cut, D))
    grad_context = launch(grad_context, list(chains.values()))
    grad_context = pump(1, grad_context)
    grad_queries, grad_before, grad_own = call(
        attention_backward_kernel, "attention_backward",
        (queries, before, own, reach, lse, grad_context), [],
        [((tokens, QUERY_COLS), F32), ((WINDOW, 2 * HEAD_DIM), BF16), ((tokens, 2 * HEAD_DIM), F32)],
        10 * tokens * QUERY_COLS * KEY_COUNT,
        [pltpu.VMEM((WINDOW + tokens, 2 * HEAD_DIM), F32)],
    )
    got = neighbour(grad_before, count, True)
    grad_queries = pump(2, grad_queries)
    grad_query_raw, query_sums = call(
        query_backward_kernel, "query_backward",
        (grad_queries, query_raw, gains, cosine_tab, sine_tab), [],
        [((tokens, QUERY_COLS), BF16), ((1, HEAD_DIM), F32)],
        20 * tokens * QUERY_COLS,
    )
    grad_query_raw = pump(3, grad_query_raw)
    grad_projected, grad_in, gain_grads = call(
        partial(input_backward_kernel, [attn_in]), "input_backward",
        (
            grad_query_raw, grad_own, got, key_raw, grad_middle, stream, gains, cosine_tab, sine_tab,
            sums, query_sums,
        ),
        [attn_in],
        [((tokens, QUERY_COLS + 2 * HEAD_DIM), BF16), ((tokens, D), F32), (gains.shape, F32)],
        2 * tokens * D * (QUERY_COLS + 2 * HEAD_DIM),
    )
    n_dp, n_seq = lax.axis_size("dp"), lax.axis_size("seq")
    gain_grads = gain_grads.astype(BF16).reshape(n_dp, n_seq, 1, -1)
    extra = jnp.pad(gain_grads, ((0, 0), (0, 0), (0, TILE - 1), (0, D - gain_grads.shape[3])))
    attn = [(grad_projected, normed), (context, grad_branch)]
    chains["attn"] = Chain(attn, "dp" if last else "seq", last, extra=extra)
    return launch(grad_in, [chains["attn"]])


PLAN = {
    0: [(1, "attn")],
    1: [(0, "ffn"), (0, "ffn_a"), (0, "ffn_b"), (1, "ffn")],
    2: [],
    3: [(1, "attn")],
    4: [(0, "ffn_a"), (0, "ffn_b")],
}


def gather_weights(w_attn_in, w_attn_out, w_ffn_in, w_ffn_out, gains):
    layers = w_attn_in.shape[0]
    kinds = [w_ffn_in.transpose(0, 2, 1), w_ffn_out, w_attn_in.transpose(0, 2, 1), w_attn_out]
    gain_rows = jnp.pad(gains, ((0, 16 - layers), (0, D - gains.shape[1])))
    packed = jnp.concatenate([kind.reshape(-1, D) for kind in kinds] + [gain_rows], axis=0)
    whole = lax.all_gather(packed, ALL, axis=0, tiled=False)
    out, at = [[] for _ in range(layers)], 0
    for kind in kinds:
        for layer in range(layers):
            out[layer].append((at, kind.shape[1]))
            at += kind.shape[1]
    gain_full = whole[:, at : at + layers, : gains.shape[1]].astype(F32)

    def of(layer):
        found = []
        for start, size in out[layer]:
            if size % TILE:
                found.append((whole[:, start : start + size].reshape(1, -1, D), 0, size * whole.shape[0]))
            else:
                found.append((whole, start, size))
        ffn_in, ffn_out, attn_in, attn_out = found
        return (attn_in, attn_out, ffn_in, ffn_out), gain_full[:, layer].reshape(1, -1)

    return of


def body(hidden_in, positions, out_grad, w_attn_in, w_attn_out, w_ffn_in, w_ffn_out, gains):
    count = hidden_in.shape[0]
    layer_count = w_attn_in.shape[0]
    layer_weights = gather_weights(w_attn_in, w_attn_out, w_ffn_in, w_ffn_out, gains)
    places = to_long(positions)
    stream = to_long(hidden_in).astype(F32)
    tables = angle_tables(places)
    tokens = places.shape[0]
    blocks = tokens // QUERY_BLOCK
    reach = jnp.minimum(places, WINDOW - 1).reshape(blocks, QUERY_BLOCK)
    reach = jnp.tile(reach, (1, HEADS))
    records, weights = [], []
    for layer_index in range(layer_count):
        weights.append(layer_weights(layer_index))
        record, stream = forward_layer(stream, *weights[-1], tables, reach, count)
        records.append(record)
        if layer_index == 0:
            stream, out_grad = lax.optimization_barrier((stream, out_grad))
            grad_stream = to_long(out_grad).astype(F32)
    hidden_out = to_short(stream.astype(BF16), count)
    chains = [{} for _ in range(layer_count + 1)]
    sums = [None] * layer_count
    for layer_index in reversed(range(layer_count)):

        def pump(where, value):
            active = [
                chains[layer_index + above][name]
                for above, name in PLAN[where]
                if name in chains[layer_index + above]
            ]
            value = advance(value, active)
            if where == 3 and layer_index + 1 < layer_count:
                above = chains[layer_index + 1]
                packed = jnp.concatenate([above["ffn"].finish(), above["attn"].finish()], axis=1)
                value, packed = lax.optimization_barrier((value, packed.astype(BF16)))
                sums[layer_index + 1] = lax.psum_scatter(packed, "seq", scatter_dimension=0)
            return value

        grad_stream = backward_layer(
            grad_stream, *weights[layer_index], records[layer_index], tables, reach, count, pump,
            chains[layer_index], layer_index > 0,
        )
    grad_stream = pump(4, grad_stream)
    input_grad = to_short(grad_stream.astype(BF16), count).astype(F32)
    found = chains[0]
    ffn = jnp.concatenate([found["ffn_a"].finish(), found["ffn_b"].finish()], axis=2)
    sums[0] = jnp.concatenate([ffn, found["attn"].finish()], axis=1)[0]
    packed = jnp.stack([entry.astype(F32) for entry in sums])
    sizes = [w_ffn_in.shape[2], w_ffn_out.shape[1], w_attn_in.shape[2], w_attn_out.shape[1]]
    parts, at = [], 0
    for size in sizes:
        parts.append(packed[:, at : at + size])
        at += size
    return (
        hidden_out,
        input_grad,
        parts[2].transpose(0, 2, 1),
        parts[3],
        parts[0].transpose(0, 2, 1),
        parts[1],
        packed[:, at, : gains.shape[1]],
    )


def solution(mesh):
    return jax.shard_map(
        body,
        mesh=mesh,
        in_specs=(
            P("dp", "seq", None),
            P("dp", "seq"),
            P("dp", "seq", None),
            P(None, None, ("dp", "seq")),
            P(None, ("dp", "seq"), None),
            P(None, None, ("dp", "seq")),
            P(None, ("dp", "seq"), None),
            P(None, ("dp", "seq")),
        ),
        out_specs=(
            P("dp", "seq", None),
            P("dp", "seq", None),
            P(None, None, ("dp", "seq")),
            P(None, ("dp", "seq"), None),
            P(None, None, ("dp", "seq")),
            P(None, ("dp", "seq"), None),
            P(None, ("dp", "seq")),
        ),
        check_vma=False,
    )
```

```python
from functools import partial

import jax
import jax.numpy as jnp
from jax import lax
from jax.experimental import pallas as pl
from jax.experimental.pallas import tpu as pltpu
from jax.sharding import PartitionSpec as P

D = 640
HEADS = 4
HEAD_DIM = 256
WINDOW = 512
QUERY_BLOCK = 256

EPSILON = 1e-06
ROPE_BASE = 10000.0
SCORE_SCALE = 0.0625
MASKED_SCORE = -1e30
BF16 = jnp.bfloat16
F32 = jnp.float32
ALL = ("dp", "seq")
TILE = 16
QUERY_COLS = HEADS * HEAD_DIM
GELU_A = 0.7978845608028654
GELU_B = 0.044715
HIDDEN_BLOCK = 512


def dot(a, b, a_dim, b_dim):
    return lax.dot_general(a, b, (((a_dim,), (b_dim,)), ((), ())), preferred_element_type=F32)


def angle_tables(places):
    half_dim = HEAD_DIM // 2
    inverse = ROPE_BASE ** (-(2.0 * jnp.arange(half_dim, dtype=F32)) / HEAD_DIM)
    phases = places.astype(F32)[..., None] * inverse
    return (jnp.cos(phases), jnp.sin(phases))


def inverse_rms(values):
    return lax.rsqrt(jnp.mean(values * values, axis=-1, keepdims=True) + EPSILON)


def rms_norm(values, gain):
    return values * inverse_rms(values) * gain


def rms_backward(values, gain, grad):
    scale = inverse_rms(values)
    weighted = grad * gain
    shared = jnp.mean(weighted * values, axis=-1, keepdims=True) * (scale * scale * scale)
    grad_gain = jnp.sum(grad * (values * scale), axis=0, keepdims=True)
    return weighted * scale - values * shared, grad_gain


def rotate(values, cosine_tab, sine_tab):
    half_dim = HEAD_DIM // 2
    first, second = values[:, :half_dim], values[:, half_dim:]
    return jnp.concatenate(
        [first * cosine_tab - second * sine_tab, second * cosine_tab + first * sine_tab], axis=-1
    )


def rotate_back(values, cosine_tab, sine_tab):
    return rotate(values, cosine_tab, -sine_tab)


def gain_of(gains_ref, which):
    starts = (0, D, 2 * D, 3 * D, 4 * D, 4 * D + HEAD_DIM)
    return gains_ref[:, starts[which] : starts[which] + (D if which < 4 else HEAD_DIM)]


PRE_ATTN, POST_ATTN, PRE_FFN, POST_FFN, QUERY_GAIN, KEY_GAIN = range(6)


def weight_rows(ref, start, size):
    shards, rows, width = ref.shape
    if shards == 1:
        return ref[0, start : start + size, :]
    first, last = start // rows, -(-(start + size) // rows)
    value = ref[first:last].reshape((last - first) * rows, width)
    skip = start - first * rows
    return value[skip : skip + size]


def fetch(weight, ref, scratch, sem):
    _, start, rows = weight
    copy = pltpu.make_async_copy(ref.at[:, pl.ds(start, rows), :], scratch, sem)
    copy.start()
    return copy


def weight_scratch(weight):
    array, _, rows = weight
    return pltpu.VMEM((array.shape[0], rows, D), BF16)


def vmem(count):
    return [pl.BlockSpec(memory_space=pltpu.VMEM)] * count


def call(kernel, name, arrays, weights, outs, flops, limit, scratch=(), handed=False):
    outs = [jax.ShapeDtypeStruct(shape, dtype) for shape, dtype in outs]
    moved = sum(a.size * a.dtype.itemsize for a in list(arrays) + outs)
    return pl.pallas_call(
        kernel,
        out_shape=tuple(outs),
        in_specs=vmem(len(arrays)) + [pl.BlockSpec(memory_space=pltpu.HBM)] * len(weights),
        out_specs=tuple(vmem(len(outs))),
        scratch_shapes=[weight_scratch(w) for w in weights if not handed]
        + ([pltpu.SemaphoreType.DMA((len(weights),))] if weights else [])
        + list(scratch),
        compiler_params=pltpu.CompilerParams(vmem_limit_bytes=limit * 2**20),
        cost_estimate=pl.CostEstimate(flops=flops, bytes_accessed=moved, transcendentals=0),
        name=name,
    )(*arrays, *[w[0] for w in weights])


def chunk_route(count, k):
    n_dp, n_seq = lax.axis_size("dp"), lax.axis_size("seq")
    chips = n_seq // (2 * count)
    pairs = []
    for dp in range(n_dp):
        for i in range(n_seq):
            chunk = i // count
            sequence = (dp % 2) * count + (i + k) % count
            target_dp = dp - dp % 2 + chunk % 2
            pairs.append((dp * n_seq + i, target_dp * n_seq + sequence * chips + chunk // 2))
    return pairs


def place(count):
    chips = lax.axis_size("seq") // (2 * count)
    return (lax.axis_index("seq") // chips) % count


def to_long(block):
    count = block.shape[0]
    me = lax.axis_index("seq")
    received = []
    for k in range(count):
        piece = lax.dynamic_index_in_dim(block, (me + k) % count, 0, keepdims=False)
        received.append(lax.ppermute(piece, ALL, chunk_route(count, k)))
    twice = jnp.stack((received[::-1] * 2)[: 2 * count - 1])
    long = lax.dynamic_slice_in_dim(twice, count - 1 - place(count), count, 0)
    return long.reshape((count * block.shape[1],) + block.shape[2:])


def to_short(long, count):
    me = lax.axis_index("seq")
    parts = long.reshape((count, long.shape[0] // count) + long.shape[1:])
    received = []
    for k in range(count):
        piece = lax.dynamic_index_in_dim(parts, (place(count) - k) % count, 0, keepdims=False)
        route = [(j, i) for i, j in chunk_route(count, k)]
        received.append(lax.ppermute(piece, ALL, route))
    twice = jnp.stack((received * 2)[: 2 * count - 1])
    return lax.dynamic_slice_in_dim(twice, (count - me % count) % count, count, 0)


def neighbour(block, count, back):
    n_dp, n_seq = lax.axis_size("dp"), lax.axis_size("seq")
    chips = n_seq // (2 * count)
    pairs = []
    for dp in range(n_dp):
        for i in range(n_seq):
            if dp % 2 == 0:
                pairs.append((dp * n_seq + i, (dp + 1) * n_seq + i))
            elif (i + 1) % chips:
                pairs.append((dp * n_seq + i, (dp - 1) * n_seq + i + 1))
    if back:
        pairs = [(j, i) for i, j in pairs]
    return lax.ppermute(block, ALL, pairs)


def bits(axis):
    out, bit = [], 1
    while bit < lax.axis_size(axis):
        out.append((axis, bit))
        bit *= 2
    return out


def order(first, scatter):
    core, *wide = bits("dp")
    near, *far = bits("seq")
    if scatter:
        return [core] + wide
    if first == "dp":
        return [core] + wide + [near] + far[::-1]
    return [core, near] + wide + far[::-1]


def swap(array, step):
    axis, bit = step
    return lax.ppermute(array, axis, [(i, i ^ bit) for i in range(lax.axis_size(axis))])


def launch(value, chains):
    chains = [chain for chain in chains if chain.pending is not None]
    if not chains:
        return value
    held = lax.optimization_barrier((value,) + tuple(chain.pending for chain in chains))
    for chain, pending in zip(chains, held[1:]):
        chain.got = swap(pending, chain.steps[0])
        chain.pending = None
    return held[0]


def advance(value, chains):
    chains = [chain for chain in chains if chain.steps]
    if not chains:
        return value
    held = lax.optimization_barrier((value,) + tuple(chain.got for chain in chains))
    for chain, got in zip(chains, held[1:]):
        chain.got = got
        chain.advance()
    return launch(held[0], chains + [part for chain in chains for part in chain.parts])


def block_numbers(scatter):
    me = lax.axis_index("dp")
    core = me % 2
    wide = [me // 2, (me // 2) ^ 1]
    leave = [2 * w + 1 - core for w in wide]
    stay = [2 * w + core for w in wide]
    along = lax.axis_index("seq") * (0 if scatter else 1)
    return jnp.stack(leave + stay + [along]).astype(jnp.int32)


def product_kernel(pairs, extra, added, outs, scatter, n_seq, numbers_ref, *refs):
    lefts, rights, refs = refs[:pairs], refs[pairs : 2 * pairs], refs[2 * pairs :]
    if extra:
        extra_ref, refs = refs[0], refs[1:]
    if added:
        got_ref, refs = refs[0], refs[1:]
    me, step = numbers_ref[4], pl.program_id(0)
    half = n_seq // 2

    def store(shard, base, value):
        entry = me ^ shard
        if not scatter:
            entry = lax.rem(entry, 2) * half + entry // 2
        place = slice(base, base + value.shape[0])
        if added:
            value = value + got_ref[0, entry, place].astype(F32)
        value = value.astype(BF16)
        for (kind, which, columns), ref in zip(outs, refs):
            if kind == "all":
                ref[0, entry, place] = value[:, columns]
                continue
            at = entry - which * half if kind == "half" else entry

            @pl.when((entry // half if kind == "half" else step) == which)
            def _():
                ref[0, at, place] = value[:, columns]

    base = 0
    for left, right in zip(lefts, rights):
        width = left.shape[1]
        rows = width // n_seq
        part = min(width, 512)
        for start in range(0, width, part):
            total = dot(left[:, start : start + part], right[...], 0, 0)
            for at in range(0, part, rows):
                store((start + at) // rows, base, total[at : at + rows])
        base += rows
    if extra:
        for shard in range(n_seq):
            store(shard, base, extra_ref[0, shard].astype(F32))


def product(factors, first, outs, got=None):
    pairs, extra, numbers, scatter = factors
    n_dp, n_seq = lax.axis_size("dp"), lax.axis_size("seq")
    tokens = pairs[0][0].shape[0]
    widths = [left.shape[1] // n_dp for left, _ in pairs]
    rows = sum(widths) // n_seq + (0 if extra is None else extra.shape[2])
    specs = [pl.BlockSpec((tokens, w), lambda i, n: (0, n[first + i])) for w in widths]
    specs += [pl.BlockSpec(right.shape, lambda i, n: (0, 0)) for _, right in pairs]
    operands = [left for left, _ in pairs] + [right for _, right in pairs]
    if extra is not None:
        specs.append(pl.BlockSpec((1,) + extra.shape[1:], lambda i, n: (n[first + i], 0, 0, 0)))
        operands.append(extra)
    if got is not None:
        specs.append(pl.BlockSpec((1, n_seq, rows, D), lambda i, n: (i, 0, 0, 0)))
        operands.append(got)
    shapes, out_specs = [], []
    for kind, _, columns in outs:
        wide = columns.stop - columns.start
        entries = n_seq // 2 if kind == "half" else n_seq
        shapes.append(jax.ShapeDtypeStruct((1 if kind == "block" else 2, entries, rows, wide), BF16))
        index = (lambda i, n: (0, 0, 0, 0)) if kind == "block" else (lambda i, n: (i, 0, 0, 0))
        out_specs.append(pl.BlockSpec((1, entries, rows, wide), index))
    return pl.pallas_call(
        partial(product_kernel, len(pairs), extra is not None, got is not None, outs, scatter, n_seq),
        grid_spec=pltpu.PrefetchScalarGridSpec(
            num_scalar_prefetch=1, grid=(2,), in_specs=specs, out_specs=out_specs
        ),
        out_shape=shapes,
        compiler_params=pltpu.CompilerParams(vmem_limit_bytes=26 * 2**20),
        cost_estimate=pl.CostEstimate(
            flops=4 * tokens * sum(widths) * D,
            bytes_accessed=4 * (tokens + 2 * D) * sum(widths),
            transcendentals=0,
        ),
        name="weight_gradient",
    )(numbers, *operands)


WHOLE, CUT = slice(0, D), 3 * D // 5


class Chain:
    def __init__(self, pairs, scatter=False, extra=None, fork=False):
        self.steps = order("dp", scatter)
        self.fork = fork
        self.parts = []
        n_dp, n_seq = lax.axis_size("dp"), lax.axis_size("seq")
        widths = [left.shape[1] // n_dp for left, _ in pairs]
        self.factors = None
        self.rows = sum(widths) // n_seq + (0 if extra is None else extra.shape[2])
        if n_dp == 4 and all(w % 128 == 0 and w % (n_seq * TILE) == 0 for w in widths):
            self.factors = (pairs, extra, block_numbers(scatter), scatter)
            (self.pending,) = product(self.factors, 0, [("all", 0, WHOLE)])
            return
        devices = n_dp * n_seq
        parts = [
            dot(left, right, 0, 0).astype(BF16).reshape(devices, -1, D) for left, right in pairs
        ]
        if extra is not None:
            parts.append(extra.reshape(devices, -1, D))
        target = jnp.arange(devices)
        source, left_over = jnp.zeros_like(target), devices
        for axis, bit in self.steps:
            left_over //= 2
            source = source + (target // left_over) % 2 * (bit * n_seq if axis == "dp" else bit)
        if scatter:
            source = source + target % n_seq
        me = lax.axis_index("dp") * n_seq
        if not scatter:
            me = me + lax.axis_index("seq")
        self.cut(jnp.take(jnp.concatenate(parts, axis=1), me ^ source, axis=0))

    def part(self, steps, keep, pending):
        chain = object.__new__(Chain)
        chain.steps, chain.factors, chain.fork, chain.parts = steps, None, False, []
        chain.keep, chain.pending = keep, pending
        self.parts.append(chain)

    def cut(self, array):
        half = array.shape[0] // 2
        self.keep, self.pending = array[:half], array[half:]

    def advance(self):
        self.steps = self.steps[1:]
        if self.factors:
            factors, self.factors = self.factors, None
            outs = [("block", 0, WHOLE), ("block", 1, WHOLE)]
            if self.fork:
                a, b = slice(0, CUT), slice(CUT, D)
                outs = [("block", 0, a), ("block", 1, a), ("half", 0, b), ("half", 1, b)]
            found = product(factors, 2, outs, self.got)
            found = [array.reshape((-1, self.rows) + array.shape[3:]) for array in found]
            if self.fork:
                self.pending = None
                self.part(order("dp", False)[1:], *found[:2])
                self.part(order("seq", False)[1:], *found[2:])
                self.steps = []
            else:
                self.keep, self.pending = found
            return
        array = self.keep.astype(F32) + self.got.astype(F32)
        if self.steps:
            self.cut(array.astype(BF16))
        else:
            self.result = array

    def finish(self):
        if self.parts:
            return jnp.concatenate([part.finish() for part in self.parts], axis=2)
        while self.steps:
            if self.pending is not None:
                self.got = swap(self.pending, self.steps[0])
                self.pending = None
            self.advance()
        return self.result


def allowed_pairs(start, key_count, reach, lanes):
    key_at = lax.broadcasted_iota(jnp.int32, (key_count, lanes), 0)
    query_at = lax.broadcasted_iota(jnp.int32, (key_count, lanes), 1) % QUERY_BLOCK
    distance = query_at + WINDOW - key_at
    return (distance >= 0) & (distance <= reach)


def stacked_heads(ref, start):
    return jnp.concatenate(
        [
            ref[start : start + QUERY_BLOCK, h * HEAD_DIM : (h + 1) * HEAD_DIM]
            for h in range(HEADS)
        ],
        axis=0,
    )


def window_rows(before_ref, own_ref, start, count, columns):
    return jnp.concatenate(
        [before_ref[start:, columns], own_ref[: count - (WINDOW - start), columns]], axis=0
    )


KEYS, VALUES = slice(0, HEAD_DIM), slice(HEAD_DIM, 2 * HEAD_DIM)
KEY_COUNT = QUERY_BLOCK + WINDOW


def key_value_kernel(weights, stream_ref, gains_ref, cos_ref, sin_ref, w_any, normed_ref, raw_ref, own_ref, w_ref, sem):
    copy = fetch(weights[0], w_any, w_ref, sem.at[0])
    normed = rms_norm(stream_ref[...], gain_of(gains_ref, PRE_ATTN)).astype(BF16)
    normed_ref[...] = normed
    copy.wait()
    raw = dot(normed, weight_rows(w_ref, QUERY_COLS, 2 * HEAD_DIM), 1, 1)
    raw_ref[...] = raw[:, KEYS]
    keys = rms_norm(raw[:, KEYS], gain_of(gains_ref, KEY_GAIN))
    own_ref[:, KEYS] = rotate(keys, cos_ref[...], sin_ref[...]).astype(BF16)
    own_ref[:, VALUES] = raw[:, VALUES].astype(BF16)


def query_kernel(normed_ref, gains_ref, cos_ref, sin_ref, w_ref, raw_ref, q_ref):
    cosine_tab, sine_tab = cos_ref[...], sin_ref[...]
    normed = normed_ref[...]
    for h in range(HEADS):
        columns = slice(h * HEAD_DIM, (h + 1) * HEAD_DIM)
        raw = dot(normed, weight_rows(w_ref, h * HEAD_DIM, HEAD_DIM), 1, 1)
        raw_ref[:, columns] = raw
        queries = rotate(rms_norm(raw, gain_of(gains_ref, QUERY_GAIN)), cosine_tab, sine_tab)
        q_ref[:, columns] = queries.astype(BF16) * SCORE_SCALE


def gelu_parts(gate):
    inner = GELU_A * (gate + GELU_B * gate * gate * gate)
    tanh = jnp.tanh(inner)
    return tanh, 0.5 * gate * (1.0 + tanh)


def block_kernel(
    weights, q_ref, before_ref, own_ref, reach_ref, stream_ref, gains_ref, wa_any, wi_any, wo_any,
    ctx_ref, lse_ref, branch_ref, middle_ref, fn_ref, gu_ref, inner_ref, fb_ref, result_ref,
    wa_ref, wi_ref, wo_ref, sem,
):
    copies = [
        fetch(weight, source, target, sem.at[i])
        for i, (weight, source, target) in enumerate(
            zip(weights, (wa_any, wi_any, wo_any), (wa_ref, wi_ref, wo_ref))
        )
    ]
    for block in range(q_ref.shape[0] // QUERY_BLOCK):
        start = block * QUERY_BLOCK
        queries = stacked_heads(q_ref, start)
        keys = window_rows(before_ref, own_ref, start, KEY_COUNT, KEYS)
        values = window_rows(before_ref, own_ref, start, KEY_COUNT, VALUES)
        allowed = allowed_pairs(start, KEY_COUNT, reach_ref[block : block + 1, :], HEADS * QUERY_BLOCK)
        scores = jnp.where(allowed, dot(keys, queries, 1, 1), MASKED_SCORE)
        row_max = jnp.max(scores, axis=0, keepdims=True)
        exps = jnp.exp(scores - row_max)
        row_sum = jnp.sum(exps, axis=0, keepdims=True)
        probs = (exps * (1.0 / row_sum)).astype(BF16)
        lse_ref[block : block + 1, :] = row_max + jnp.log(row_sum)
        context = dot(probs, values, 0, 0).astype(BF16)
        for h in range(HEADS):
            ctx_ref[start : start + QUERY_BLOCK, h * HEAD_DIM : (h + 1) * HEAD_DIM] = context[
                h * QUERY_BLOCK : (h + 1) * QUERY_BLOCK
            ]
    copies[0].wait()
    branch = dot(ctx_ref[...], weight_rows(wa_ref, 0, QUERY_COLS), 1, 0)
    branch_ref[...] = branch
    middle = stream_ref[...] + rms_norm(branch, gain_of(gains_ref, POST_ATTN))
    middle_ref[...] = middle
    ffn_normed = rms_norm(middle, gain_of(gains_ref, PRE_FFN)).astype(BF16)
    fn_ref[...] = ffn_normed
    copies[1].wait()
    copies[2].wait()
    hidden = inner_ref.shape[1]
    total = jnp.zeros(branch_ref.shape, F32)
    for start in range(0, hidden, HIDDEN_BLOCK):
        gate_cols = slice(start, start + HIDDEN_BLOCK)
        up_cols = slice(hidden + start, hidden + start + HIDDEN_BLOCK)
        gate = dot(ffn_normed, weight_rows(wi_ref, start, HIDDEN_BLOCK), 1, 1)
        up = dot(ffn_normed, weight_rows(wi_ref, hidden + start, HIDDEN_BLOCK), 1, 1)
        gu_ref[:, gate_cols] = gate.astype(BF16)
        gu_ref[:, up_cols] = up.astype(BF16)
        inner = (gelu_parts(gate)[1] * up).astype(BF16)
        inner_ref[:, gate_cols] = inner
        total += dot(inner, weight_rows(wo_ref, start, HIDDEN_BLOCK), 1, 0)
    fb_ref[...] = total
    result_ref[...] = middle + rms_norm(total, gain_of(gains_ref, POST_FFN))


def forward_layer(stream, weights, gains, tables, reach, count):
    tokens = stream.shape[0]
    cosine_tab, sine_tab = tables
    attn_in, attn_out, ffn_in, ffn_out = weights
    hidden = ffn_out[0].shape[0] * ffn_out[2]
    normed, key_raw, own, fetched = call(
        partial(key_value_kernel, [attn_in]), "key_value",
        (stream, gains, cosine_tab, sine_tab), [attn_in],
        [
            ((tokens, D), BF16), ((tokens, HEAD_DIM), F32), ((tokens, 2 * HEAD_DIM), BF16),
            ((attn_in[0].shape[0], attn_in[2], D), BF16),
        ],
        4 * tokens * D * HEAD_DIM, 12, handed=True,
    )
    before = neighbour(own, count, False)
    query_raw, queries = call(
        query_kernel, "query", (normed, gains, cosine_tab, sine_tab, fetched), [],
        [((tokens, QUERY_COLS), F32), ((tokens, QUERY_COLS), BF16)],
        2 * tokens * D * QUERY_COLS, 12,
    )
    context, lse, branch, middle, ffn_normed, gate_up, inner, ffn_branch, result = call(
        partial(block_kernel, [attn_out, ffn_in, ffn_out]), "block_forward",
        (queries, before, own, reach, stream, gains), [attn_out, ffn_in, ffn_out],
        [
            ((tokens, QUERY_COLS), BF16), (reach.shape, F32), ((tokens, D), F32), ((tokens, D), F32),
            ((tokens, D), BF16), ((tokens, 2 * hidden), BF16), ((tokens, hidden), BF16),
            ((tokens, D), F32), ((tokens, D), F32),
        ],
        2 * tokens * (D * (QUERY_COLS + 3 * hidden) + 2 * QUERY_COLS * KEY_COUNT), 32,
    )
    record = (
        stream, normed, query_raw, key_raw, queries, before, own, lse, context,
        branch, middle, ffn_normed, gate_up, inner, ffn_branch,
    )
    return record, result


def block_backward_kernel(
    weights, grad_ref, fb_ref, gu_ref, middle_ref, branch_ref, gains_ref, wa_any, wi_any, wo_any,
    gfb_ref, ggu_ref, gb_ref, gctx_ref, gmid_ref, sums_ref,
    wa_ref, wi_ref, wo_ref, sem,
):
    copies = [None] * 3
    for i, source, target in ((2, wo_any, wo_ref), (1, wi_any, wi_ref), (0, wa_any, wa_ref)):
        copies[i] = fetch(weights[i], source, target, sem.at[i])
    grad_out = grad_ref[...]
    grad_ffn_branch, post_ffn = rms_backward(fb_ref[...], gain_of(gains_ref, POST_FFN), grad_out)
    grad_ffn_branch = grad_ffn_branch.astype(BF16)
    gfb_ref[...] = grad_ffn_branch
    copies[2].wait()
    hidden = gu_ref.shape[1] // 2
    total = jnp.zeros(grad_ref.shape, F32)
    for start in range(0, hidden, HIDDEN_BLOCK):
        gate_cols = slice(start, start + HIDDEN_BLOCK)
        up_cols = slice(hidden + start, hidden + start + HIDDEN_BLOCK)
        grad_inner = dot(grad_ffn_branch, weight_rows(wo_ref, start, HIDDEN_BLOCK), 1, 1)
        gate = gu_ref[:, gate_cols].astype(F32)
        up = gu_ref[:, up_cols].astype(F32)
        tanh, value = gelu_parts(gate)
        slope = 0.5 * (1.0 + tanh) + 0.5 * gate * (1.0 - tanh * tanh) * GELU_A * (
            1.0 + 3.0 * GELU_B * gate * gate
        )
        grad_gate = (grad_inner * up * slope).astype(BF16)
        grad_up = (grad_inner * value).astype(BF16)
        ggu_ref[:, gate_cols] = grad_gate
        ggu_ref[:, up_cols] = grad_up
        if start == 0:
            copies[1].wait()
        total += dot(grad_gate, weight_rows(wi_ref, start, HIDDEN_BLOCK), 1, 0)
        total += dot(grad_up, weight_rows(wi_ref, hidden + start, HIDDEN_BLOCK), 1, 0)
    grad_part, pre_ffn = rms_backward(middle_ref[...], gain_of(gains_ref, PRE_FFN), total)
    grad_middle = grad_out + grad_part
    gmid_ref[...] = grad_middle
    grad_branch, post_attn = rms_backward(branch_ref[...], gain_of(gains_ref, POST_ATTN), grad_middle)
    grad_branch = grad_branch.astype(BF16)
    gb_ref[...] = grad_branch
    sums_ref[0:1, :] = post_attn
    sums_ref[1:2, :] = pre_ffn
    sums_ref[2:3, :] = post_ffn
    copies[0].wait()
    gctx_ref[...] = dot(grad_branch, weight_rows(wa_ref, 0, QUERY_COLS), 1, 1).astype(BF16)


def attention_backward_kernel(
    q_ref, before_ref, own_ref, reach_ref, lse_ref, g_ref, dq_ref, gbefore_ref, gown_ref, acc
):
    acc[...] = jnp.zeros_like(acc)
    for block in range(q_ref.shape[0] // QUERY_BLOCK):
        start = block * QUERY_BLOCK
        queries = stacked_heads(q_ref, start)
        grads = stacked_heads(g_ref, start)
        keys = window_rows(before_ref, own_ref, start, KEY_COUNT, KEYS)
        values = window_rows(before_ref, own_ref, start, KEY_COUNT, VALUES)
        allowed = allowed_pairs(start, KEY_COUNT, reach_ref[block : block + 1, :], HEADS * QUERY_BLOCK)
        scores = jnp.where(allowed, dot(keys, queries, 1, 1), MASKED_SCORE)
        probs = jnp.exp(scores - lse_ref[block : block + 1, :])
        grad_probs = dot(values, grads, 1, 1)
        inner = jnp.sum(probs * grad_probs, axis=0, keepdims=True)
        grad_scores = (probs * (grad_probs - inner)).astype(BF16)
        acc[start : start + KEY_COUNT, VALUES] += dot(probs.astype(BF16), grads, 1, 0)
        acc[start : start + KEY_COUNT, KEYS] += dot(grad_scores, queries, 1, 0)
        grad_queries = dot(grad_scores, keys, 0, 0) * SCORE_SCALE
        for h in range(HEADS):
            dq_ref[start : start + QUERY_BLOCK, h * HEAD_DIM : (h + 1) * HEAD_DIM] = grad_queries[
                h * QUERY_BLOCK : (h + 1) * QUERY_BLOCK
            ]
    gbefore_ref[...] = acc[:WINDOW, :].astype(BF16)
    gown_ref[...] = acc[WINDOW:, :]


def query_backward_kernel(dq_ref, raw_ref, gains_ref, cos_ref, sin_ref, gq_ref, sums_ref):
    cosine_tab, sine_tab = cos_ref[...], sin_ref[...]
    sums = jnp.zeros((1, HEAD_DIM), F32)
    for h in range(HEADS):
        columns = slice(h * HEAD_DIM, (h + 1) * HEAD_DIM)
        grad = rotate_back(dq_ref[:, columns], cosine_tab, sine_tab)
        grad, part = rms_backward(raw_ref[:, columns], gain_of(gains_ref, QUERY_GAIN), grad)
        gq_ref[:, columns] = grad.astype(BF16)
        sums += part
    sums_ref[...] = sums


def input_backward_kernel(
    weights, gq_ref, gown_ref, got_ref, kraw_ref, gmid_ref, stream_ref, gains_ref, cos_ref, sin_ref,
    sums_ref, qsums_ref, w_any, gproj_ref, gin_ref, ggains_ref, w_ref, sem,
):
    copy = fetch(weights[0], w_any, w_ref, sem.at[0])
    total = gown_ref[...] + got_ref[...].astype(F32)
    grad_keys = rotate_back(total[:, KEYS], cos_ref[...], sin_ref[...])
    grad_keys, key_sums = rms_backward(kraw_ref[...], gain_of(gains_ref, KEY_GAIN), grad_keys)
    gproj_ref[:, :QUERY_COLS] = gq_ref[...]
    gproj_ref[:, QUERY_COLS : QUERY_COLS + HEAD_DIM] = grad_keys.astype(BF16)
    gproj_ref[:, QUERY_COLS + HEAD_DIM :] = total[:, VALUES].astype(BF16)
    copy.wait()
    grad_normed = dot(gproj_ref[...], weight_rows(w_ref, 0, QUERY_COLS + 2 * HEAD_DIM), 1, 0)
    grad_part, sums = rms_backward(stream_ref[...], gain_of(gains_ref, PRE_ATTN), grad_normed)
    gin_ref[...] = gmid_ref[...] + grad_part
    found = [sums] + [sums_ref[i : i + 1, :] for i in range(3)] + [qsums_ref[...], key_sums]
    ggains_ref[...] = jnp.concatenate(found, axis=1)


def backward_layer(grad_out, weights, gains, record, tables, reach, count, pump, chains, last):
    attn_in, attn_out, ffn_in, ffn_out = weights
    cosine_tab, sine_tab = tables
    (
        stream, normed, query_raw, key_raw, queries, before, own, lse, context,
        branch, middle, ffn_normed, gate_up, inner, ffn_branch,
    ) = record
    tokens = stream.shape[0]
    hidden = inner.shape[1]
    grad_out = pump(0, grad_out)
    grad_ffn_branch, grad_gate_up, grad_branch, grad_context, grad_middle, sums = call(
        partial(block_backward_kernel, [attn_out, ffn_in, ffn_out]), "block_backward",
        (grad_out, ffn_branch, gate_up, middle, branch, gains), [attn_out, ffn_in, ffn_out],
        [
            ((tokens, D), BF16), ((tokens, 2 * hidden), BF16), ((tokens, D), BF16),
            ((tokens, QUERY_COLS), BF16), ((tokens, D), F32), ((8, D), F32),
        ],
        2 * tokens * D * (QUERY_COLS + 3 * hidden), 26,
    )
    grad_context = pump(1, grad_context)
    ffn = [(grad_gate_up, ffn_normed), (inner, grad_ffn_branch)]
    chains["ffn"] = Chain(ffn, last, fork=not last)
    grad_context = launch(grad_context, list(chains.values()))
    grad_queries, grad_before, grad_own = call(
        attention_backward_kernel, "attention_backward",
        (queries, before, own, reach, lse, grad_context), [],
        [((tokens, QUERY_COLS), F32), ((WINDOW, 2 * HEAD_DIM), BF16), ((tokens, 2 * HEAD_DIM), F32)],
        10 * tokens * QUERY_COLS * KEY_COUNT, 26,
        [pltpu.VMEM((WINDOW + tokens, 2 * HEAD_DIM), F32)],
    )
    got = neighbour(grad_before, count, True)
    grad_queries = pump(2, grad_queries)
    grad_query_raw, query_sums = call(
        query_backward_kernel, "query_backward",
        (grad_queries, query_raw, gains, cosine_tab, sine_tab), [],
        [((tokens, QUERY_COLS), BF16), ((1, HEAD_DIM), F32)],
        20 * tokens * QUERY_COLS, 12,
    )
    grad_query_raw = pump(3, grad_query_raw)
    grad_projected, grad_in, gain_grads = call(
        partial(input_backward_kernel, [attn_in]), "input_backward",
        (
            grad_query_raw, grad_own, got, key_raw, grad_middle, stream, gains, cosine_tab, sine_tab,
            sums, query_sums,
        ),
        [attn_in],
        [((tokens, QUERY_COLS + 2 * HEAD_DIM), BF16), ((tokens, D), F32), (gains.shape, F32)],
        2 * tokens * D * (QUERY_COLS + 2 * HEAD_DIM), 14,
    )
    n_dp, n_seq = lax.axis_size("dp"), lax.axis_size("seq")
    gain_grads = gain_grads.astype(BF16).reshape(n_dp, n_seq, 1, -1)
    extra = jnp.pad(gain_grads, ((0, 0), (0, 0), (0, TILE - 1), (0, D - gain_grads.shape[3])))
    attn = [(grad_projected, normed), (context, grad_branch)]
    chains["attn"] = Chain(attn, last, extra)
    return launch(grad_in, [chains["attn"]])


PLAN = {
    0: [(1, "attn")],
    1: [(1, "ffn")],
    2: [(0, "ffn"), (1, "attn")],
    3: [],
}


def pack_weights(w_attn_in, w_attn_out, w_ffn_in, w_ffn_out, gains):
    gain_rows = jnp.pad(gains[None, :], ((0, TILE - 1), (0, D - gains.shape[0])))
    return jnp.concatenate([w_ffn_in.T, w_ffn_out, w_attn_in.T, w_attn_out, gain_rows], axis=0)


def gather_weights(packed, sizes, gain_count):
    whole = lax.all_gather(packed, ALL, axis=0, tiled=False)
    found, at = [], 0
    for size in sizes:
        if size % TILE:
            found.append((whole[:, at : at + size].reshape(1, -1, D), 0, size * whole.shape[0]))
        else:
            found.append((whole, at, size))
        at += size
    ffn_in, ffn_out, attn_in, attn_out = found
    gain_full = whole[:, at, :gain_count].astype(F32).reshape(1, -1)
    return (attn_in, attn_out, ffn_in, ffn_out), gain_full


def body(hidden_in, positions, out_grad, w_attn_in, w_attn_out, w_ffn_in, w_ffn_out, gains):
    count = hidden_in.shape[0]
    layer_count = w_attn_in.shape[0]
    sizes = [w_ffn_in.shape[2], w_ffn_out.shape[1], w_attn_in.shape[2], w_attn_out.shape[1]]
    packed = [
        pack_weights(w_attn_in[l], w_attn_out[l], w_ffn_in[l], w_ffn_out[l], gains[l])
        for l in range(layer_count)
    ]
    weights = [gather_weights(packed[0], sizes, gains.shape[1])]
    places = to_long(positions)
    stream = to_long(hidden_in).astype(F32)
    tables = angle_tables(places)
    tokens = places.shape[0]
    blocks = tokens // QUERY_BLOCK
    reach = jnp.minimum(places, WINDOW - 1).reshape(blocks, QUERY_BLOCK)
    reach = jnp.tile(reach, (1, HEADS))
    records = []
    stream, later = lax.optimization_barrier((stream, packed[1:]))
    weights += [gather_weights(entry, sizes, gains.shape[1]) for entry in later]
    for layer_index in range(layer_count):
        record, stream = forward_layer(stream, *weights[layer_index], tables, reach, count)
        records.append(record)
        if layer_index == 0:
            stream, out_grad = lax.optimization_barrier((stream, out_grad))
            grad_stream = to_long(out_grad).astype(F32)
    hidden_out = to_short(stream.astype(BF16), count)
    outputs = {"hidden": hidden_out}
    chains = [{} for _ in range(layer_count + 1)]
    sums = [None] * layer_count
    for layer_index in reversed(range(layer_count)):

        def pump(where, value):
            active = [
                chains[layer_index + above][name]
                for above, name in PLAN[where]
                if name in chains[layer_index + above]
            ]
            value = advance(value, active)
            if where == 1 and layer_index + 1 == layer_count:
                value, outputs["hidden"] = lax.optimization_barrier((value, outputs["hidden"]))
            if where == 2 and layer_index + 1 < layer_count:
                above = chains[layer_index + 1]
                packed = jnp.concatenate([above["ffn"].finish(), above["attn"].finish()], axis=1)
                value, packed = lax.optimization_barrier((value, packed.astype(BF16)))
                sums[layer_index + 1] = lax.psum_scatter(packed, "seq", scatter_dimension=0)
            return value

        grad_stream = backward_layer(
            grad_stream, *weights[layer_index], records[layer_index], tables, reach, count, pump,
            chains[layer_index], layer_index > 0,
        )
    attn, ffn = [chains[0]["attn"]], chains[0]["ffn"].parts or [chains[0]["ffn"]]
    grad_stream = advance(grad_stream, ffn)
    grad_stream = advance(grad_stream, attn)
    grad_stream = advance(grad_stream, ffn)
    short = to_short(grad_stream.astype(BF16), count)
    mark = advance(grad_stream[:8], attn)
    mark = advance(mark, ffn)
    mark = advance(mark, attn)
    mark = advance(mark, ffn)
    mark, short = lax.optimization_barrier((mark, short))
    mark = advance(mark, attn)
    sums[0] = jnp.concatenate([chains[0]["ffn"].finish(), chains[0]["attn"].finish()], axis=1)[0]
    packed = jnp.stack([entry.astype(F32) for entry in sums])
    parts, at = [], 0
    for size in sizes:
        parts.append(packed[:, at : at + size])
        at += size
    return (
        outputs["hidden"],
        short.astype(F32),
        parts[2].transpose(0, 2, 1),
        parts[3],
        parts[0].transpose(0, 2, 1),
        parts[1],
        packed[:, at, : gains.shape[1]],
    )


def solution(mesh):
    return jax.shard_map(
        body,
        mesh=mesh,
        in_specs=(
            P("dp", "seq", None),
            P("dp", "seq"),
            P("dp", "seq", None),
            P(None, None, ("dp", "seq")),
            P(None, ("dp", "seq"), None),
            P(None, None, ("dp", "seq")),
            P(None, ("dp", "seq"), None),
            P(None, ("dp", "seq")),
        ),
        out_specs=(
            P("dp", "seq", None),
            P("dp", "seq", None),
            P(None, None, ("dp", "seq")),
            P(None, ("dp", "seq"), None),
            P(None, None, ("dp", "seq")),
            P(None, ("dp", "seq"), None),
            P(None, ("dp", "seq")),
        ),
        check_vma=False,
    )
```

```python
from functools import partial

import jax
import jax.numpy as jnp
from jax import lax
from jax.experimental import pallas as pl
from jax.experimental.pallas import tpu as pltpu
from jax.sharding import PartitionSpec as P

D = 640
HEADS = 4
HEAD_DIM = 256
WINDOW = 512
QUERY_BLOCK = 256

EPSILON = 1e-06
ROPE_BASE = 10000.0
SCORE_SCALE = 0.0625
MASKED_SCORE = -1e30
BF16 = jnp.bfloat16
VMEM_LIMIT = 44 * 2**20
VMEM_LIMIT_PRODUCT = 44 * 2**20
F32 = jnp.float32
ALL = ("dp", "seq")
TILE = 16
QUERY_COLS = HEADS * HEAD_DIM
GELU_A = 0.7978845608028654
GELU_B = 0.044715
HIDDEN_BLOCK = 512


def dot(a, b, a_dim, b_dim):
    return lax.dot_general(a, b, (((a_dim,), (b_dim,)), ((), ())), preferred_element_type=F32)


def angle_tables(places):
    half_dim = HEAD_DIM // 2
    inverse = ROPE_BASE ** (-(2.0 * jnp.arange(half_dim, dtype=F32)) / HEAD_DIM)
    phases = places.astype(F32)[..., None] * inverse
    return (jnp.cos(phases), jnp.sin(phases))


def inverse_rms(values):
    return lax.rsqrt(jnp.mean(values * values, axis=-1, keepdims=True) + EPSILON)


def rms_norm(values, gain):
    return values * inverse_rms(values) * gain


def rms_backward(values, gain, grad):
    scale = inverse_rms(values)
    weighted = grad * gain
    shared = jnp.mean(weighted * values, axis=-1, keepdims=True) * (scale * scale * scale)
    grad_gain = jnp.sum(grad * (values * scale), axis=0, keepdims=True)
    return weighted * scale - values * shared, grad_gain


def rotate(values, cosine_tab, sine_tab):
    half_dim = HEAD_DIM // 2
    first, second = values[:, :half_dim], values[:, half_dim:]
    return jnp.concatenate(
        [first * cosine_tab - second * sine_tab, second * cosine_tab + first * sine_tab], axis=-1
    )


def rotate_back(values, cosine_tab, sine_tab):
    return rotate(values, cosine_tab, -sine_tab)


def gain_of(gains_ref, which):
    starts = (0, D, 2 * D, 3 * D, 4 * D, 4 * D + HEAD_DIM)
    return gains_ref[:, starts[which] : starts[which] + (D if which < 4 else HEAD_DIM)]


PRE_ATTN, POST_ATTN, PRE_FFN, POST_FFN, QUERY_GAIN, KEY_GAIN = range(6)


def weight_rows(ref, start, size):
    shards, rows, width = ref.shape
    if shards == 1:
        return ref[0, start : start + size, :]
    first, last = start // rows, -(-(start + size) // rows)
    value = ref[first:last].reshape((last - first) * rows, width)
    skip = start - first * rows
    return value[skip : skip + size]


def fetch(weight, ref, scratch, sem):
    _, start, rows = weight
    copy = pltpu.make_async_copy(ref.at[:, pl.ds(start, rows), :], scratch, sem)
    copy.start()
    return copy


def weight_scratch(weight):
    array, _, rows = weight
    return pltpu.VMEM((array.shape[0], rows, D), BF16)


def vmem(count):
    return [pl.BlockSpec(memory_space=pltpu.VMEM)] * count


def call(kernel, name, arrays, weights, outs, flops, limit, scratch=(), handed=False):
    outs = [jax.ShapeDtypeStruct(shape, dtype) for shape, dtype in outs]
    moved = sum(a.size * a.dtype.itemsize for a in list(arrays) + outs)
    return pl.pallas_call(
        kernel,
        out_shape=tuple(outs),
        in_specs=vmem(len(arrays)) + [pl.BlockSpec(memory_space=pltpu.HBM)] * len(weights),
        out_specs=tuple(vmem(len(outs))),
        scratch_shapes=[weight_scratch(w) for w in weights if not handed]
        + ([pltpu.SemaphoreType.DMA((len(weights),))] if weights else [])
        + list(scratch),
        compiler_params=pltpu.CompilerParams(vmem_limit_bytes=VMEM_LIMIT),
        cost_estimate=pl.CostEstimate(flops=flops // 64, bytes_accessed=moved // 64, transcendentals=0),
        name=name,
    )(*arrays, *[w[0] for w in weights])


def chunk_route(count, k):
    n_dp, n_seq = lax.axis_size("dp"), lax.axis_size("seq")
    chips = n_seq // (2 * count)
    pairs = []
    for dp in range(n_dp):
        for i in range(n_seq):
            chunk = i // count
            sequence = (dp % 2) * count + (i + k) % count
            target_dp = dp - dp % 2 + chunk % 2
            pairs.append((dp * n_seq + i, target_dp * n_seq + sequence * chips + chunk // 2))
    return pairs


def place(count):
    chips = lax.axis_size("seq") // (2 * count)
    return (lax.axis_index("seq") // chips) % count


def to_long(block):
    count = block.shape[0]
    me = lax.axis_index("seq")
    received = []
    for k in range(count):
        piece = lax.dynamic_index_in_dim(block, (me + k) % count, 0, keepdims=False)
        received.append(lax.ppermute(piece, ALL, chunk_route(count, k)))
    twice = jnp.stack((received[::-1] * 2)[: 2 * count - 1])
    long = lax.dynamic_slice_in_dim(twice, count - 1 - place(count), count, 0)
    return long.reshape((count * block.shape[1],) + block.shape[2:])


def to_short(long, count):
    me = lax.axis_index("seq")
    parts = long.reshape((count, long.shape[0] // count) + long.shape[1:])
    received = []
    for k in range(count):
        piece = lax.dynamic_index_in_dim(parts, (place(count) - k) % count, 0, keepdims=False)
        route = [(j, i) for i, j in chunk_route(count, k)]
        received.append(lax.ppermute(piece, ALL, route))
    twice = jnp.stack((received * 2)[: 2 * count - 1])
    return lax.dynamic_slice_in_dim(twice, (count - me % count) % count, count, 0)


def neighbour(block, count, back):
    n_dp, n_seq = lax.axis_size("dp"), lax.axis_size("seq")
    chips = n_seq // (2 * count)
    pairs = []
    for dp in range(n_dp):
        for i in range(n_seq):
            if dp % 2 == 0:
                pairs.append((dp * n_seq + i, (dp + 1) * n_seq + i))
            elif (i + 1) % chips:
                pairs.append((dp * n_seq + i, (dp - 1) * n_seq + i + 1))
    if back:
        pairs = [(j, i) for i, j in pairs]
    return lax.ppermute(block, ALL, pairs)


def bits(axis):
    out, bit = [], 1
    while bit < lax.axis_size(axis):
        out.append((axis, bit))
        bit *= 2
    return out


def order(first, scatter):
    core, *wide = bits("dp")
    near, *far = bits("seq")
    if scatter:
        return [core] + wide
    if first == "dp":
        return [core] + wide + [near] + far[::-1]
    return [core, near] + wide + far[::-1]


def swap(array, step):
    axis, bit = step
    return lax.ppermute(array, axis, [(i, i ^ bit) for i in range(lax.axis_size(axis))])


def launch(value, chains):
    chains = [chain for chain in chains if chain.pending is not None]
    if not chains:
        return value
    held = lax.optimization_barrier((value,) + tuple(chain.pending for chain in chains))
    for chain, pending in zip(chains, held[1:]):
        chain.got = swap(pending, chain.steps[0])
        chain.pending = None
    return held[0]


def advance(value, chains):
    chains = [chain for chain in chains if chain.steps]
    if not chains:
        return value
    held = lax.optimization_barrier((value,) + tuple(chain.got for chain in chains))
    for chain, got in zip(chains, held[1:]):
        chain.got = got
        chain.advance()
    return launch(held[0], chains + [part for chain in chains for part in chain.parts])


def block_numbers(scatter):
    me = lax.axis_index("dp")
    core = me % 2
    wide = [me // 2, (me // 2) ^ 1]
    leave = [2 * w + 1 - core for w in wide]
    stay = [2 * w + core for w in wide]
    along = lax.axis_index("seq") * (0 if scatter else 1)
    return jnp.stack(leave + stay + [along]).astype(jnp.int32)


def product_kernel(pairs, extra, added, outs, scatter, n_seq, numbers_ref, *refs):
    lefts, rights, refs = refs[:pairs], refs[pairs : 2 * pairs], refs[2 * pairs :]
    if extra:
        extra_ref, refs = refs[0], refs[1:]
    if added:
        got_ref, refs = refs[0], refs[1:]
    me, step = numbers_ref[4], pl.program_id(0)
    half = n_seq // 2

    def store(shard, base, value):
        entry = me ^ shard
        if not scatter:
            entry = lax.rem(entry, 2) * half + entry // 2
        place = slice(base, base + value.shape[0])
        if added:
            value = value + got_ref[0, entry, place].astype(F32)
        value = value.astype(BF16)
        for (kind, which, columns), ref in zip(outs, refs):
            if kind == "all":
                ref[0, entry, place] = value[:, columns]
                continue
            at = entry - which * half if kind == "half" else entry

            @pl.when((entry // half if kind == "half" else step) == which)
            def _():
                ref[0, at, place] = value[:, columns]

    base = 0
    for left, right in zip(lefts, rights):
        width = left.shape[1]
        rows = width // n_seq
        part = min(width, 512)
        for start in range(0, width, part):
            total = dot(left[:, start : start + part], right[...], 0, 0)
            for at in range(0, part, rows):
                store((start + at) // rows, base, total[at : at + rows])
        base += rows
    if extra:
        for shard in range(n_seq):
            store(shard, base, extra_ref[0, shard].astype(F32))


def product(factors, first, outs, got=None):
    pairs, extra, numbers, scatter = factors
    n_dp, n_seq = lax.axis_size("dp"), lax.axis_size("seq")
    tokens = pairs[0][0].shape[0]
    widths = [left.shape[1] // n_dp for left, _ in pairs]
    rows = sum(widths) // n_seq + (0 if extra is None else extra.shape[2])
    specs = [pl.BlockSpec((tokens, w), lambda i, n: (0, n[first + i])) for w in widths]
    specs += [pl.BlockSpec(right.shape, lambda i, n: (0, 0)) for _, right in pairs]
    operands = [left for left, _ in pairs] + [right for _, right in pairs]
    if extra is not None:
        specs.append(pl.BlockSpec((1,) + extra.shape[1:], lambda i, n: (n[first + i], 0, 0, 0)))
        operands.append(extra)
    if got is not None:
        specs.append(pl.BlockSpec((1, n_seq, rows, D), lambda i, n: (i, 0, 0, 0)))
        operands.append(got)
    shapes, out_specs = [], []
    for kind, _, columns in outs:
        wide = columns.stop - columns.start
        entries = n_seq // 2 if kind == "half" else n_seq
        shapes.append(jax.ShapeDtypeStruct((1 if kind == "block" else 2, entries, rows, wide), BF16))
        index = (lambda i, n: (0, 0, 0, 0)) if kind == "block" else (lambda i, n: (i, 0, 0, 0))
        out_specs.append(pl.BlockSpec((1, entries, rows, wide), index))
    return pl.pallas_call(
        partial(product_kernel, len(pairs), extra is not None, got is not None, outs, scatter, n_seq),
        grid_spec=pltpu.PrefetchScalarGridSpec(
            num_scalar_prefetch=1, grid=(2,), in_specs=specs, out_specs=out_specs
        ),
        out_shape=shapes,
        compiler_params=pltpu.CompilerParams(vmem_limit_bytes=VMEM_LIMIT_PRODUCT),
        cost_estimate=pl.CostEstimate(
            flops=tokens * sum(widths) * D // 16,
            bytes_accessed=(tokens + 2 * D) * sum(widths) // 16,
            transcendentals=0,
        ),
        name="weight_gradient",
    )(numbers, *operands)


WHOLE, CUT = slice(0, D), 3 * D // 5


class Chain:
    def __init__(self, pairs, scatter=False, extra=None, fork=False):
        self.steps = order("dp", scatter)
        self.fork = fork
        self.parts = []
        n_dp, n_seq = lax.axis_size("dp"), lax.axis_size("seq")
        widths = [left.shape[1] // n_dp for left, _ in pairs]
        self.factors = None
        self.rows = sum(widths) // n_seq + (0 if extra is None else extra.shape[2])
        if n_dp == 4 and all(w % 128 == 0 and w % (n_seq * TILE) == 0 for w in widths):
            self.factors = (pairs, extra, block_numbers(scatter), scatter)
            (self.pending,) = product(self.factors, 0, [("all", 0, WHOLE)])
            return
        devices = n_dp * n_seq
        parts = [
            dot(left, right, 0, 0).astype(BF16).reshape(devices, -1, D) for left, right in pairs
        ]
        if extra is not None:
            parts.append(extra.reshape(devices, -1, D))
        target = jnp.arange(devices)
        source, left_over = jnp.zeros_like(target), devices
        for axis, bit in self.steps:
            left_over //= 2
            source = source + (target // left_over) % 2 * (bit * n_seq if axis == "dp" else bit)
        if scatter:
            source = source + target % n_seq
        me = lax.axis_index("dp") * n_seq
        if not scatter:
            me = me + lax.axis_index("seq")
        self.cut(jnp.take(jnp.concatenate(parts, axis=1), me ^ source, axis=0))

    def part(self, steps, keep, pending):
        chain = object.__new__(Chain)
        chain.steps, chain.factors, chain.fork, chain.parts = steps, None, False, []
        chain.keep, chain.pending = keep, pending
        self.parts.append(chain)

    def cut(self, array):
        half = array.shape[0] // 2
        self.keep, self.pending = array[:half], array[half:]

    def advance(self):
        self.steps = self.steps[1:]
        if self.factors:
            factors, self.factors = self.factors, None
            outs = [("block", 0, WHOLE), ("block", 1, WHOLE)]
            if self.fork:
                a, b = slice(0, CUT), slice(CUT, D)
                outs = [("block", 0, a), ("block", 1, a), ("half", 0, b), ("half", 1, b)]
            found = product(factors, 2, outs, self.got)
            found = [array.reshape((-1, self.rows) + array.shape[3:]) for array in found]
            if self.fork:
                self.pending = None
                self.part(order("dp", False)[1:], *found[:2])
                self.part(order("seq", False)[1:], *found[2:])
                self.steps = []
            else:
                self.keep, self.pending = found
            return
        array = self.keep.astype(F32) + self.got.astype(F32)
        if self.steps:
            self.cut(array.astype(BF16))
        else:
            self.result = array

    def finish(self):
        if self.parts:
            return jnp.concatenate([part.finish() for part in self.parts], axis=2)
        while self.steps:
            if self.pending is not None:
                self.got = swap(self.pending, self.steps[0])
                self.pending = None
            self.advance()
        return self.result


def allowed_pairs(start, key_count, reach, lanes):
    key_at = lax.broadcasted_iota(jnp.int32, (key_count, lanes), 0)
    query_at = lax.broadcasted_iota(jnp.int32, (key_count, lanes), 1) % QUERY_BLOCK
    distance = query_at + WINDOW - key_at
    return (distance >= 0) & (distance <= reach)


def stacked_heads(ref, start):
    return jnp.concatenate(
        [
            ref[start : start + QUERY_BLOCK, h * HEAD_DIM : (h + 1) * HEAD_DIM]
            for h in range(HEADS)
        ],
        axis=0,
    )


def window_rows(before_ref, own_ref, start, count, columns):
    return jnp.concatenate(
        [before_ref[start:, columns], own_ref[: count - (WINDOW - start), columns]], axis=0
    )


KEYS, VALUES = slice(0, HEAD_DIM), slice(HEAD_DIM, 2 * HEAD_DIM)
KEY_COUNT = QUERY_BLOCK + WINDOW


def key_value_kernel(weights, stream_ref, gains_ref, cos_ref, sin_ref, w_any, normed_ref, raw_ref, own_ref, w_ref, sem):
    copy = fetch(weights[0], w_any, w_ref, sem.at[0])
    normed = rms_norm(stream_ref[...], gain_of(gains_ref, PRE_ATTN)).astype(BF16)
    normed_ref[...] = normed
    copy.wait()
    raw = dot(normed, weight_rows(w_ref, QUERY_COLS, 2 * HEAD_DIM), 1, 1)
    raw_ref[...] = raw[:, KEYS]
    keys = rms_norm(raw[:, KEYS], gain_of(gains_ref, KEY_GAIN))
    own_ref[:, KEYS] = rotate(keys, cos_ref[...], sin_ref[...]).astype(BF16)
    own_ref[:, VALUES] = raw[:, VALUES].astype(BF16)


def query_kernel(normed_ref, gains_ref, cos_ref, sin_ref, w_ref, raw_ref, q_ref):
    cosine_tab, sine_tab = cos_ref[...], sin_ref[...]
    normed = normed_ref[...]
    for h in range(HEADS):
        columns = slice(h * HEAD_DIM, (h + 1) * HEAD_DIM)
        raw = dot(normed, weight_rows(w_ref, h * HEAD_DIM, HEAD_DIM), 1, 1)
        raw_ref[:, columns] = raw
        queries = rotate(rms_norm(raw, gain_of(gains_ref, QUERY_GAIN)), cosine_tab, sine_tab)
        q_ref[:, columns] = queries.astype(BF16) * SCORE_SCALE


def gelu_parts(gate):
    inner = GELU_A * (gate + GELU_B * gate * gate * gate)
    tanh = jnp.tanh(inner)
    return tanh, 0.5 * gate * (1.0 + tanh)


def block_kernel(
    weights, q_ref, before_ref, own_ref, reach_ref, stream_ref, gains_ref, wa_any, wi_any, wo_any,
    ctx_ref, lse_ref, branch_ref, middle_ref, fn_ref, gu_ref, inner_ref, fb_ref, result_ref,
    wa_ref, wi_ref, wo_ref, sem,
):
    copies = [
        fetch(weight, source, target, sem.at[i])
        for i, (weight, source, target) in enumerate(
            zip(weights, (wa_any, wi_any, wo_any), (wa_ref, wi_ref, wo_ref))
        )
    ]
    for block in range(q_ref.shape[0] // QUERY_BLOCK):
        start = block * QUERY_BLOCK
        queries = stacked_heads(q_ref, start)
        keys = window_rows(before_ref, own_ref, start, KEY_COUNT, KEYS)
        values = window_rows(before_ref, own_ref, start, KEY_COUNT, VALUES)
        allowed = allowed_pairs(start, KEY_COUNT, reach_ref[block : block + 1, :], HEADS * QUERY_BLOCK)
        scores = jnp.where(allowed, dot(keys, queries, 1, 1), MASKED_SCORE)
        row_max = jnp.max(scores, axis=0, keepdims=True)
        exps = jnp.exp(scores - row_max)
        row_sum = jnp.sum(exps, axis=0, keepdims=True)
        probs = (exps * (1.0 / row_sum)).astype(BF16)
        lse_ref[block : block + 1, :] = row_max + jnp.log(row_sum)
        context = dot(probs, values, 0, 0).astype(BF16)
        for h in range(HEADS):
            ctx_ref[start : start + QUERY_BLOCK, h * HEAD_DIM : (h + 1) * HEAD_DIM] = context[
                h * QUERY_BLOCK : (h + 1) * QUERY_BLOCK
            ]
    copies[0].wait()
    branch = dot(ctx_ref[...], weight_rows(wa_ref, 0, QUERY_COLS), 1, 0)
    branch_ref[...] = branch
    middle = stream_ref[...] + rms_norm(branch, gain_of(gains_ref, POST_ATTN))
    middle_ref[...] = middle
    ffn_normed = rms_norm(middle, gain_of(gains_ref, PRE_FFN)).astype(BF16)
    fn_ref[...] = ffn_normed
    copies[1].wait()
    copies[2].wait()
    hidden = inner_ref.shape[1]
    total = jnp.zeros(branch_ref.shape, F32)
    for start in range(0, hidden, HIDDEN_BLOCK):
        gate_cols = slice(start, start + HIDDEN_BLOCK)
        up_cols = slice(hidden + start, hidden + start + HIDDEN_BLOCK)
        gate = dot(ffn_normed, weight_rows(wi_ref, start, HIDDEN_BLOCK), 1, 1)
        up = dot(ffn_normed, weight_rows(wi_ref, hidden + start, HIDDEN_BLOCK), 1, 1)
        gu_ref[:, gate_cols] = gate.astype(BF16)
        gu_ref[:, up_cols] = up.astype(BF16)
        inner = (gelu_parts(gate)[1] * up).astype(BF16)
        inner_ref[:, gate_cols] = inner
        total += dot(inner, weight_rows(wo_ref, start, HIDDEN_BLOCK), 1, 0)
    fb_ref[...] = total
    result_ref[...] = middle + rms_norm(total, gain_of(gains_ref, POST_FFN))


def forward_layer(stream, weights, gains, tables, reach, count):
    tokens = stream.shape[0]
    cosine_tab, sine_tab = tables
    attn_in, attn_out, ffn_in, ffn_out = weights
    hidden = ffn_out[0].shape[0] * ffn_out[2]
    normed, key_raw, own, fetched = call(
        partial(key_value_kernel, [attn_in]), "key_value",
        (stream, gains, cosine_tab, sine_tab), [attn_in],
        [
            ((tokens, D), BF16), ((tokens, HEAD_DIM), F32), ((tokens, 2 * HEAD_DIM), BF16),
            ((attn_in[0].shape[0], attn_in[2], D), BF16),
        ],
        4 * tokens * D * HEAD_DIM, 12, handed=True,
    )
    before = neighbour(own, count, False)
    query_raw, queries = call(
        query_kernel, "query", (normed, gains, cosine_tab, sine_tab, fetched), [],
        [((tokens, QUERY_COLS), F32), ((tokens, QUERY_COLS), BF16)],
        2 * tokens * D * QUERY_COLS, 12,
    )
    context, lse, branch, middle, ffn_normed, gate_up, inner, ffn_branch, result = call(
        partial(block_kernel, [attn_out, ffn_in, ffn_out]), "block_forward",
        (queries, before, own, reach, stream, gains), [attn_out, ffn_in, ffn_out],
        [
            ((tokens, QUERY_COLS), BF16), (reach.shape, F32), ((tokens, D), F32), ((tokens, D), F32),
            ((tokens, D), BF16), ((tokens, 2 * hidden), BF16), ((tokens, hidden), BF16),
            ((tokens, D), F32), ((tokens, D), F32),
        ],
        2 * tokens * (D * (QUERY_COLS + 3 * hidden) + 2 * QUERY_COLS * KEY_COUNT), 32,
    )
    record = (
        stream, normed, query_raw, key_raw, queries, before, own, lse, context,
        branch, middle, ffn_normed, gate_up, inner, ffn_branch,
    )
    return record, result


def block_backward_kernel(
    weights, grad_ref, fb_ref, gu_ref, middle_ref, branch_ref, gains_ref, wa_any, wi_any, wo_any,
    gfb_ref, ggu_ref, gb_ref, gctx_ref, gmid_ref, sums_ref,
    wa_ref, wi_ref, wo_ref, sem,
):
    copies = [None] * 3
    for i, source, target in ((2, wo_any, wo_ref), (1, wi_any, wi_ref), (0, wa_any, wa_ref)):
        copies[i] = fetch(weights[i], source, target, sem.at[i])
    grad_out = grad_ref[...]
    grad_ffn_branch, post_ffn = rms_backward(fb_ref[...], gain_of(gains_ref, POST_FFN), grad_out)
    grad_ffn_branch = grad_ffn_branch.astype(BF16)
    gfb_ref[...] = grad_ffn_branch
    copies[2].wait()
    hidden = gu_ref.shape[1] // 2
    total = jnp.zeros(grad_ref.shape, F32)
    for start in range(0, hidden, HIDDEN_BLOCK):
        gate_cols = slice(start, start + HIDDEN_BLOCK)
        up_cols = slice(hidden + start, hidden + start + HIDDEN_BLOCK)
        grad_inner = dot(grad_ffn_branch, weight_rows(wo_ref, start, HIDDEN_BLOCK), 1, 1)
        gate = gu_ref[:, gate_cols].astype(F32)
        up = gu_ref[:, up_cols].astype(F32)
        tanh, value = gelu_parts(gate)
        slope = 0.5 * (1.0 + tanh) + 0.5 * gate * (1.0 - tanh * tanh) * GELU_A * (
            1.0 + 3.0 * GELU_B * gate * gate
        )
        grad_gate = (grad_inner * up * slope).astype(BF16)
        grad_up = (grad_inner * value).astype(BF16)
        ggu_ref[:, gate_cols] = grad_gate
        ggu_ref[:, up_cols] = grad_up
        if start == 0:
            copies[1].wait()
        total += dot(grad_gate, weight_rows(wi_ref, start, HIDDEN_BLOCK), 1, 0)
        total += dot(grad_up, weight_rows(wi_ref, hidden + start, HIDDEN_BLOCK), 1, 0)
    grad_part, pre_ffn = rms_backward(middle_ref[...], gain_of(gains_ref, PRE_FFN), total)
    grad_middle = grad_out + grad_part
    gmid_ref[...] = grad_middle
    grad_branch, post_attn = rms_backward(branch_ref[...], gain_of(gains_ref, POST_ATTN), grad_middle)
    grad_branch = grad_branch.astype(BF16)
    gb_ref[...] = grad_branch
    sums_ref[0:1, :] = post_attn
    sums_ref[1:2, :] = pre_ffn
    sums_ref[2:3, :] = post_ffn
    copies[0].wait()
    gctx_ref[...] = dot(grad_branch, weight_rows(wa_ref, 0, QUERY_COLS), 1, 1).astype(BF16)


def attention_backward_kernel(
    q_ref, before_ref, own_ref, reach_ref, lse_ref, g_ref, dq_ref, gbefore_ref, gown_ref, acc
):
    acc[...] = jnp.zeros_like(acc)
    for block in range(q_ref.shape[0] // QUERY_BLOCK):
        start = block * QUERY_BLOCK
        queries = stacked_heads(q_ref, start)
        grads = stacked_heads(g_ref, start)
        keys = window_rows(before_ref, own_ref, start, KEY_COUNT, KEYS)
        values = window_rows(before_ref, own_ref, start, KEY_COUNT, VALUES)
        allowed = allowed_pairs(start, KEY_COUNT, reach_ref[block : block + 1, :], HEADS * QUERY_BLOCK)
        scores = jnp.where(allowed, dot(keys, queries, 1, 1), MASKED_SCORE)
        probs = jnp.exp(scores - lse_ref[block : block + 1, :])
        grad_probs = dot(values, grads, 1, 1)
        inner = jnp.sum(probs * grad_probs, axis=0, keepdims=True)
        grad_scores = (probs * (grad_probs - inner)).astype(BF16)
        acc[start : start + KEY_COUNT, VALUES] += dot(probs.astype(BF16), grads, 1, 0)
        acc[start : start + KEY_COUNT, KEYS] += dot(grad_scores, queries, 1, 0)
        grad_queries = dot(grad_scores, keys, 0, 0) * SCORE_SCALE
        for h in range(HEADS):
            dq_ref[start : start + QUERY_BLOCK, h * HEAD_DIM : (h + 1) * HEAD_DIM] = grad_queries[
                h * QUERY_BLOCK : (h + 1) * QUERY_BLOCK
            ]
    gbefore_ref[...] = acc[:WINDOW, :].astype(BF16)
    gown_ref[...] = acc[WINDOW:, :]


def query_backward_kernel(dq_ref, raw_ref, gains_ref, cos_ref, sin_ref, gq_ref, sums_ref):
    cosine_tab, sine_tab = cos_ref[...], sin_ref[...]
    sums = jnp.zeros((1, HEAD_DIM), F32)
    for h in range(HEADS):
        columns = slice(h * HEAD_DIM, (h + 1) * HEAD_DIM)
        grad = rotate_back(dq_ref[:, columns], cosine_tab, sine_tab)
        grad, part = rms_backward(raw_ref[:, columns], gain_of(gains_ref, QUERY_GAIN), grad)
        gq_ref[:, columns] = grad.astype(BF16)
        sums += part
    sums_ref[...] = sums


def input_backward_kernel(
    weights, gq_ref, gown_ref, got_ref, kraw_ref, gmid_ref, stream_ref, gains_ref, cos_ref, sin_ref,
    sums_ref, qsums_ref, w_any, gproj_ref, gin_ref, ggains_ref, w_ref, sem,
):
    copy = fetch(weights[0], w_any, w_ref, sem.at[0])
    total = gown_ref[...] + got_ref[...].astype(F32)
    grad_keys = rotate_back(total[:, KEYS], cos_ref[...], sin_ref[...])
    grad_keys, key_sums = rms_backward(kraw_ref[...], gain_of(gains_ref, KEY_GAIN), grad_keys)
    gproj_ref[:, :QUERY_COLS] = gq_ref[...]
    gproj_ref[:, QUERY_COLS : QUERY_COLS + HEAD_DIM] = grad_keys.astype(BF16)
    gproj_ref[:, QUERY_COLS + HEAD_DIM :] = total[:, VALUES].astype(BF16)
    copy.wait()
    grad_normed = dot(gproj_ref[...], weight_rows(w_ref, 0, QUERY_COLS + 2 * HEAD_DIM), 1, 0)
    grad_part, sums = rms_backward(stream_ref[...], gain_of(gains_ref, PRE_ATTN), grad_normed)
    gin_ref[...] = gmid_ref[...] + grad_part
    found = [sums] + [sums_ref[i : i + 1, :] for i in range(3)] + [qsums_ref[...], key_sums]
    ggains_ref[...] = jnp.concatenate(found, axis=1)


def backward_layer(grad_out, weights, gains, record, tables, reach, count, pump, chains, last):
    attn_in, attn_out, ffn_in, ffn_out = weights
    cosine_tab, sine_tab = tables
    (
        stream, normed, query_raw, key_raw, queries, before, own, lse, context,
        branch, middle, ffn_normed, gate_up, inner, ffn_branch,
    ) = record
    tokens = stream.shape[0]
    hidden = inner.shape[1]
    grad_out = pump(0, grad_out)
    grad_ffn_branch, grad_gate_up, grad_branch, grad_context, grad_middle, sums = call(
        partial(block_backward_kernel, [attn_out, ffn_in, ffn_out]), "block_backward",
        (grad_out, ffn_branch, gate_up, middle, branch, gains), [attn_out, ffn_in, ffn_out],
        [
            ((tokens, D), BF16), ((tokens, 2 * hidden), BF16), ((tokens, D), BF16),
            ((tokens, QUERY_COLS), BF16), ((tokens, D), F32), ((8, D), F32),
        ],
        2 * tokens * D * (QUERY_COLS + 3 * hidden), 26,
    )
    grad_context = pump(1, grad_context)
    ffn = [(grad_gate_up, ffn_normed), (inner, grad_ffn_branch)]
    chains["ffn"] = Chain(ffn, last, fork=not last)
    grad_context = launch(grad_context, list(chains.values()))
    grad_queries, grad_before, grad_own = call(
        attention_backward_kernel, "attention_backward",
        (queries, before, own, reach, lse, grad_context), [],
        [((tokens, QUERY_COLS), F32), ((WINDOW, 2 * HEAD_DIM), BF16), ((tokens, 2 * HEAD_DIM), F32)],
        10 * tokens * QUERY_COLS * KEY_COUNT, 26,
        [pltpu.VMEM((WINDOW + tokens, 2 * HEAD_DIM), F32)],
    )
    got = neighbour(grad_before, count, True)
    grad_queries = pump(2, grad_queries)
    grad_query_raw, query_sums = call(
        query_backward_kernel, "query_backward",
        (grad_queries, query_raw, gains, cosine_tab, sine_tab), [],
        [((tokens, QUERY_COLS), BF16), ((1, HEAD_DIM), F32)],
        20 * tokens * QUERY_COLS, 12,
    )
    grad_query_raw = pump(3, grad_query_raw)
    grad_projected, grad_in, gain_grads = call(
        partial(input_backward_kernel, [attn_in]), "input_backward",
        (
            grad_query_raw, grad_own, got, key_raw, grad_middle, stream, gains, cosine_tab, sine_tab,
            sums, query_sums,
        ),
        [attn_in],
        [((tokens, QUERY_COLS + 2 * HEAD_DIM), BF16), ((tokens, D), F32), (gains.shape, F32)],
        2 * tokens * D * (QUERY_COLS + 2 * HEAD_DIM), 14,
    )
    n_dp, n_seq = lax.axis_size("dp"), lax.axis_size("seq")
    gain_grads = gain_grads.astype(BF16).reshape(n_dp, n_seq, 1, -1)
    extra = jnp.pad(gain_grads, ((0, 0), (0, 0), (0, TILE - 1), (0, D - gain_grads.shape[3])))
    attn = [(grad_projected, normed), (context, grad_branch)]
    chains["attn"] = Chain(attn, last, extra)
    return launch(grad_in, [chains["attn"]])


PLAN = {
    0: [(1, "attn")],
    1: [(1, "ffn"), (1, "attn")],
    2: [(0, "ffn")],
    3: [],
}


def gather_weights(shards, gains, behind):
    layers = gains.shape[0]
    gain_rows = jnp.pad(gains, ((0, TILE - layers), (0, D - gains.shape[1])))
    first = [(kind, l) for l in range(layers) for kind in range(len(shards)) if l == 0 or kind >= 2]
    later = [(kind, l) for l in range(1, layers) for kind in range(2)]
    found, rest = {}, None
    for names in (first, later):
        parts = [shards[kind][l] for kind, l in names]
        if names is first:
            parts.append(gain_rows)
        packed = jnp.concatenate(parts, axis=0)
        if names is later:
            behind, packed = lax.optimization_barrier((behind, packed))
        whole = lax.all_gather(packed, ALL, axis=0, tiled=False)
        at = 0
        for kind, l in names:
            size = shards[kind].shape[1]
            if size % TILE:
                found[kind, l] = (whole[:, at : at + size].reshape(1, -1, D), 0, size * whole.shape[0])
            else:
                found[kind, l] = (whole, at, size)
            at += size
        if names is first:
            gain_full = whole[:, at : at + layers, : gains.shape[1]].astype(F32)
    out = []
    for l in range(layers):
        ffn_in, ffn_out, attn_in, attn_out = [found[kind, l] for kind in range(4)]
        out.append(((attn_in, attn_out, ffn_in, ffn_out), gain_full[:, l].reshape(1, -1)))
    return out, behind


def body(hidden_in, positions, out_grad, w_attn_in, w_attn_out, w_ffn_in, w_ffn_out, gains):
    count = hidden_in.shape[0]
    layer_count = w_attn_in.shape[0]
    sizes = [w_ffn_in.shape[2], w_ffn_out.shape[1], w_attn_in.shape[2], w_attn_out.shape[1]]
    shards = [w_ffn_in.transpose(0, 2, 1), w_ffn_out, w_attn_in.transpose(0, 2, 1), w_attn_out]
    places = to_long(positions)
    stream = to_long(hidden_in).astype(F32)
    tables = angle_tables(places)
    tokens = places.shape[0]
    blocks = tokens // QUERY_BLOCK
    reach = jnp.minimum(places, WINDOW - 1).reshape(blocks, QUERY_BLOCK)
    reach = jnp.tile(reach, (1, HEADS))
    records = []
    weights, stream = gather_weights(shards, gains, stream)
    for layer_index in range(layer_count):
        record, stream = forward_layer(stream, *weights[layer_index], tables, reach, count)
        records.append(record)
        if layer_index == 0:
            stream, out_grad = lax.optimization_barrier((stream, out_grad))
            grad_stream = to_long(out_grad).astype(F32)
    hidden_out = to_short(stream.astype(BF16), count)
    outputs = {"hidden": hidden_out}
    chains = [{} for _ in range(layer_count + 1)]
    sums = [None] * layer_count
    for layer_index in reversed(range(layer_count)):

        def pump(where, value):
            active = [
                chains[layer_index + above][name]
                for above, name in PLAN[where]
                if name in chains[layer_index + above]
            ]
            value = advance(value, active)
            if where == 1 and layer_index + 1 == layer_count:
                value, outputs["hidden"] = lax.optimization_barrier((value, outputs["hidden"]))
            if where == 1 and layer_index + 1 < layer_count:
                above = chains[layer_index + 1]
                packed = jnp.concatenate([above["ffn"].finish(), above["attn"].finish()], axis=1)
                value, packed = lax.optimization_barrier((value, packed.astype(BF16)))
                sums[layer_index + 1] = lax.psum_scatter(packed, "seq", scatter_dimension=0)
            return value

        grad_stream = backward_layer(
            grad_stream, *weights[layer_index], records[layer_index], tables, reach, count, pump,
            chains[layer_index], layer_index > 0,
        )
    attn, ffn = [chains[0]["attn"]], chains[0]["ffn"].parts or [chains[0]["ffn"]]
    mark = grad_stream[:8]
    mark = advance(mark, ffn)
    mark = advance(mark, attn)
    mark = advance(mark, ffn)
    mark = advance(mark, attn)
    mark = advance(mark, ffn)
    mark, grad_stream = lax.optimization_barrier((mark, grad_stream))
    short = to_short(grad_stream.astype(BF16), count)
    mark = advance(mark, attn)
    mark = advance(mark, ffn)
    mark = advance(mark, attn)
    sums[0] = jnp.concatenate([chains[0]["ffn"].finish(), chains[0]["attn"].finish()], axis=1)[0]
    packed = jnp.stack([entry.astype(F32) for entry in sums])
    parts, at = [], 0
    for size in sizes:
        parts.append(packed[:, at : at + size])
        at += size
    return (
        outputs["hidden"],
        short.astype(F32),
        parts[2].transpose(0, 2, 1),
        parts[3],
        parts[0].transpose(0, 2, 1),
        parts[1],
        packed[:, at, : gains.shape[1]],
    )


def solution(mesh):
    return jax.shard_map(
        body,
        mesh=mesh,
        in_specs=(
            P("dp", "seq", None),
            P("dp", "seq"),
            P("dp", "seq", None),
            P(None, None, ("dp", "seq")),
            P(None, ("dp", "seq"), None),
            P(None, None, ("dp", "seq")),
            P(None, ("dp", "seq"), None),
            P(None, ("dp", "seq")),
        ),
        out_specs=(
            P("dp", "seq", None),
            P("dp", "seq", None),
            P(None, None, ("dp", "seq")),
            P(None, ("dp", "seq"), None),
            P(None, None, ("dp", "seq")),
            P(None, ("dp", "seq"), None),
            P(None, ("dp", "seq")),
        ),
        check_vma=False,
    )
```

```python
from functools import partial

import jax
import jax.numpy as jnp
from jax import lax
from jax.experimental import pallas as pl
from jax.experimental.pallas import tpu as pltpu
from jax.sharding import PartitionSpec as P

D = 640
HEADS = 4
HEAD_DIM = 256
WINDOW = 512
QUERY_BLOCK = 256

EPSILON = 1e-06
ROPE_BASE = 10000.0
SCORE_SCALE = 0.0625
MASKED_SCORE = -1e30
BF16 = jnp.bfloat16
VMEM_LIMIT = 44 * 2**20
VMEM_LIMIT_PRODUCT = 44 * 2**20
F32 = jnp.float32
ALL = ("dp", "seq")
TILE = 16
QUERY_COLS = HEADS * HEAD_DIM
GELU_A = 0.7978845608028654
GELU_B = 0.044715
HIDDEN_BLOCK = 512


def dot(a, b, a_dim, b_dim):
    return lax.dot_general(a, b, (((a_dim,), (b_dim,)), ((), ())), preferred_element_type=F32)


def angle_tables(places):
    half_dim = HEAD_DIM // 2
    inverse = ROPE_BASE ** (-(2.0 * jnp.arange(half_dim, dtype=F32)) / HEAD_DIM)
    phases = places.astype(F32)[..., None] * inverse
    return (jnp.cos(phases), jnp.sin(phases))


def inverse_rms(values):
    return lax.rsqrt(jnp.mean(values * values, axis=-1, keepdims=True) + EPSILON)


def rms_norm(values, gain):
    return values * inverse_rms(values) * gain


def rms_backward(values, gain, grad):
    scale = inverse_rms(values)
    weighted = grad * gain
    shared = jnp.mean(weighted * values, axis=-1, keepdims=True) * (scale * scale * scale)
    grad_gain = jnp.sum(grad * (values * scale), axis=0, keepdims=True)
    return weighted * scale - values * shared, grad_gain


def rotate(values, cosine_tab, sine_tab):
    half_dim = HEAD_DIM // 2
    first, second = values[:, :half_dim], values[:, half_dim:]
    return jnp.concatenate(
        [first * cosine_tab - second * sine_tab, second * cosine_tab + first * sine_tab], axis=-1
    )


def rotate_back(values, cosine_tab, sine_tab):
    return rotate(values, cosine_tab, -sine_tab)


def gain_of(gains_ref, which):
    starts = (0, D, 2 * D, 3 * D, 4 * D, 4 * D + HEAD_DIM)
    return gains_ref[:, starts[which] : starts[which] + (D if which < 4 else HEAD_DIM)]


PRE_ATTN, POST_ATTN, PRE_FFN, POST_FFN, QUERY_GAIN, KEY_GAIN = range(6)


def weight_rows(ref, start, size):
    shards, rows, width = ref.shape
    if shards == 1:
        return ref[0, start : start + size, :]
    first, last = start // rows, -(-(start + size) // rows)
    value = ref[first:last].reshape((last - first) * rows, width)
    skip = start - first * rows
    return value[skip : skip + size]


def fetch(weight, ref, scratch, sem):
    _, start, rows = weight
    copy = pltpu.make_async_copy(ref.at[:, pl.ds(start, rows), :], scratch, sem)
    copy.start()
    return copy


def weight_scratch(weight):
    array, _, rows = weight
    return pltpu.VMEM((array.shape[0], rows, D), BF16)


def vmem(count):
    return [pl.BlockSpec(memory_space=pltpu.VMEM)] * count


def call(kernel, name, arrays, weights, outs, flops, limit, scratch=(), handed=False):
    outs = [jax.ShapeDtypeStruct(shape, dtype) for shape, dtype in outs]
    moved = sum(a.size * a.dtype.itemsize for a in list(arrays) + outs)
    return pl.pallas_call(
        kernel,
        out_shape=tuple(outs),
        in_specs=vmem(len(arrays)) + [pl.BlockSpec(memory_space=pltpu.HBM)] * len(weights),
        out_specs=tuple(vmem(len(outs))),
        scratch_shapes=[weight_scratch(w) for w in weights if not handed]
        + ([pltpu.SemaphoreType.DMA((len(weights),))] if weights else [])
        + list(scratch),
        compiler_params=pltpu.CompilerParams(vmem_limit_bytes=VMEM_LIMIT),
        cost_estimate=pl.CostEstimate(flops=flops // 64, bytes_accessed=moved // 64, transcendentals=0),
        name=name,
    )(*arrays, *[w[0] for w in weights])


def chunk_route(count, k):
    n_dp, n_seq = lax.axis_size("dp"), lax.axis_size("seq")
    chips = n_seq // (2 * count)
    pairs = []
    for dp in range(n_dp):
        for i in range(n_seq):
            chunk = i // count
            sequence = (dp % 2) * count + (i + k) % count
            target_dp = dp - dp % 2 + chunk % 2
            pairs.append((dp * n_seq + i, target_dp * n_seq + sequence * chips + chunk // 2))
    return pairs


def place(count):
    chips = lax.axis_size("seq") // (2 * count)
    return (lax.axis_index("seq") // chips) % count


def to_long(block):
    count = block.shape[0]
    me = lax.axis_index("seq")
    received = []
    for k in range(count):
        piece = lax.dynamic_index_in_dim(block, (me + k) % count, 0, keepdims=False)
        received.append(lax.ppermute(piece, ALL, chunk_route(count, k)))
    twice = jnp.stack((received[::-1] * 2)[: 2 * count - 1])
    long = lax.dynamic_slice_in_dim(twice, count - 1 - place(count), count, 0)
    return long.reshape((count * block.shape[1],) + block.shape[2:])


def to_short(long, count):
    me = lax.axis_index("seq")
    parts = long.reshape((count, long.shape[0] // count) + long.shape[1:])
    received = []
    for k in range(count):
        piece = lax.dynamic_index_in_dim(parts, (place(count) - k) % count, 0, keepdims=False)
        route = [(j, i) for i, j in chunk_route(count, k)]
        received.append(lax.ppermute(piece, ALL, route))
    twice = jnp.stack((received * 2)[: 2 * count - 1])
    return lax.dynamic_slice_in_dim(twice, (count - me % count) % count, count, 0)


def neighbour(block, count, back):
    n_dp, n_seq = lax.axis_size("dp"), lax.axis_size("seq")
    chips = n_seq // (2 * count)
    pairs = []
    for dp in range(n_dp):
        for i in range(n_seq):
            if dp % 2 == 0:
                pairs.append((dp * n_seq + i, (dp + 1) * n_seq + i))
            elif (i + 1) % chips:
                pairs.append((dp * n_seq + i, (dp - 1) * n_seq + i + 1))
    if back:
        pairs = [(j, i) for i, j in pairs]
    return lax.ppermute(block, ALL, pairs)


def bits(axis):
    out, bit = [], 1
    while bit < lax.axis_size(axis):
        out.append((axis, bit))
        bit *= 2
    return out


def order(first, scatter):
    core, *wide = bits("dp")
    near, *far = bits("seq")
    if scatter:
        return [core] + wide
    if first == "dp":
        return [core] + wide + [near] + far[::-1]
    return [core, near] + wide + far[::-1]


def swap(array, step):
    axis, bit = step
    return lax.ppermute(array, axis, [(i, i ^ bit) for i in range(lax.axis_size(axis))])


def launch(value, chains):
    chains = [chain for chain in chains if chain.pending is not None]
    if not chains:
        return value
    held = lax.optimization_barrier((value,) + tuple(chain.pending for chain in chains))
    for chain, pending in zip(chains, held[1:]):
        chain.got = swap(pending, chain.steps[0])
        chain.sent, chain.pending = pending, None
    return held[0]


def advance(value, chains, after=()):
    chains = [chain for chain in chains if chain.steps]
    if not chains:
        return value
    held = lax.optimization_barrier((value,) + tuple(chain.got for chain in chains))
    for chain, got in zip(chains, held[1:]):
        chain.got = got
        chain.advance(after)
    return launch(held[0], chains + [part for chain in chains for part in chain.parts])


def block_numbers(scatter):
    me = lax.axis_index("dp")
    core = me % 2
    wide = [me // 2, (me // 2) ^ 1]
    leave = [2 * w + 1 - core for w in wide]
    stay = [2 * w + core for w in wide]
    along = lax.axis_index("seq") * (0 if scatter else 1)
    return jnp.stack(leave + stay + [along]).astype(jnp.int32)


def product_kernel(pairs, extra, added, outs, scatter, n_seq, numbers_ref, *refs):
    lefts, rights, refs = refs[:pairs], refs[pairs : 2 * pairs], refs[2 * pairs :]
    if extra:
        extra_ref, refs = refs[0], refs[1:]
    if added:
        got_ref, refs = refs[0], refs[1:]
    me, step = numbers_ref[4], pl.program_id(0)
    half = n_seq // 2

    def store(shard, base, value):
        entry = me ^ shard
        if not scatter:
            entry = lax.rem(entry, 2) * half + entry // 2
        place = slice(base, base + value.shape[0])
        if added:
            value = value + got_ref[0, entry, place].astype(F32)
        value = value.astype(BF16)
        for (kind, which, columns), ref in zip(outs, refs):
            if kind == "all":
                ref[0, entry, place] = value[:, columns]
                continue
            at = entry - which * half if kind == "half" else entry

            @pl.when((entry // half if kind == "half" else step) == which)
            def _():
                ref[0, at, place] = value[:, columns]

    base = 0
    for left, right in zip(lefts, rights):
        width = left.shape[1]
        rows = width // n_seq
        part = min(width, 512)
        for start in range(0, width, part):
            total = dot(left[:, start : start + part], right[...], 0, 0)
            for at in range(0, part, rows):
                store((start + at) // rows, base, total[at : at + rows])
        base += rows
    if extra:
        for shard in range(n_seq):
            store(shard, base, extra_ref[0, shard].astype(F32))


def product(factors, first, outs, got=None):
    pairs, extra, numbers, scatter = factors
    n_dp, n_seq = lax.axis_size("dp"), lax.axis_size("seq")
    tokens = pairs[0][0].shape[0]
    widths = [left.shape[1] // n_dp for left, _ in pairs]
    rows = sum(widths) // n_seq + (0 if extra is None else extra.shape[2])
    specs = [pl.BlockSpec((tokens, w), lambda i, n: (0, n[first + i])) for w in widths]
    specs += [pl.BlockSpec(right.shape, lambda i, n: (0, 0)) for _, right in pairs]
    operands = [left for left, _ in pairs] + [right for _, right in pairs]
    if extra is not None:
        specs.append(pl.BlockSpec((1,) + extra.shape[1:], lambda i, n: (n[first + i], 0, 0, 0)))
        operands.append(extra)
    if got is not None:
        specs.append(pl.BlockSpec((1, n_seq, rows, D), lambda i, n: (i, 0, 0, 0)))
        operands.append(got)
    shapes, out_specs = [], []
    for kind, _, columns in outs:
        wide = columns.stop - columns.start
        entries = n_seq // 2 if kind == "half" else n_seq
        shapes.append(jax.ShapeDtypeStruct((1 if kind == "block" else 2, entries, rows, wide), BF16))
        index = (lambda i, n: (0, 0, 0, 0)) if kind == "block" else (lambda i, n: (i, 0, 0, 0))
        out_specs.append(pl.BlockSpec((1, entries, rows, wide), index))
    return pl.pallas_call(
        partial(product_kernel, len(pairs), extra is not None, got is not None, outs, scatter, n_seq),
        grid_spec=pltpu.PrefetchScalarGridSpec(
            num_scalar_prefetch=1, grid=(2,), in_specs=specs, out_specs=out_specs
        ),
        out_shape=shapes,
        compiler_params=pltpu.CompilerParams(vmem_limit_bytes=VMEM_LIMIT_PRODUCT),
        cost_estimate=pl.CostEstimate(
            flops=tokens * sum(widths) * D // 16,
            bytes_accessed=(tokens + 2 * D) * sum(widths) // 16,
            transcendentals=0,
        ),
        name="weight_gradient",
    )(numbers, *operands)


WHOLE, CUT = slice(0, D), 3 * D // 5


def fold_kernel(k0_ref, k1_ref, g0_ref, g1_ref, *refs):
    keep_ref, send_ref = refs[-2:]
    keep_ref[...] = (k0_ref[...].astype(F32) + g0_ref[...].astype(F32)).astype(BF16)
    send_ref[...] = (k1_ref[...].astype(F32) + g1_ref[...].astype(F32)).astype(BF16)


def fold(keep, got, after):
    half = keep.shape[0] // 2
    block = (1,) + keep.shape[1:]
    near = pl.BlockSpec(block, lambda i: (i, 0, 0))
    far = pl.BlockSpec(block, lambda i: (i + half, 0, 0))
    return pl.pallas_call(
        fold_kernel,
        grid=(half,),
        in_specs=[near, far, near, far] + [pl.BlockSpec(memory_space=pltpu.HBM)] * len(after),
        out_specs=[near, near],
        out_shape=[jax.ShapeDtypeStruct((half,) + keep.shape[1:], BF16)] * 2,
        compiler_params=pltpu.CompilerParams(vmem_limit_bytes=VMEM_LIMIT_PRODUCT),
        name="fold_sums",
    )(keep, keep, got, got, *after)


class Chain:
    def __init__(self, pairs, scatter=False, extra=None, fork=False, first="dp"):
        self.steps = order(first, scatter)
        self.fork = fork
        self.parts = []
        n_dp, n_seq = lax.axis_size("dp"), lax.axis_size("seq")
        widths = [left.shape[1] // n_dp for left, _ in pairs]
        self.factors = None
        self.rows = sum(widths) // n_seq + (0 if extra is None else extra.shape[2])
        if n_dp == 4 and all(w % 128 == 0 and w % (n_seq * TILE) == 0 for w in widths):
            self.factors = (pairs, extra, block_numbers(scatter), scatter)
            (self.pending,) = product(self.factors, 0, [("all", 0, WHOLE)])
            return
        devices = n_dp * n_seq
        parts = [
            dot(left, right, 0, 0).astype(BF16).reshape(devices, -1, D) for left, right in pairs
        ]
        if extra is not None:
            parts.append(extra.reshape(devices, -1, D))
        target = jnp.arange(devices)
        source, left_over = jnp.zeros_like(target), devices
        for axis, bit in self.steps:
            left_over //= 2
            source = source + (target // left_over) % 2 * (bit * n_seq if axis == "dp" else bit)
        if scatter:
            source = source + target % n_seq
        me = lax.axis_index("dp") * n_seq
        if not scatter:
            me = me + lax.axis_index("seq")
        self.cut(jnp.take(jnp.concatenate(parts, axis=1), me ^ source, axis=0))

    def part(self, steps, keep, pending):
        chain = object.__new__(Chain)
        chain.steps, chain.factors, chain.fork, chain.parts = steps, None, False, []
        chain.rows = self.rows
        chain.keep, chain.pending = keep, pending
        self.parts.append(chain)

    def cut(self, array):
        half = array.shape[0] // 2
        self.keep, self.pending = array[:half], array[half:]

    def advance(self, after=()):
        self.steps = self.steps[1:]
        if after and self.steps and not self.factors and self.rows % TILE == 0:
            self.keep, self.pending = fold(self.keep, self.got, after)
            return
        if self.factors:
            factors, self.factors = self.factors, None
            kind = "block" if self.steps[0][0] == "dp" else "half"
            outs = [(kind, 0, WHOLE), (kind, 1, WHOLE)]
            if self.fork:
                a, b = slice(0, CUT), slice(CUT, D)
                outs = [("block", 0, a), ("block", 1, a), ("half", 0, b), ("half", 1, b)]
            found = product(factors, 2, outs, self.got)
            found = [array.reshape((-1, self.rows) + array.shape[3:]) for array in found]
            if self.fork:
                self.pending = None
                self.part(order("dp", False)[1:], *found[:2])
                self.part(order("seq", False)[1:], *found[2:])
                self.steps = []
            else:
                self.keep, self.pending = found
            return
        array = self.keep.astype(F32) + self.got.astype(F32)
        if self.steps:
            self.cut(array.astype(BF16))
        else:
            self.result = array

    def finish(self):
        if self.parts:
            return jnp.concatenate([part.finish() for part in self.parts], axis=2)
        while self.steps:
            if self.pending is not None:
                self.got = swap(self.pending, self.steps[0])
                self.pending = None
            self.advance()
        return self.result


def round_kernel(waits, value_ref, *refs):
    refs[waits][...] = value_ref[...].astype(BF16)


def rounded(value, after):
    return pl.pallas_call(
        partial(round_kernel, len(after)),
        in_specs=[pl.BlockSpec(memory_space=pltpu.VMEM)] + [pl.BlockSpec(memory_space=pltpu.HBM)] * len(after),
        out_specs=pl.BlockSpec(memory_space=pltpu.VMEM),
        out_shape=jax.ShapeDtypeStruct(value.shape, BF16),
        compiler_params=pltpu.CompilerParams(vmem_limit_bytes=VMEM_LIMIT_PRODUCT),
        name="round_gradient",
    )(value, *after)


def allowed_pairs(start, key_count, reach, lanes):
    key_at = lax.broadcasted_iota(jnp.int32, (key_count, lanes), 0)
    query_at = lax.broadcasted_iota(jnp.int32, (key_count, lanes), 1) % QUERY_BLOCK
    distance = query_at + WINDOW - key_at
    return (distance >= 0) & (distance <= reach)


def stacked_heads(ref, start):
    return jnp.concatenate(
        [
            ref[start : start + QUERY_BLOCK, h * HEAD_DIM : (h + 1) * HEAD_DIM]
            for h in range(HEADS)
        ],
        axis=0,
    )


def window_rows(before_ref, own_ref, start, count, columns):
    return jnp.concatenate(
        [before_ref[start:, columns], own_ref[: count - (WINDOW - start), columns]], axis=0
    )


KEYS, VALUES = slice(0, HEAD_DIM), slice(HEAD_DIM, 2 * HEAD_DIM)
KEY_COUNT = QUERY_BLOCK + WINDOW


def key_value_kernel(weights, stream_ref, gains_ref, cos_ref, sin_ref, w_any, normed_ref, raw_ref, own_ref, w_ref, sem):
    copy = fetch(weights[0], w_any, w_ref, sem.at[0])
    normed = rms_norm(stream_ref[...], gain_of(gains_ref, PRE_ATTN)).astype(BF16)
    normed_ref[...] = normed
    copy.wait()
    raw = dot(normed, weight_rows(w_ref, QUERY_COLS, 2 * HEAD_DIM), 1, 1)
    raw_ref[...] = raw[:, KEYS]
    keys = rms_norm(raw[:, KEYS], gain_of(gains_ref, KEY_GAIN))
    own_ref[:, KEYS] = rotate(keys, cos_ref[...], sin_ref[...]).astype(BF16)
    own_ref[:, VALUES] = raw[:, VALUES].astype(BF16)


def query_kernel(normed_ref, gains_ref, cos_ref, sin_ref, w_ref, raw_ref, q_ref):
    cosine_tab, sine_tab = cos_ref[...], sin_ref[...]
    normed = normed_ref[...]
    for h in range(HEADS):
        columns = slice(h * HEAD_DIM, (h + 1) * HEAD_DIM)
        raw = dot(normed, weight_rows(w_ref, h * HEAD_DIM, HEAD_DIM), 1, 1)
        raw_ref[:, columns] = raw
        queries = rotate(rms_norm(raw, gain_of(gains_ref, QUERY_GAIN)), cosine_tab, sine_tab)
        q_ref[:, columns] = queries.astype(BF16) * SCORE_SCALE


def gelu_parts(gate):
    inner = GELU_A * (gate + GELU_B * gate * gate * gate)
    tanh = jnp.tanh(inner)
    return tanh, 0.5 * gate * (1.0 + tanh)


def block_kernel(
    weights, q_ref, before_ref, own_ref, reach_ref, stream_ref, gains_ref, wa_any, wi_any, wo_any,
    ctx_ref, lse_ref, branch_ref, middle_ref, fn_ref, gu_ref, inner_ref, fb_ref, result_ref,
    wa_ref, wi_ref, wo_ref, sem,
):
    copies = [
        fetch(weight, source, target, sem.at[i])
        for i, (weight, source, target) in enumerate(
            zip(weights, (wa_any, wi_any, wo_any), (wa_ref, wi_ref, wo_ref))
        )
    ]
    for block in range(q_ref.shape[0] // QUERY_BLOCK):
        start = block * QUERY_BLOCK
        queries = stacked_heads(q_ref, start)
        keys = window_rows(before_ref, own_ref, start, KEY_COUNT, KEYS)
        values = window_rows(before_ref, own_ref, start, KEY_COUNT, VALUES)
        allowed = allowed_pairs(start, KEY_COUNT, reach_ref[block : block + 1, :], HEADS * QUERY_BLOCK)
        scores = jnp.where(allowed, dot(keys, queries, 1, 1), MASKED_SCORE)
        row_max = jnp.max(scores, axis=0, keepdims=True)
        exps = jnp.exp(scores - row_max)
        row_sum = jnp.sum(exps, axis=0, keepdims=True)
        probs = (exps * (1.0 / row_sum)).astype(BF16)
        lse_ref[block : block + 1, :] = row_max + jnp.log(row_sum)
        context = dot(probs, values, 0, 0).astype(BF16)
        for h in range(HEADS):
            ctx_ref[start : start + QUERY_BLOCK, h * HEAD_DIM : (h + 1) * HEAD_DIM] = context[
                h * QUERY_BLOCK : (h + 1) * QUERY_BLOCK
            ]
    copies[0].wait()
    branch = dot(ctx_ref[...], weight_rows(wa_ref, 0, QUERY_COLS), 1, 0)
    branch_ref[...] = branch
    middle = stream_ref[...] + rms_norm(branch, gain_of(gains_ref, POST_ATTN))
    middle_ref[...] = middle
    ffn_normed = rms_norm(middle, gain_of(gains_ref, PRE_FFN)).astype(BF16)
    fn_ref[...] = ffn_normed
    copies[1].wait()
    copies[2].wait()
    hidden = inner_ref.shape[1]
    total = jnp.zeros(branch_ref.shape, F32)
    for start in range(0, hidden, HIDDEN_BLOCK):
        gate_cols = slice(start, start + HIDDEN_BLOCK)
        up_cols = slice(hidden + start, hidden + start + HIDDEN_BLOCK)
        gate = dot(ffn_normed, weight_rows(wi_ref, start, HIDDEN_BLOCK), 1, 1)
        up = dot(ffn_normed, weight_rows(wi_ref, hidden + start, HIDDEN_BLOCK), 1, 1)
        gu_ref[:, gate_cols] = gate.astype(BF16)
        gu_ref[:, up_cols] = up.astype(BF16)
        inner = (gelu_parts(gate)[1] * up).astype(BF16)
        inner_ref[:, gate_cols] = inner
        total += dot(inner, weight_rows(wo_ref, start, HIDDEN_BLOCK), 1, 0)
    fb_ref[...] = total
    result_ref[...] = middle + rms_norm(total, gain_of(gains_ref, POST_FFN))


def forward_layer(stream, weights, gains, tables, reach, count):
    tokens = stream.shape[0]
    cosine_tab, sine_tab = tables
    attn_in, attn_out, ffn_in, ffn_out = weights
    hidden = ffn_out[0].shape[0] * ffn_out[2]
    normed, key_raw, own, fetched = call(
        partial(key_value_kernel, [attn_in]), "key_value",
        (stream, gains, cosine_tab, sine_tab), [attn_in],
        [
            ((tokens, D), BF16), ((tokens, HEAD_DIM), F32), ((tokens, 2 * HEAD_DIM), BF16),
            ((attn_in[0].shape[0], attn_in[2], D), BF16),
        ],
        4 * tokens * D * HEAD_DIM, 12, handed=True,
    )
    before = neighbour(own, count, False)
    query_raw, queries = call(
        query_kernel, "query", (normed, gains, cosine_tab, sine_tab, fetched), [],
        [((tokens, QUERY_COLS), F32), ((tokens, QUERY_COLS), BF16)],
        2 * tokens * D * QUERY_COLS, 12,
    )
    context, lse, branch, middle, ffn_normed, gate_up, inner, ffn_branch, result = call(
        partial(block_kernel, [attn_out, ffn_in, ffn_out]), "block_forward",
        (queries, before, own, reach, stream, gains), [attn_out, ffn_in, ffn_out],
        [
            ((tokens, QUERY_COLS), BF16), (reach.shape, F32), ((tokens, D), F32), ((tokens, D), F32),
            ((tokens, D), BF16), ((tokens, 2 * hidden), BF16), ((tokens, hidden), BF16),
            ((tokens, D), F32), ((tokens, D), F32),
        ],
        2 * tokens * (D * (QUERY_COLS + 3 * hidden) + 2 * QUERY_COLS * KEY_COUNT), 32,
    )
    record = (
        stream, normed, query_raw, key_raw, queries, before, own, lse, context,
        branch, middle, ffn_normed, gate_up, inner, ffn_branch,
    )
    return record, result


def block_backward_kernel(
    weights, grad_ref, fb_ref, gu_ref, middle_ref, branch_ref, gains_ref, wa_any, wi_any, wo_any,
    gfb_ref, ggu_ref, gb_ref, gctx_ref, gmid_ref, sums_ref,
    wa_ref, wi_ref, wo_ref, sem,
):
    copies = [None] * 3
    for i, source, target in ((2, wo_any, wo_ref), (1, wi_any, wi_ref), (0, wa_any, wa_ref)):
        copies[i] = fetch(weights[i], source, target, sem.at[i])
    grad_out = grad_ref[...]
    grad_ffn_branch, post_ffn = rms_backward(fb_ref[...], gain_of(gains_ref, POST_FFN), grad_out)
    grad_ffn_branch = grad_ffn_branch.astype(BF16)
    gfb_ref[...] = grad_ffn_branch
    copies[2].wait()
    hidden = gu_ref.shape[1] // 2
    total = jnp.zeros(grad_ref.shape, F32)
    for start in range(0, hidden, HIDDEN_BLOCK):
        gate_cols = slice(start, start + HIDDEN_BLOCK)
        up_cols = slice(hidden + start, hidden + start + HIDDEN_BLOCK)
        grad_inner = dot(grad_ffn_branch, weight_rows(wo_ref, start, HIDDEN_BLOCK), 1, 1)
        gate = gu_ref[:, gate_cols].astype(F32)
        up = gu_ref[:, up_cols].astype(F32)
        tanh, value = gelu_parts(gate)
        slope = 0.5 * (1.0 + tanh) + 0.5 * gate * (1.0 - tanh * tanh) * GELU_A * (
            1.0 + 3.0 * GELU_B * gate * gate
        )
        grad_gate = (grad_inner * up * slope).astype(BF16)
        grad_up = (grad_inner * value).astype(BF16)
        ggu_ref[:, gate_cols] = grad_gate
        ggu_ref[:, up_cols] = grad_up
        if start == 0:
            copies[1].wait()
        total += dot(grad_gate, weight_rows(wi_ref, start, HIDDEN_BLOCK), 1, 0)
        total += dot(grad_up, weight_rows(wi_ref, hidden + start, HIDDEN_BLOCK), 1, 0)
    grad_part, pre_ffn = rms_backward(middle_ref[...], gain_of(gains_ref, PRE_FFN), total)
    grad_middle = grad_out + grad_part
    gmid_ref[...] = grad_middle
    grad_branch, post_attn = rms_backward(branch_ref[...], gain_of(gains_ref, POST_ATTN), grad_middle)
    grad_branch = grad_branch.astype(BF16)
    gb_ref[...] = grad_branch
    sums_ref[0:1, :] = post_attn
    sums_ref[1:2, :] = pre_ffn
    sums_ref[2:3, :] = post_ffn
    copies[0].wait()
    gctx_ref[...] = dot(grad_branch, weight_rows(wa_ref, 0, QUERY_COLS), 1, 1).astype(BF16)


def attention_backward_kernel(
    q_ref, before_ref, own_ref, reach_ref, lse_ref, g_ref, dq_ref, gbefore_ref, gown_ref, acc
):
    acc[...] = jnp.zeros_like(acc)
    for block in range(q_ref.shape[0] // QUERY_BLOCK):
        start = block * QUERY_BLOCK
        queries = stacked_heads(q_ref, start)
        grads = stacked_heads(g_ref, start)
        keys = window_rows(before_ref, own_ref, start, KEY_COUNT, KEYS)
        values = window_rows(before_ref, own_ref, start, KEY_COUNT, VALUES)
        allowed = allowed_pairs(start, KEY_COUNT, reach_ref[block : block + 1, :], HEADS * QUERY_BLOCK)
        scores = jnp.where(allowed, dot(keys, queries, 1, 1), MASKED_SCORE)
        probs = jnp.exp(scores - lse_ref[block : block + 1, :])
        grad_probs = dot(values, grads, 1, 1)
        inner = jnp.sum(probs * grad_probs, axis=0, keepdims=True)
        grad_scores = (probs * (grad_probs - inner)).astype(BF16)
        acc[start : start + KEY_COUNT, VALUES] += dot(probs.astype(BF16), grads, 1, 0)
        acc[start : start + KEY_COUNT, KEYS] += dot(grad_scores, queries, 1, 0)
        grad_queries = dot(grad_scores, keys, 0, 0) * SCORE_SCALE
        for h in range(HEADS):
            dq_ref[start : start + QUERY_BLOCK, h * HEAD_DIM : (h + 1) * HEAD_DIM] = grad_queries[
                h * QUERY_BLOCK : (h + 1) * QUERY_BLOCK
            ]
    gbefore_ref[...] = acc[:WINDOW, :].astype(BF16)
    gown_ref[...] = acc[WINDOW:, :]


def query_backward_kernel(dq_ref, raw_ref, gains_ref, cos_ref, sin_ref, gq_ref, sums_ref):
    cosine_tab, sine_tab = cos_ref[...], sin_ref[...]
    sums = jnp.zeros((1, HEAD_DIM), F32)
    for h in range(HEADS):
        columns = slice(h * HEAD_DIM, (h + 1) * HEAD_DIM)
        grad = rotate_back(dq_ref[:, columns], cosine_tab, sine_tab)
        grad, part = rms_backward(raw_ref[:, columns], gain_of(gains_ref, QUERY_GAIN), grad)
        gq_ref[:, columns] = grad.astype(BF16)
        sums += part
    sums_ref[...] = sums


def input_backward_kernel(
    weights, gq_ref, gown_ref, got_ref, kraw_ref, gmid_ref, stream_ref, gains_ref, cos_ref, sin_ref,
    sums_ref, qsums_ref, w_any, gproj_ref, gin_ref, ggains_ref, w_ref, sem,
):
    copy = fetch(weights[0], w_any, w_ref, sem.at[0])
    total = gown_ref[...] + got_ref[...].astype(F32)
    grad_keys = rotate_back(total[:, KEYS], cos_ref[...], sin_ref[...])
    grad_keys, key_sums = rms_backward(kraw_ref[...], gain_of(gains_ref, KEY_GAIN), grad_keys)
    gproj_ref[:, :QUERY_COLS] = gq_ref[...]
    gproj_ref[:, QUERY_COLS : QUERY_COLS + HEAD_DIM] = grad_keys.astype(BF16)
    gproj_ref[:, QUERY_COLS + HEAD_DIM :] = total[:, VALUES].astype(BF16)
    copy.wait()
    grad_normed = dot(gproj_ref[...], weight_rows(w_ref, 0, QUERY_COLS + 2 * HEAD_DIM), 1, 0)
    grad_part, sums = rms_backward(stream_ref[...], gain_of(gains_ref, PRE_ATTN), grad_normed)
    gin_ref[...] = gmid_ref[...] + grad_part
    found = [sums] + [sums_ref[i : i + 1, :] for i in range(3)] + [qsums_ref[...], key_sums]
    ggains_ref[...] = jnp.concatenate(found, axis=1)


def backward_layer(grad_out, weights, gains, record, tables, reach, count, pump, chains, last):
    attn_in, attn_out, ffn_in, ffn_out = weights
    cosine_tab, sine_tab = tables
    (
        stream, normed, query_raw, key_raw, queries, before, own, lse, context,
        branch, middle, ffn_normed, gate_up, inner, ffn_branch,
    ) = record
    tokens = stream.shape[0]
    hidden = inner.shape[1]
    grad_out = pump(0, grad_out)
    grad_ffn_branch, grad_gate_up, grad_branch, grad_context, grad_middle, sums = call(
        partial(block_backward_kernel, [attn_out, ffn_in, ffn_out]), "block_backward",
        (grad_out, ffn_branch, gate_up, middle, branch, gains), [attn_out, ffn_in, ffn_out],
        [
            ((tokens, D), BF16), ((tokens, 2 * hidden), BF16), ((tokens, D), BF16),
            ((tokens, QUERY_COLS), BF16), ((tokens, D), F32), ((8, D), F32),
        ],
        2 * tokens * D * (QUERY_COLS + 3 * hidden), 26,
    )
    grad_context = pump(1, grad_context)
    ffn = [(grad_gate_up, ffn_normed), (inner, grad_ffn_branch)]
    chains["ffn"] = Chain(ffn, last, fork=not last)
    grad_context = launch(grad_context, list(chains.values()))
    grad_queries, grad_before, grad_own = call(
        attention_backward_kernel, "attention_backward",
        (queries, before, own, reach, lse, grad_context), [],
        [((tokens, QUERY_COLS), F32), ((WINDOW, 2 * HEAD_DIM), BF16), ((tokens, 2 * HEAD_DIM), F32)],
        10 * tokens * QUERY_COLS * KEY_COUNT, 26,
        [pltpu.VMEM((WINDOW + tokens, 2 * HEAD_DIM), F32)],
    )
    got = neighbour(grad_before, count, True)
    grad_queries = pump(2, grad_queries)
    grad_query_raw, query_sums = call(
        query_backward_kernel, "query_backward",
        (grad_queries, query_raw, gains, cosine_tab, sine_tab), [],
        [((tokens, QUERY_COLS), BF16), ((1, HEAD_DIM), F32)],
        20 * tokens * QUERY_COLS, 12,
    )
    grad_query_raw = pump(3, grad_query_raw)
    grad_projected, grad_in, gain_grads = call(
        partial(input_backward_kernel, [attn_in]), "input_backward",
        (
            grad_query_raw, grad_own, got, key_raw, grad_middle, stream, gains, cosine_tab, sine_tab,
            sums, query_sums,
        ),
        [attn_in],
        [((tokens, QUERY_COLS + 2 * HEAD_DIM), BF16), ((tokens, D), F32), (gains.shape, F32)],
        2 * tokens * D * (QUERY_COLS + 2 * HEAD_DIM), 14,
    )
    n_dp, n_seq = lax.axis_size("dp"), lax.axis_size("seq")
    gain_grads = gain_grads.astype(BF16).reshape(n_dp, n_seq, 1, -1)
    extra = jnp.pad(gain_grads, ((0, 0), (0, 0), (0, TILE - 1), (0, D - gain_grads.shape[3])))
    attn = [(grad_projected, normed), (context, grad_branch)]
    chains["attn"] = Chain(attn, extra=extra, first="seq" if last else "dp")
    return launch(grad_in, [chains["attn"]])


PLAN = {
    0: [(1, "attn")],
    1: [(1, "ffn")],
    2: [(0, "ffn"), (1, "attn")],
    3: [(1, "attn")],
}


def gather_weights(shards, gains, behind):
    layers = gains.shape[0]
    gain_rows = jnp.pad(gains, ((0, TILE - layers), (0, D - gains.shape[1])))
    first = [(kind, l) for l in range(layers) for kind in range(len(shards)) if l == 0 or kind >= 2]
    later = [(kind, l) for l in range(1, layers) for kind in range(2)]
    found, rest = {}, None
    for names in (first, later):
        parts = [shards[kind][l] for kind, l in names]
        if names is first:
            parts.append(gain_rows)
        packed = jnp.concatenate(parts, axis=0)
        if names is later:
            behind, packed = lax.optimization_barrier((behind, packed))
        whole = lax.all_gather(packed, ALL, axis=0, tiled=False)
        at = 0
        for kind, l in names:
            size = shards[kind].shape[1]
            if size % TILE:
                found[kind, l] = (whole[:, at : at + size].reshape(1, -1, D), 0, size * whole.shape[0])
            else:
                found[kind, l] = (whole, at, size)
            at += size
        if names is first:
            gain_full = whole[:, at : at + layers, : gains.shape[1]].astype(F32)
    out = []
    for l in range(layers):
        ffn_in, ffn_out, attn_in, attn_out = [found[kind, l] for kind in range(4)]
        out.append(((attn_in, attn_out, ffn_in, ffn_out), gain_full[:, l].reshape(1, -1)))
    return out, behind


def body(hidden_in, positions, out_grad, w_attn_in, w_attn_out, w_ffn_in, w_ffn_out, gains):
    count = hidden_in.shape[0]
    layer_count = w_attn_in.shape[0]
    sizes = [w_ffn_in.shape[2], w_ffn_out.shape[1], w_attn_in.shape[2], w_attn_out.shape[1]]
    shards = [w_ffn_in.transpose(0, 2, 1), w_ffn_out, w_attn_in.transpose(0, 2, 1), w_attn_out]
    places = to_long(positions)
    stream = to_long(hidden_in).astype(F32)
    tables = angle_tables(places)
    tokens = places.shape[0]
    blocks = tokens // QUERY_BLOCK
    reach = jnp.minimum(places, WINDOW - 1).reshape(blocks, QUERY_BLOCK)
    reach = jnp.tile(reach, (1, HEADS))
    records = []
    weights, stream = gather_weights(shards, gains, stream)
    for layer_index in range(layer_count):
        record, stream = forward_layer(stream, *weights[layer_index], tables, reach, count)
        records.append(record)
        if layer_index == 0:
            stream, out_grad = lax.optimization_barrier((stream, out_grad))
            grad_stream = to_long(out_grad).astype(F32)
    hidden_out = to_short(stream.astype(BF16), count)
    outputs = {"hidden": hidden_out}
    chains = [{} for _ in range(layer_count + 1)]
    sums = [None] * layer_count
    for layer_index in reversed(range(layer_count)):

        def pump(where, value):
            active = [
                chains[layer_index + above][name]
                for above, name in PLAN[where]
                if name in chains[layer_index + above]
            ]
            value = advance(value, active)
            if where == 1 and layer_index + 1 == layer_count:
                value, outputs["hidden"] = lax.optimization_barrier((value, outputs["hidden"]))
            if where == 1 and layer_index + 1 < layer_count:
                above = chains[layer_index + 1]
                packed = above["ffn"].finish().astype(BF16)
                sums[layer_index + 1] = lax.psum_scatter(packed, "seq", scatter_dimension=0)
            return value

        grad_stream = backward_layer(
            grad_stream, *weights[layer_index], records[layer_index], tables, reach, count, pump,
            chains[layer_index], layer_index > 0,
        )
    attn, ffn = [chains[0]["attn"]], chains[0]["ffn"].parts or [chains[0]["ffn"]]
    mark = grad_stream[:8]
    mark = advance(mark, ffn, [chain.sent for chain in attn])
    for chains_now in (attn, ffn):
        mark = advance(mark, chains_now)
    short = to_short(rounded(grad_stream, [chain.keep for chain in ffn]), count)
    for layer in range(1, layer_count):
        found = chains[layer]["attn"].finish()[0]
        sums[layer] = jnp.concatenate([sums[layer].astype(F32), found], axis=0)
    for chains_now in (attn, ffn, attn, ffn, attn):
        mark = advance(mark, chains_now)
    sums[0] = jnp.concatenate([chains[0]["ffn"].finish(), chains[0]["attn"].finish()], axis=1)[0]
    packed = jnp.stack([entry.astype(F32) for entry in sums])
    parts, at = [], 0
    for size in sizes:
        parts.append(packed[:, at : at + size])
        at += size
    return (
        outputs["hidden"],
        short.astype(F32),
        parts[2].transpose(0, 2, 1),
        parts[3],
        parts[0].transpose(0, 2, 1),
        parts[1],
        packed[:, at, : gains.shape[1]],
    )


def solution(mesh):
    return jax.shard_map(
        body,
        mesh=mesh,
        in_specs=(
            P("dp", "seq", None),
            P("dp", "seq"),
            P("dp", "seq", None),
            P(None, None, ("dp", "seq")),
            P(None, ("dp", "seq"), None),
            P(None, None, ("dp", "seq")),
            P(None, ("dp", "seq"), None),
            P(None, ("dp", "seq")),
        ),
        out_specs=(
            P("dp", "seq", None),
            P("dp", "seq", None),
            P(None, None, ("dp", "seq")),
            P(None, ("dp", "seq"), None),
            P(None, None, ("dp", "seq")),
            P(None, ("dp", "seq"), None),
            P(None, ("dp", "seq")),
        ),
        check_vma=False,
    )
```

```python
from functools import partial

import jax
import jax.numpy as jnp
from jax import lax
from jax.experimental import pallas as pl
from jax.experimental.pallas import tpu as pltpu
from jax.sharding import PartitionSpec as P

D = 640
HEADS = 4
HEAD_DIM = 256
WINDOW = 512
QUERY_BLOCK = 256

EPSILON = 1e-06
ROPE_BASE = 10000.0
SCORE_SCALE = 0.0625
MASKED_SCORE = -1e30
BF16 = jnp.bfloat16
VMEM_LIMIT = 44 * 2**20
VMEM_LIMIT_PRODUCT = 44 * 2**20
F32 = jnp.float32
ALL = ("dp", "seq")
TILE = 16
QUERY_COLS = HEADS * HEAD_DIM
GELU_A = 0.7978845608028654
GELU_B = 0.044715
HIDDEN_BLOCK = 512


def dot(a, b, a_dim, b_dim):
    return lax.dot_general(a, b, (((a_dim,), (b_dim,)), ((), ())), preferred_element_type=F32)


def angle_tables(places):
    half_dim = HEAD_DIM // 2
    inverse = ROPE_BASE ** (-(2.0 * jnp.arange(half_dim, dtype=F32)) / HEAD_DIM)
    phases = places.astype(F32)[..., None] * inverse
    return (jnp.cos(phases), jnp.sin(phases))


def inverse_rms(values):
    return lax.rsqrt(jnp.mean(values * values, axis=-1, keepdims=True) + EPSILON)


def rms_norm(values, gain):
    return values * inverse_rms(values) * gain


def rms_backward(values, gain, grad):
    scale = inverse_rms(values)
    weighted = grad * gain
    shared = jnp.mean(weighted * values, axis=-1, keepdims=True) * (scale * scale * scale)
    grad_gain = jnp.sum(grad * (values * scale), axis=0, keepdims=True)
    return weighted * scale - values * shared, grad_gain


def rotate(values, cosine_tab, sine_tab):
    half_dim = HEAD_DIM // 2
    first, second = values[:, :half_dim], values[:, half_dim:]
    return jnp.concatenate(
        [first * cosine_tab - second * sine_tab, second * cosine_tab + first * sine_tab], axis=-1
    )


def rotate_back(values, cosine_tab, sine_tab):
    return rotate(values, cosine_tab, -sine_tab)


def gain_of(gains_ref, which):
    starts = (0, D, 2 * D, 3 * D, 4 * D, 4 * D + HEAD_DIM)
    return gains_ref[:, starts[which] : starts[which] + (D if which < 4 else HEAD_DIM)]


PRE_ATTN, POST_ATTN, PRE_FFN, POST_FFN, QUERY_GAIN, KEY_GAIN = range(6)


def weight_rows(ref, start, size):
    shards, rows, width = ref.shape
    if shards == 1:
        return ref[0, start : start + size, :]
    first, last = start // rows, -(-(start + size) // rows)
    value = ref[first:last].reshape((last - first) * rows, width)
    skip = start - first * rows
    return value[skip : skip + size]


def fetch(weight, ref, scratch, sem):
    _, start, rows = weight
    copy = pltpu.make_async_copy(ref.at[:, pl.ds(start, rows), :], scratch, sem)
    copy.start()
    return copy


def weight_scratch(weight):
    array, _, rows = weight
    return pltpu.VMEM((array.shape[0], rows, D), BF16)


def vmem(count):
    return [pl.BlockSpec(memory_space=pltpu.VMEM)] * count


def call(kernel, name, arrays, weights, outs, flops, limit, scratch=(), handed=False):
    outs = [jax.ShapeDtypeStruct(shape, dtype) for shape, dtype in outs]
    moved = sum(a.size * a.dtype.itemsize for a in list(arrays) + outs)
    return pl.pallas_call(
        kernel,
        out_shape=tuple(outs),
        in_specs=vmem(len(arrays)) + [pl.BlockSpec(memory_space=pltpu.HBM)] * len(weights),
        out_specs=tuple(vmem(len(outs))),
        scratch_shapes=[weight_scratch(w) for w in weights if not handed]
        + ([pltpu.SemaphoreType.DMA((len(weights),))] if weights else [])
        + list(scratch),
        compiler_params=pltpu.CompilerParams(vmem_limit_bytes=VMEM_LIMIT),
        cost_estimate=pl.CostEstimate(flops=flops // 64, bytes_accessed=moved // 64, transcendentals=0),
        name=name,
    )(*arrays, *[w[0] for w in weights])


def chunk_route(count, k):
    n_dp, n_seq = lax.axis_size("dp"), lax.axis_size("seq")
    chips = n_seq // (2 * count)
    pairs = []
    for dp in range(n_dp):
        for i in range(n_seq):
            chunk = i // count
            sequence = (dp % 2) * count + (i + k) % count
            target_dp = dp - dp % 2 + chunk % 2
            pairs.append((dp * n_seq + i, target_dp * n_seq + sequence * chips + chunk // 2))
    return pairs


def place(count):
    chips = lax.axis_size("seq") // (2 * count)
    return (lax.axis_index("seq") // chips) % count


def to_long(block):
    count = block.shape[0]
    me = lax.axis_index("seq")
    received = []
    for k in range(count):
        piece = lax.dynamic_index_in_dim(block, (me + k) % count, 0, keepdims=False)
        received.append(lax.ppermute(piece, ALL, chunk_route(count, k)))
    twice = jnp.stack((received[::-1] * 2)[: 2 * count - 1])
    long = lax.dynamic_slice_in_dim(twice, count - 1 - place(count), count, 0)
    return long.reshape((count * block.shape[1],) + block.shape[2:])


def to_short(long, count):
    me = lax.axis_index("seq")
    parts = long.reshape((count, long.shape[0] // count) + long.shape[1:])
    received = []
    for k in range(count):
        piece = lax.dynamic_index_in_dim(parts, (place(count) - k) % count, 0, keepdims=False)
        route = [(j, i) for i, j in chunk_route(count, k)]
        received.append(lax.ppermute(piece, ALL, route))
    twice = jnp.stack((received * 2)[: 2 * count - 1])
    return lax.dynamic_slice_in_dim(twice, (count - me % count) % count, count, 0)


def neighbour(block, count, back):
    n_dp, n_seq = lax.axis_size("dp"), lax.axis_size("seq")
    chips = n_seq // (2 * count)
    pairs = []
    for dp in range(n_dp):
        for i in range(n_seq):
            if dp % 2 == 0:
                pairs.append((dp * n_seq + i, (dp + 1) * n_seq + i))
            elif (i + 1) % chips:
                pairs.append((dp * n_seq + i, (dp - 1) * n_seq + i + 1))
    if back:
        pairs = [(j, i) for i, j in pairs]
    return lax.ppermute(block, ALL, pairs)


def bits(axis):
    out, bit = [], 1
    while bit < lax.axis_size(axis):
        out.append((axis, bit))
        bit *= 2
    return out


def order(first, scatter):
    core, *wide = bits("dp")
    near, *far = bits("seq")
    if scatter:
        return [core] + wide
    if first == "dp":
        return [core] + wide + [near] + far[::-1]
    return [core, near] + wide + far[::-1]


def swap(array, step):
    axis, bit = step
    return lax.ppermute(array, axis, [(i, i ^ bit) for i in range(lax.axis_size(axis))])


def launch(value, chains):
    chains = [chain for chain in chains if chain.pending is not None]
    if not chains:
        return value
    held = lax.optimization_barrier((value,) + tuple(chain.pending for chain in chains))
    for chain, pending in zip(chains, held[1:]):
        chain.got = swap(pending, chain.steps[0])
        chain.pending = None
    return held[0]


def advance(value, chains):
    chains = [chain for chain in chains if chain.steps]
    if not chains:
        return value
    held = lax.optimization_barrier((value,) + tuple(chain.got for chain in chains))
    for chain, got in zip(chains, held[1:]):
        chain.got = got
        chain.advance()
    return launch(held[0], chains + [part for chain in chains for part in chain.parts])


def block_numbers(scatter):
    me = lax.axis_index("dp")
    core = me % 2
    wide = [me // 2, (me // 2) ^ 1]
    leave = [2 * w + 1 - core for w in wide]
    stay = [2 * w + core for w in wide]
    along = lax.axis_index("seq") * (0 if scatter else 1)
    return jnp.stack(leave + stay + [along]).astype(jnp.int32)


def product_kernel(pairs, extra, added, outs, scatter, n_seq, numbers_ref, *refs):
    lefts, rights, refs = refs[:pairs], refs[pairs : 2 * pairs], refs[2 * pairs :]
    if extra:
        extra_ref, refs = refs[0], refs[1:]
    if added:
        got_ref, refs = refs[0], refs[1:]
    me, step = numbers_ref[4], pl.program_id(0)
    half = n_seq // 2

    def store(shard, base, value):
        entry = me ^ shard
        if not scatter:
            entry = lax.rem(entry, 2) * half + entry // 2
        place = slice(base, base + value.shape[0])
        if added:
            value = value + got_ref[0, entry, place].astype(F32)
        value = value.astype(BF16)
        for (kind, which, columns), ref in zip(outs, refs):
            if kind == "all":
                ref[0, entry, place] = value[:, columns]
                continue
            at = entry - which * half if kind == "half" else entry

            @pl.when((entry // half if kind == "half" else step) == which)
            def _():
                ref[0, at, place] = value[:, columns]

    base = 0
    for left, right in zip(lefts, rights):
        width = left.shape[1]
        rows = width // n_seq
        part = min(width, 512)
        for start in range(0, width, part):
            total = dot(left[:, start : start + part], right[...], 0, 0)
            for at in range(0, part, rows):
                store((start + at) // rows, base, total[at : at + rows])
        base += rows
    if extra:
        for shard in range(n_seq):
            store(shard, base, extra_ref[0, shard].astype(F32))


def product(factors, first, outs, got=None):
    pairs, extra, numbers, scatter = factors
    n_dp, n_seq = lax.axis_size("dp"), lax.axis_size("seq")
    tokens = pairs[0][0].shape[0]
    widths = [left.shape[1] // n_dp for left, _ in pairs]
    rows = sum(widths) // n_seq + (0 if extra is None else extra.shape[2])
    specs = [pl.BlockSpec((tokens, w), lambda i, n: (0, n[first + i])) for w in widths]
    specs += [pl.BlockSpec(right.shape, lambda i, n: (0, 0)) for _, right in pairs]
    operands = [left for left, _ in pairs] + [right for _, right in pairs]
    if extra is not None:
        specs.append(pl.BlockSpec((1,) + extra.shape[1:], lambda i, n: (n[first + i], 0, 0, 0)))
        operands.append(extra)
    if got is not None:
        specs.append(pl.BlockSpec((1, n_seq, rows, D), lambda i, n: (i, 0, 0, 0)))
        operands.append(got)
    shapes, out_specs = [], []
    for kind, _, columns in outs:
        wide = columns.stop - columns.start
        entries = n_seq // 2 if kind == "half" else n_seq
        shapes.append(jax.ShapeDtypeStruct((1 if kind == "block" else 2, entries, rows, wide), BF16))
        index = (lambda i, n: (0, 0, 0, 0)) if kind == "block" else (lambda i, n: (i, 0, 0, 0))
        out_specs.append(pl.BlockSpec((1, entries, rows, wide), index))
    return pl.pallas_call(
        partial(product_kernel, len(pairs), extra is not None, got is not None, outs, scatter, n_seq),
        grid_spec=pltpu.PrefetchScalarGridSpec(
            num_scalar_prefetch=1, grid=(2,), in_specs=specs, out_specs=out_specs
        ),
        out_shape=shapes,
        compiler_params=pltpu.CompilerParams(vmem_limit_bytes=VMEM_LIMIT_PRODUCT),
        cost_estimate=pl.CostEstimate(
            flops=tokens * sum(widths) * D // 16,
            bytes_accessed=(tokens + 2 * D) * sum(widths) // 16,
            transcendentals=0,
        ),
        name="weight_gradient",
    )(numbers, *operands)


WHOLE, CUT = slice(0, D), 3 * D // 5


class Chain:
    def __init__(self, pairs, scatter=False, extra=None, fork=False):
        self.steps = order("dp", scatter)
        self.fork = fork
        self.parts = []
        n_dp, n_seq = lax.axis_size("dp"), lax.axis_size("seq")
        widths = [left.shape[1] // n_dp for left, _ in pairs]
        self.factors = None
        self.rows = sum(widths) // n_seq + (0 if extra is None else extra.shape[2])
        if n_dp == 4 and all(w % 128 == 0 and w % (n_seq * TILE) == 0 for w in widths):
            self.factors = (pairs, extra, block_numbers(scatter), scatter)
            (self.pending,) = product(self.factors, 0, [("all", 0, WHOLE)])
            return
        devices = n_dp * n_seq
        parts = [
            dot(left, right, 0, 0).astype(BF16).reshape(devices, -1, D) for left, right in pairs
        ]
        if extra is not None:
            parts.append(extra.reshape(devices, -1, D))
        target = jnp.arange(devices)
        source, left_over = jnp.zeros_like(target), devices
        for axis, bit in self.steps:
            left_over //= 2
            source = source + (target // left_over) % 2 * (bit * n_seq if axis == "dp" else bit)
        if scatter:
            source = source + target % n_seq
        me = lax.axis_index("dp") * n_seq
        if not scatter:
            me = me + lax.axis_index("seq")
        self.cut(jnp.take(jnp.concatenate(parts, axis=1), me ^ source, axis=0))

    def part(self, steps, keep, pending):
        chain = object.__new__(Chain)
        chain.steps, chain.factors, chain.fork, chain.parts = steps, None, False, []
        chain.keep, chain.pending = keep, pending
        self.parts.append(chain)

    def cut(self, array):
        half = array.shape[0] // 2
        self.keep, self.pending = array[:half], array[half:]

    def advance(self):
        self.steps = self.steps[1:]
        if self.factors:
            factors, self.factors = self.factors, None
            outs = [("block", 0, WHOLE), ("block", 1, WHOLE)]
            if self.fork:
                a, b = slice(0, CUT), slice(CUT, D)
                outs = [("block", 0, a), ("block", 1, a), ("half", 0, b), ("half", 1, b)]
            found = product(factors, 2, outs, self.got)
            found = [array.reshape((-1, self.rows) + array.shape[3:]) for array in found]
            if self.fork:
                self.pending = None
                self.part(order("dp", False)[1:], *found[:2])
                self.part(order("seq", False)[1:], *found[2:])
                self.steps = []
            else:
                self.keep, self.pending = found
            return
        array = self.keep.astype(F32) + self.got.astype(F32)
        if self.steps:
            self.cut(array.astype(BF16))
        else:
            self.result = array

    def finish(self):
        if self.parts:
            return jnp.concatenate([part.finish() for part in self.parts], axis=2)
        while self.steps:
            if self.pending is not None:
                self.got = swap(self.pending, self.steps[0])
                self.pending = None
            self.advance()
        return self.result


def round_kernel(waits, value_ref, *refs):
    refs[waits][...] = value_ref[...].astype(BF16)


def rounded(value, after):
    return pl.pallas_call(
        partial(round_kernel, len(after)),
        in_specs=[pl.BlockSpec(memory_space=pltpu.VMEM)] + [pl.BlockSpec(memory_space=pltpu.HBM)] * len(after),
        out_specs=pl.BlockSpec(memory_space=pltpu.VMEM),
        out_shape=jax.ShapeDtypeStruct(value.shape, BF16),
        compiler_params=pltpu.CompilerParams(vmem_limit_bytes=VMEM_LIMIT_PRODUCT),
        name="round_gradient",
    )(value, *after)


def allowed_pairs(start, key_count, reach, lanes):
    key_at = lax.broadcasted_iota(jnp.int32, (key_count, lanes), 0)
    query_at = lax.broadcasted_iota(jnp.int32, (key_count, lanes), 1) % QUERY_BLOCK
    distance = query_at + WINDOW - key_at
    return (distance >= 0) & (distance <= reach)


def stacked_heads(ref, start):
    return jnp.concatenate(
        [
            ref[start : start + QUERY_BLOCK, h * HEAD_DIM : (h + 1) * HEAD_DIM]
            for h in range(HEADS)
        ],
        axis=0,
    )


def window_rows(before_ref, own_ref, start, count, columns):
    return jnp.concatenate(
        [before_ref[start:, columns], own_ref[: count - (WINDOW - start), columns]], axis=0
    )


KEYS, VALUES = slice(0, HEAD_DIM), slice(HEAD_DIM, 2 * HEAD_DIM)
KEY_COUNT = QUERY_BLOCK + WINDOW


def key_value_kernel(weights, stream_ref, gains_ref, cos_ref, sin_ref, w_any, normed_ref, raw_ref, own_ref, w_ref, sem):
    copy = fetch(weights[0], w_any, w_ref, sem.at[0])
    normed = rms_norm(stream_ref[...], gain_of(gains_ref, PRE_ATTN)).astype(BF16)
    normed_ref[...] = normed
    copy.wait()
    raw = dot(normed, weight_rows(w_ref, QUERY_COLS, 2 * HEAD_DIM), 1, 1)
    raw_ref[...] = raw[:, KEYS]
    keys = rms_norm(raw[:, KEYS], gain_of(gains_ref, KEY_GAIN))
    own_ref[:, KEYS] = rotate(keys, cos_ref[...], sin_ref[...]).astype(BF16)
    own_ref[:, VALUES] = raw[:, VALUES].astype(BF16)


def query_kernel(normed_ref, gains_ref, cos_ref, sin_ref, w_ref, raw_ref, q_ref):
    cosine_tab, sine_tab = cos_ref[...], sin_ref[...]
    normed = normed_ref[...]
    for h in range(HEADS):
        columns = slice(h * HEAD_DIM, (h + 1) * HEAD_DIM)
        raw = dot(normed, weight_rows(w_ref, h * HEAD_DIM, HEAD_DIM), 1, 1)
        raw_ref[:, columns] = raw
        queries = rotate(rms_norm(raw, gain_of(gains_ref, QUERY_GAIN)), cosine_tab, sine_tab)
        q_ref[:, columns] = queries.astype(BF16) * SCORE_SCALE


def gelu_parts(gate):
    inner = GELU_A * (gate + GELU_B * gate * gate * gate)
    tanh = jnp.tanh(inner)
    return tanh, 0.5 * gate * (1.0 + tanh)


def block_kernel(
    weights, q_ref, before_ref, own_ref, reach_ref, stream_ref, gains_ref, wa_any, wi_any, wo_any,
    ctx_ref, lse_ref, branch_ref, middle_ref, fn_ref, gu_ref, inner_ref, fb_ref, result_ref,
    wa_ref, wi_ref, wo_ref, sem,
):
    copies = [
        fetch(weight, source, target, sem.at[i])
        for i, (weight, source, target) in enumerate(
            zip(weights, (wa_any, wi_any, wo_any), (wa_ref, wi_ref, wo_ref))
        )
    ]
    for block in range(q_ref.shape[0] // QUERY_BLOCK):
        start = block * QUERY_BLOCK
        queries = stacked_heads(q_ref, start)
        keys = window_rows(before_ref, own_ref, start, KEY_COUNT, KEYS)
        values = window_rows(before_ref, own_ref, start, KEY_COUNT, VALUES)
        allowed = allowed_pairs(start, KEY_COUNT, reach_ref[block : block + 1, :], HEADS * QUERY_BLOCK)
        scores = jnp.where(allowed, dot(keys, queries, 1, 1), MASKED_SCORE)
        row_max = jnp.max(scores, axis=0, keepdims=True)
        exps = jnp.exp(scores - row_max)
        row_sum = jnp.sum(exps, axis=0, keepdims=True)
        probs = (exps * (1.0 / row_sum)).astype(BF16)
        lse_ref[block : block + 1, :] = row_max + jnp.log(row_sum)
        context = dot(probs, values, 0, 0).astype(BF16)
        for h in range(HEADS):
            ctx_ref[start : start + QUERY_BLOCK, h * HEAD_DIM : (h + 1) * HEAD_DIM] = context[
                h * QUERY_BLOCK : (h + 1) * QUERY_BLOCK
            ]
    copies[0].wait()
    branch = dot(ctx_ref[...], weight_rows(wa_ref, 0, QUERY_COLS), 1, 0)
    branch_ref[...] = branch
    middle = stream_ref[...] + rms_norm(branch, gain_of(gains_ref, POST_ATTN))
    middle_ref[...] = middle
    ffn_normed = rms_norm(middle, gain_of(gains_ref, PRE_FFN)).astype(BF16)
    fn_ref[...] = ffn_normed
    copies[1].wait()
    copies[2].wait()
    hidden = inner_ref.shape[1]
    total = jnp.zeros(branch_ref.shape, F32)
    for start in range(0, hidden, HIDDEN_BLOCK):
        gate_cols = slice(start, start + HIDDEN_BLOCK)
        up_cols = slice(hidden + start, hidden + start + HIDDEN_BLOCK)
        gate = dot(ffn_normed, weight_rows(wi_ref, start, HIDDEN_BLOCK), 1, 1)
        up = dot(ffn_normed, weight_rows(wi_ref, hidden + start, HIDDEN_BLOCK), 1, 1)
        gu_ref[:, gate_cols] = gate.astype(BF16)
        gu_ref[:, up_cols] = up.astype(BF16)
        inner = (gelu_parts(gate)[1] * up).astype(BF16)
        inner_ref[:, gate_cols] = inner
        total += dot(inner, weight_rows(wo_ref, start, HIDDEN_BLOCK), 1, 0)
    fb_ref[...] = total
    result_ref[...] = middle + rms_norm(total, gain_of(gains_ref, POST_FFN))


def forward_layer(stream, weights, gains, tables, reach, count):
    tokens = stream.shape[0]
    cosine_tab, sine_tab = tables
    attn_in, attn_out, ffn_in, ffn_out = weights
    hidden = ffn_out[0].shape[0] * ffn_out[2]
    normed, key_raw, own, fetched = call(
        partial(key_value_kernel, [attn_in]), "key_value",
        (stream, gains, cosine_tab, sine_tab), [attn_in],
        [
            ((tokens, D), BF16), ((tokens, HEAD_DIM), F32), ((tokens, 2 * HEAD_DIM), BF16),
            ((attn_in[0].shape[0], attn_in[2], D), BF16),
        ],
        4 * tokens * D * HEAD_DIM, 12, handed=True,
    )
    before = neighbour(own, count, False)
    query_raw, queries = call(
        query_kernel, "query", (normed, gains, cosine_tab, sine_tab, fetched), [],
        [((tokens, QUERY_COLS), F32), ((tokens, QUERY_COLS), BF16)],
        2 * tokens * D * QUERY_COLS, 12,
    )
    context, lse, branch, middle, ffn_normed, gate_up, inner, ffn_branch, result = call(
        partial(block_kernel, [attn_out, ffn_in, ffn_out]), "block_forward",
        (queries, before, own, reach, stream, gains), [attn_out, ffn_in, ffn_out],
        [
            ((tokens, QUERY_COLS), BF16), (reach.shape, F32), ((tokens, D), F32), ((tokens, D), F32),
            ((tokens, D), BF16), ((tokens, 2 * hidden), BF16), ((tokens, hidden), BF16),
            ((tokens, D), F32), ((tokens, D), F32),
        ],
        2 * tokens * (D * (QUERY_COLS + 3 * hidden) + 2 * QUERY_COLS * KEY_COUNT), 32,
    )
    record = (
        stream, normed, query_raw, key_raw, queries, before, own, lse, context,
        branch, middle, ffn_normed, gate_up, inner, ffn_branch,
    )
    return record, result


def block_backward_kernel(
    weights, grad_ref, fb_ref, gu_ref, middle_ref, branch_ref, gains_ref, wa_any, wi_any, wo_any,
    gfb_ref, ggu_ref, gb_ref, gctx_ref, gmid_ref, sums_ref,
    wa_ref, wi_ref, wo_ref, sem,
):
    copies = [None] * 3
    for i, source, target in ((2, wo_any, wo_ref), (1, wi_any, wi_ref), (0, wa_any, wa_ref)):
        copies[i] = fetch(weights[i], source, target, sem.at[i])
    grad_out = grad_ref[...]
    grad_ffn_branch, post_ffn = rms_backward(fb_ref[...], gain_of(gains_ref, POST_FFN), grad_out)
    grad_ffn_branch = grad_ffn_branch.astype(BF16)
    gfb_ref[...] = grad_ffn_branch
    copies[2].wait()
    hidden = gu_ref.shape[1] // 2
    total = jnp.zeros(grad_ref.shape, F32)
    for start in range(0, hidden, HIDDEN_BLOCK):
        gate_cols = slice(start, start + HIDDEN_BLOCK)
        up_cols = slice(hidden + start, hidden + start + HIDDEN_BLOCK)
        grad_inner = dot(grad_ffn_branch, weight_rows(wo_ref, start, HIDDEN_BLOCK), 1, 1)
        gate = gu_ref[:, gate_cols].astype(F32)
        up = gu_ref[:, up_cols].astype(F32)
        tanh, value = gelu_parts(gate)
        slope = 0.5 * (1.0 + tanh) + 0.5 * gate * (1.0 - tanh * tanh) * GELU_A * (
            1.0 + 3.0 * GELU_B * gate * gate
        )
        grad_gate = (grad_inner * up * slope).astype(BF16)
        grad_up = (grad_inner * value).astype(BF16)
        ggu_ref[:, gate_cols] = grad_gate
        ggu_ref[:, up_cols] = grad_up
        if start == 0:
            copies[1].wait()
        total += dot(grad_gate, weight_rows(wi_ref, start, HIDDEN_BLOCK), 1, 0)
        total += dot(grad_up, weight_rows(wi_ref, hidden + start, HIDDEN_BLOCK), 1, 0)
    grad_part, pre_ffn = rms_backward(middle_ref[...], gain_of(gains_ref, PRE_FFN), total)
    grad_middle = grad_out + grad_part
    gmid_ref[...] = grad_middle
    grad_branch, post_attn = rms_backward(branch_ref[...], gain_of(gains_ref, POST_ATTN), grad_middle)
    grad_branch = grad_branch.astype(BF16)
    gb_ref[...] = grad_branch
    sums_ref[0:1, :] = post_attn
    sums_ref[1:2, :] = pre_ffn
    sums_ref[2:3, :] = post_ffn
    copies[0].wait()
    gctx_ref[...] = dot(grad_branch, weight_rows(wa_ref, 0, QUERY_COLS), 1, 1).astype(BF16)


def attention_backward_kernel(
    q_ref, before_ref, own_ref, reach_ref, lse_ref, g_ref, dq_ref, gbefore_ref, gown_ref, acc
):
    acc[...] = jnp.zeros_like(acc)
    for block in range(q_ref.shape[0] // QUERY_BLOCK):
        start = block * QUERY_BLOCK
        queries = stacked_heads(q_ref, start)
        grads = stacked_heads(g_ref, start)
        keys = window_rows(before_ref, own_ref, start, KEY_COUNT, KEYS)
        values = window_rows(before_ref, own_ref, start, KEY_COUNT, VALUES)
        allowed = allowed_pairs(start, KEY_COUNT, reach_ref[block : block + 1, :], HEADS * QUERY_BLOCK)
        scores = jnp.where(allowed, dot(keys, queries, 1, 1), MASKED_SCORE)
        probs = jnp.exp(scores - lse_ref[block : block + 1, :])
        grad_probs = dot(values, grads, 1, 1)
        inner = jnp.sum(probs * grad_probs, axis=0, keepdims=True)
        grad_scores = (probs * (grad_probs - inner)).astype(BF16)
        acc[start : start + KEY_COUNT, VALUES] += dot(probs.astype(BF16), grads, 1, 0)
        acc[start : start + KEY_COUNT, KEYS] += dot(grad_scores, queries, 1, 0)
        grad_queries = dot(grad_scores, keys, 0, 0) * SCORE_SCALE
        for h in range(HEADS):
            dq_ref[start : start + QUERY_BLOCK, h * HEAD_DIM : (h + 1) * HEAD_DIM] = grad_queries[
                h * QUERY_BLOCK : (h + 1) * QUERY_BLOCK
            ]
    gbefore_ref[...] = acc[:WINDOW, :].astype(BF16)
    gown_ref[...] = acc[WINDOW:, :]


def query_backward_kernel(dq_ref, raw_ref, gains_ref, cos_ref, sin_ref, gq_ref, sums_ref):
    cosine_tab, sine_tab = cos_ref[...], sin_ref[...]
    sums = jnp.zeros((1, HEAD_DIM), F32)
    for h in range(HEADS):
        columns = slice(h * HEAD_DIM, (h + 1) * HEAD_DIM)
        grad = rotate_back(dq_ref[:, columns], cosine_tab, sine_tab)
        grad, part = rms_backward(raw_ref[:, columns], gain_of(gains_ref, QUERY_GAIN), grad)
        gq_ref[:, columns] = grad.astype(BF16)
        sums += part
    sums_ref[...] = sums


def input_backward_kernel(
    weights, gq_ref, gown_ref, got_ref, kraw_ref, gmid_ref, stream_ref, gains_ref, cos_ref, sin_ref,
    sums_ref, qsums_ref, w_any, gproj_ref, gin_ref, ggains_ref, w_ref, sem,
):
    copy = fetch(weights[0], w_any, w_ref, sem.at[0])
    total = gown_ref[...] + got_ref[...].astype(F32)
    grad_keys = rotate_back(total[:, KEYS], cos_ref[...], sin_ref[...])
    grad_keys, key_sums = rms_backward(kraw_ref[...], gain_of(gains_ref, KEY_GAIN), grad_keys)
    gproj_ref[:, :QUERY_COLS] = gq_ref[...]
    gproj_ref[:, QUERY_COLS : QUERY_COLS + HEAD_DIM] = grad_keys.astype(BF16)
    gproj_ref[:, QUERY_COLS + HEAD_DIM :] = total[:, VALUES].astype(BF16)
    copy.wait()
    grad_normed = dot(gproj_ref[...], weight_rows(w_ref, 0, QUERY_COLS + 2 * HEAD_DIM), 1, 0)
    grad_part, sums = rms_backward(stream_ref[...], gain_of(gains_ref, PRE_ATTN), grad_normed)
    gin_ref[...] = gmid_ref[...] + grad_part
    found = [sums] + [sums_ref[i : i + 1, :] for i in range(3)] + [qsums_ref[...], key_sums]
    ggains_ref[...] = jnp.concatenate(found, axis=1)


def backward_layer(grad_out, weights, gains, record, tables, reach, count, pump, chains, last):
    attn_in, attn_out, ffn_in, ffn_out = weights
    cosine_tab, sine_tab = tables
    (
        stream, normed, query_raw, key_raw, queries, before, own, lse, context,
        branch, middle, ffn_normed, gate_up, inner, ffn_branch,
    ) = record
    tokens = stream.shape[0]
    hidden = inner.shape[1]
    grad_out = pump(0, grad_out)
    grad_ffn_branch, grad_gate_up, grad_branch, grad_context, grad_middle, sums = call(
        partial(block_backward_kernel, [attn_out, ffn_in, ffn_out]), "block_backward",
        (grad_out, ffn_branch, gate_up, middle, branch, gains), [attn_out, ffn_in, ffn_out],
        [
            ((tokens, D), BF16), ((tokens, 2 * hidden), BF16), ((tokens, D), BF16),
            ((tokens, QUERY_COLS), BF16), ((tokens, D), F32), ((8, D), F32),
        ],
        2 * tokens * D * (QUERY_COLS + 3 * hidden), 26,
    )
    grad_context = pump(1, grad_context)
    ffn = [(grad_gate_up, ffn_normed), (inner, grad_ffn_branch)]
    chains["ffn"] = Chain(ffn, last, fork=not last)
    grad_context = launch(grad_context, list(chains.values()))
    grad_queries, grad_before, grad_own = call(
        attention_backward_kernel, "attention_backward",
        (queries, before, own, reach, lse, grad_context), [],
        [((tokens, QUERY_COLS), F32), ((WINDOW, 2 * HEAD_DIM), BF16), ((tokens, 2 * HEAD_DIM), F32)],
        10 * tokens * QUERY_COLS * KEY_COUNT, 26,
        [pltpu.VMEM((WINDOW + tokens, 2 * HEAD_DIM), F32)],
    )
    got = neighbour(grad_before, count, True)
    grad_queries = pump(2, grad_queries)
    grad_query_raw, query_sums = call(
        query_backward_kernel, "query_backward",
        (grad_queries, query_raw, gains, cosine_tab, sine_tab), [],
        [((tokens, QUERY_COLS), BF16), ((1, HEAD_DIM), F32)],
        20 * tokens * QUERY_COLS, 12,
    )
    grad_query_raw = pump(3, grad_query_raw)
    grad_projected, grad_in, gain_grads = call(
        partial(input_backward_kernel, [attn_in]), "input_backward",
        (
            grad_query_raw, grad_own, got, key_raw, grad_middle, stream, gains, cosine_tab, sine_tab,
            sums, query_sums,
        ),
        [attn_in],
        [((tokens, QUERY_COLS + 2 * HEAD_DIM), BF16), ((tokens, D), F32), (gains.shape, F32)],
        2 * tokens * D * (QUERY_COLS + 2 * HEAD_DIM), 14,
    )
    n_dp, n_seq = lax.axis_size("dp"), lax.axis_size("seq")
    gain_grads = gain_grads.astype(BF16).reshape(n_dp, n_seq, 1, -1)
    extra = jnp.pad(gain_grads, ((0, 0), (0, 0), (0, TILE - 1), (0, D - gain_grads.shape[3])))
    attn = [(grad_projected, normed), (context, grad_branch)]
    chains["attn"] = Chain(attn, last, extra)
    return launch(grad_in, [chains["attn"]])


PLAN = {
    0: [(1, "attn")],
    1: [(1, "ffn"), (1, "attn")],
    2: [(0, "ffn")],
    3: [],
}


def gather_weights(shards, gains, behind):
    layers = gains.shape[0]
    gain_rows = jnp.pad(gains, ((0, TILE - layers), (0, D - gains.shape[1])))
    first = [(kind, l) for l in range(layers) for kind in range(len(shards)) if l == 0 or kind >= 2]
    later = [(kind, l) for l in range(1, layers) for kind in range(2)]
    found, rest = {}, None
    for names in (first, later):
        parts = [shards[kind][l] for kind, l in names]
        if names is first:
            parts.append(gain_rows)
        packed = jnp.concatenate(parts, axis=0)
        if names is later:
            behind, packed = lax.optimization_barrier((behind, packed))
        whole = lax.all_gather(packed, ALL, axis=0, tiled=False)
        at = 0
        for kind, l in names:
            size = shards[kind].shape[1]
            if size % TILE:
                found[kind, l] = (whole[:, at : at + size].reshape(1, -1, D), 0, size * whole.shape[0])
            else:
                found[kind, l] = (whole, at, size)
            at += size
        if names is first:
            gain_full = whole[:, at : at + layers, : gains.shape[1]].astype(F32)
    out = []
    for l in range(layers):
        ffn_in, ffn_out, attn_in, attn_out = [found[kind, l] for kind in range(4)]
        out.append(((attn_in, attn_out, ffn_in, ffn_out), gain_full[:, l].reshape(1, -1)))
    return out, behind


def body(hidden_in, positions, out_grad, w_attn_in, w_attn_out, w_ffn_in, w_ffn_out, gains):
    count = hidden_in.shape[0]
    layer_count = w_attn_in.shape[0]
    sizes = [w_ffn_in.shape[2], w_ffn_out.shape[1], w_attn_in.shape[2], w_attn_out.shape[1]]
    shards = [w_ffn_in.transpose(0, 2, 1), w_ffn_out, w_attn_in.transpose(0, 2, 1), w_attn_out]
    places = to_long(positions)
    stream = to_long(hidden_in).astype(F32)
    tables = angle_tables(places)
    tokens = places.shape[0]
    blocks = tokens // QUERY_BLOCK
    reach = jnp.minimum(places, WINDOW - 1).reshape(blocks, QUERY_BLOCK)
    reach = jnp.tile(reach, (1, HEADS))
    records = []
    weights, stream = gather_weights(shards, gains, stream)
    for layer_index in range(layer_count):
        record, stream = forward_layer(stream, *weights[layer_index], tables, reach, count)
        records.append(record)
        if layer_index == 0:
            stream, out_grad = lax.optimization_barrier((stream, out_grad))
            grad_stream = to_long(out_grad).astype(F32)
    hidden_out = to_short(stream.astype(BF16), count)
    outputs = {"hidden": hidden_out}
    chains = [{} for _ in range(layer_count + 1)]
    sums = [None] * layer_count
    for layer_index in reversed(range(layer_count)):

        def pump(where, value):
            active = [
                chains[layer_index + above][name]
                for above, name in PLAN[where]
                if name in chains[layer_index + above]
            ]
            value = advance(value, active)
            if where == 1 and layer_index + 1 == layer_count:
                value, outputs["hidden"] = lax.optimization_barrier((value, outputs["hidden"]))
            if where == 1 and layer_index + 1 < layer_count:
                above = chains[layer_index + 1]
                packed = jnp.concatenate([above["ffn"].finish(), above["attn"].finish()], axis=1)
                value, packed = lax.optimization_barrier((value, packed.astype(BF16)))
                sums[layer_index + 1] = lax.psum_scatter(packed, "seq", scatter_dimension=0)
            return value

        grad_stream = backward_layer(
            grad_stream, *weights[layer_index], records[layer_index], tables, reach, count, pump,
            chains[layer_index], layer_index > 0,
        )
    attn, ffn = [chains[0]["attn"]], chains[0]["ffn"].parts or [chains[0]["ffn"]]
    mark = grad_stream[:8]
    for chains_now in (ffn, attn, ffn):
        mark = advance(mark, chains_now)
    short = to_short(rounded(grad_stream, [chain.keep for chain in ffn]), count)
    for chains_now in (attn, ffn, attn, ffn, attn):
        mark = advance(mark, chains_now)
    sums[0] = jnp.concatenate([chains[0]["ffn"].finish(), chains[0]["attn"].finish()], axis=1)[0]
    packed = jnp.stack([entry.astype(F32) for entry in sums])
    parts, at = [], 0
    for size in sizes:
        parts.append(packed[:, at : at + size])
        at += size
    return (
        outputs["hidden"],
        short.astype(F32),
        parts[2].transpose(0, 2, 1),
        parts[3],
        parts[0].transpose(0, 2, 1),
        parts[1],
        packed[:, at, : gains.shape[1]],
    )


def solution(mesh):
    return jax.shard_map(
        body,
        mesh=mesh,
        in_specs=(
            P("dp", "seq", None),
            P("dp", "seq"),
            P("dp", "seq", None),
            P(None, None, ("dp", "seq")),
            P(None, ("dp", "seq"), None),
            P(None, None, ("dp", "seq")),
            P(None, ("dp", "seq"), None),
            P(None, ("dp", "seq")),
        ),
        out_specs=(
            P("dp", "seq", None),
            P("dp", "seq", None),
            P(None, None, ("dp", "seq")),
            P(None, ("dp", "seq"), None),
            P(None, None, ("dp", "seq")),
            P(None, ("dp", "seq"), None),
            P(None, ("dp", "seq")),
        ),
        check_vma=False,
    )
```
